32 devices in a mesh: dp: 4 (over y, x), fsdp: 8 (over z, core).
Axes of the slice: x: 2, y: 2, z: 4, core: 2. Of those that a mesh axis runs over, the one named last changes fastest.
Arguments:
- tok_ids: int32 [32, 128], P(('dp', 'fsdp')), may hold values from 0 to 50303
- targets: int32 [32, 128], P(('dp', 'fsdp')), may hold values from 0 to 50303
- loss_mask: int32 [32, 128], P(('dp', 'fsdp')), may hold values 0 or 1
- embed: float32 [50304, 768], P('fsdp'), may hold values from -0.4375 to 0.4375
- embed_m: float32 [50304, 768], P('fsdp'), may hold values from -7.6293945e-06 to 7.6293945e-06
- embed_v: float32 [50304, 768], P('fsdp'), may hold values from 2.1455721e-12 to 8.5822885e-12
- posit: float32 [1024, 768], P('fsdp'), may hold values from -3 to 3
- posit_m: float32 [1024, 768], P('fsdp'), may hold values from -7.6293945e-06 to 7.6293945e-06
- posit_v: float32 [1024, 768], P('fsdp'), may hold values from 2.1455721e-12 to 8.5822885e-12
- attn_in: float32 [768, 2304], P('fsdp'), may hold values from -0.21875 to 0.21875
- attn_in_m: float32 [768, 2304], P('fsdp'), may hold values from -7.6293945e-06 to 7.6293945e-06
- attn_in_v: float32 [768, 2304], P('fsdp'), may hold values from 2.1455721e-12 to 8.5822885e-12
- attn_out: float32 [768, 768], P('fsdp'), may hold values from -1.25 to 1.25
- attn_out_m: float32 [768, 768], P('fsdp'), may hold values from -7.6293945e-06 to 7.6293945e-06
- attn_out_v: float32 [768, 768], P('fsdp'), may hold values from 2.1455721e-12 to 8.5822885e-12
- mlp_in: float32 [768, 3072], P('fsdp'), may hold values from -0.21875 to 0.21875
- mlp_in_m: float32 [768, 3072], P('fsdp'), may hold values from -7.6293945e-06 to 7.6293945e-06
- mlp_in_v: float32 [768, 3072], P('fsdp'), may hold values from 2.1455721e-12 to 8.5822885e-12
- mlp_out: float32 [3072, 768], P('fsdp'), may hold values from -0.109375 to 0.109375
- mlp_out_m: float32 [3072, 768], P('fsdp'), may hold values from -7.6293945e-06 to 7.6293945e-06
- mlp_out_v: float32 [3072, 768], P('fsdp'), may hold values from 2.1455721e-12 to 8.5822885e-12
- small: float32 [109824], P('fsdp'), may hold values from -1 to 1.4
- small_m: float32 [109824], P('fsdp'), may hold values from -2.670288e-05 to 2.670288e-05
- small_v: float32 [109824], P('fsdp'), may hold values from 1.9310149e-11 to 7.7240596e-11
Outputs:
- loss: float32 [], replicated
- grad_norm: float32 [], replicated
- embed_new: float32 [50304, 768], P('fsdp')
- embed_m_new: float32 [50304, 768], P('fsdp')
- embed_v_new: float32 [50304, 768], P('fsdp')
- posit_new: float32 [1024, 768], P('fsdp')
- posit_m_new: float32 [1024, 768], P('fsdp')
- posit_v_new: float32 [1024, 768], P('fsdp')
- attn_in_new: float32 [768, 2304], P('fsdp')
- attn_in_m_new: float32 [768, 2304], P('fsdp')
- attn_in_v_new: float32 [768, 2304], P('fsdp')
- attn_out_new: float32 [768, 768], P('fsdp')
- attn_out_m_new: float32 [768, 768], P('fsdp')
- attn_out_v_new: float32 [768, 768], P('fsdp')
- mlp_in_new: float32 [768, 3072], P('fsdp')
- mlp_in_m_new: float32 [768, 3072], P('fsdp')
- mlp_in_v_new: float32 [768, 3072], P('fsdp')
- mlp_out_new: float32 [3072, 768], P('fsdp')
- mlp_out_m_new: float32 [3072, 768], P('fsdp')
- mlp_out_v_new: float32 [3072, 768], P('fsdp')
- small_new: float32 [109824], P('fsdp')
- small_m_new: float32 [109824], P('fsdp')
- small_v_new: float32 [109824], P('fsdp')
The draws below stay inside these ranges and needn't reach their ends.
All inputs are finite; a program needn't handle non-finite values. No bound on the sum of `loss_mask` on one device may be relied on, other than what follows from the above.
Results may differ from the reference program's by a relative error of at most 0.01.
Values may be sent and summed in bfloat16 or wider, within the bound.
A program may use at most 384 MiB of HBM per device.

```python
import math
import jax
import jax.numpy as jnp
import numpy as np
from jax import lax

D = 768
H = 12
HD = 64
FF = 3072
V = 50304
NPOS = 1024
SEQ = 128
STEP = 2
SEQS = 32
NSMALL = 109824
NPARAM = 46607616


def draw_small(key, part):
    key_gain, key_norm, key_bias, key_maps = jax.random.split(key, 4)
    gains = jax.random.uniform(key_gain, (3, D), jnp.float32, 0.6, 1.4)
    norm_bias = jnp.clip(0.3 * jax.random.normal(key_norm, (3, D), jnp.float32), -1.0, 1.0)
    norms = jnp.stack([gains, norm_bias], axis=1).reshape(-1)
    biases = jnp.clip(0.3 * jax.random.normal(key_bias, (5 * D + FF,), jnp.float32), -1.0, 1.0)
    maps = jnp.clip(HD ** (-0.5) * jax.random.normal(key_maps, (2 * H * HD * HD,), jnp.float32), -0.5, 0.5)
    return jnp.concatenate([norms, biases, maps])


def set_ends(drawn, rng, least, largest):
    spot = [jax.random.randint(jax.random.fold_in(rng, axis), (), 0, length) for axis, length in enumerate(drawn.shape)]
    main_axis = drawn.shape.index(max(drawn.shape))
    beside = spot[:main_axis] + [(spot[main_axis] + 1) % drawn.shape[main_axis]] + spot[main_axis + 1:]
    return drawn.at[tuple(spot)].set(least).at[tuple(beside)].set(largest)


def block_levels(stream_key, shape, shards, smallest, top_value):
    def one(position, parts):
        heights = jax.random.uniform(jax.random.fold_in(jax.random.fold_in(stream_key, 6), position), (parts,), jnp.float32, smallest / len(shards), top_value / len(shards))
        return jnp.repeat(jnp.exp(heights), shape[position] // parts).reshape((-1,) + (1,) * (len(shape) - position - 1))

    factor_of = one(*shards[0])
    for cut in shards[1:]:
        factor_of = factor_of * one(*cut)
    return factor_of


def rank_bounds(count, slope):
    portions = [(1 << 20) // math.isqrt(rank ** slope) + 1 for rank in range(1, count + 1)]
    scale = 1 + sum(portions) // (1 << 30)
    return np.cumsum(np.array([max(1, weight // scale) for weight in portions]))


def skewed_ids(own_key, shape, amount, skew):
    grid = rank_bounds(amount, skew)
    pick = jax.random.randint(jax.random.fold_in(own_key, 1), shape, 0, int(grid[amount - 1]))
    rank = jnp.searchsorted(jnp.asarray(grid, jnp.int32), pick, side="right")
    return jax.random.permutation(jax.random.fold_in(own_key, 2), amount)[rank].astype(jnp.int32)


def bell_draw(stream_key, shape, width, most, cuts=(), held_as=jnp.bfloat16):
    values = width * jax.random.normal(stream_key, shape, jnp.float32)
    if cuts:
        values = values * block_levels(stream_key, shape, cuts, -0.22, 0.18)
    return jnp.clip(values, -most, most).astype(held_as)


def setup_inputs(seed: int = 0) -> dict:
    splits = jax.random.split(jax.random.key(seed), 25)
    tok_ids = set_ends(skewed_ids(splits[0], (SEQS, SEQ), V, 2), jax.random.fold_in(splits[0], 3), 0, V - 1).astype(jnp.int32)
    targets = set_ends(skewed_ids(splits[1], (SEQS, SEQ), V, 2), jax.random.fold_in(splits[1], 3), 0, V - 1).astype(jnp.int32)
    loss_mask = set_ends((jax.random.randint(splits[2], (SEQS, SEQ), 0, 10) < 7).astype(jnp.int32), jax.random.fold_in(splits[2], 1), 0, 1)
    embed = bell_draw(splits[3], (V, D), (D // 4) ** -0.5, 0.4375, ((0, 8),), jnp.float32)
    embed_m = bell_draw(splits[4], (V, D), (0.01 * NPARAM ** -0.5), 7.62939453125e-06, ((0, 8),), jnp.float32)
    embed_v = jnp.clip(2.1455721314206366e-12 + 6.43671639426191e-12 * jax.random.uniform(splits[5], (V, D), jnp.float32) ** block_levels(splits[5], (V, D), ((0, 8),), -0.2, 0.2), 2.1455721314206366e-12, 8.582288525682547e-12)
    posit = bell_draw(splits[6], (NPOS, D), 0.5, 3.0, ((0, 8),), jnp.float32)
    posit_m = bell_draw(splits[7], (NPOS, D), (0.01 * NPARAM ** -0.5), 7.62939453125e-06, ((0, 8),), jnp.float32)
    posit_v = jnp.clip(2.1455721314206366e-12 + 6.43671639426191e-12 * jax.random.uniform(splits[8], (NPOS, D), jnp.float32) ** block_levels(splits[8], (NPOS, D), ((0, 8),), -0.2, 0.2), 2.1455721314206366e-12, 8.582288525682547e-12)
    attn_in = bell_draw(splits[9], (D, 3 * D), D ** -0.5, 0.21875, ((0, 8),), jnp.float32)
    attn_in_m = bell_draw(splits[10], (D, 3 * D), (0.01 * NPARAM ** -0.5), 7.62939453125e-06, ((0, 8),), jnp.float32)
    attn_in_v = jnp.clip(2.1455721314206366e-12 + 6.43671639426191e-12 * jax.random.uniform(splits[11], (D, 3 * D), jnp.float32) ** block_levels(splits[11], (D, 3 * D), ((0, 8),), -0.2, 0.2), 2.1455721314206366e-12, 8.582288525682547e-12)
    attn_out = bell_draw(splits[12], (D, D), (D // 32) ** -0.5, 1.25, ((0, 8),), jnp.float32)
    attn_out_m = bell_draw(splits[13], (D, D), (0.01 * NPARAM ** -0.5), 7.62939453125e-06, ((0, 8),), jnp.float32)
    attn_out_v = jnp.clip(2.1455721314206366e-12 + 6.43671639426191e-12 * jax.random.uniform(splits[14], (D, D), jnp.float32) ** block_levels(splits[14], (D, D), ((0, 8),), -0.2, 0.2), 2.1455721314206366e-12, 8.582288525682547e-12)
    mlp_in = bell_draw(splits[15], (D, FF), D ** -0.5, 0.21875, ((0, 8),), jnp.float32)
    mlp_in_m = bell_draw(splits[16], (D, FF), (0.01 * NPARAM ** -0.5), 7.62939453125e-06, ((0, 8),), jnp.float32)
    mlp_in_v = jnp.clip(2.1455721314206366e-12 + 6.43671639426191e-12 * jax.random.uniform(splits[17], (D, FF), jnp.float32) ** block_levels(splits[17], (D, FF), ((0, 8),), -0.2, 0.2), 2.1455721314206366e-12, 8.582288525682547e-12)
    mlp_out = bell_draw(splits[18], (FF, D), FF ** -0.5, 0.109375, ((0, 8),), jnp.float32)
    mlp_out_m = bell_draw(splits[19], (FF, D), (0.01 * NPARAM ** -0.5), 7.62939453125e-06, ((0, 8),), jnp.float32)
    mlp_out_v = jnp.clip(2.1455721314206366e-12 + 6.43671639426191e-12 * jax.random.uniform(splits[20], (FF, D), jnp.float32) ** block_levels(splits[20], (FF, D), ((0, 8),), -0.2, 0.2), 2.1455721314206366e-12, 8.582288525682547e-12)
    small = draw_small(jax.random.fold_in(splits[24], 71), 0)
    small_m = bell_draw(splits[22], (NSMALL,), (0.03 * NPARAM ** -0.5), 2.6702880859375e-05, ((0, 8),), jnp.float32)
    small_v = jnp.clip(1.9310148965945295e-11 + 5.7930446897835886e-11 * jax.random.uniform(splits[23], (NSMALL,), jnp.float32) ** block_levels(splits[23], (NSMALL,), ((0, 8),), -0.2, 0.2), 1.9310148965945295e-11, 7.724059586378118e-11)
    return dict(tok_ids=tok_ids, targets=targets, loss_mask=loss_mask, embed=embed, embed_m=embed_m, embed_v=embed_v, posit=posit, posit_m=posit_m, posit_v=posit_v, attn_in=attn_in, attn_in_m=attn_in_m, attn_in_v=attn_in_v, attn_out=attn_out, attn_out_m=attn_out_m, attn_out_v=attn_out_v, mlp_in=mlp_in, mlp_in_m=mlp_in_m, mlp_in_v=mlp_in_v, mlp_out=mlp_out, mlp_out_m=mlp_out_m, mlp_out_v=mlp_out_v, small=small, small_m=small_m, small_v=small_v)


EPS = 1e-05
CLIP_LIMIT = 0.01
BETA = 0.5
DECAY = 0.1
ADAM_EPS = 1e-08
HIGH = lax.Precision.HIGHEST

@jax.custom_vjp
def low(v):
    return lax.optimization_barrier(v.astype(jnp.bfloat16)).astype(jnp.float32)

@jax.custom_vjp
def low_back(v):
    return v

def low_keep(v):
    return (low(v), None)

def low_pass(kept, grad):
    return (grad,)

def back_keep(v):
    return (v, None)

def back_low(kept, grad):
    return (low(grad),)
low.defvjp(low_keep, low_pass)
low_back.defvjp(back_keep, back_low)

def matmul(left, right):
    return jnp.dot(left, right, precision=HIGH, preferred_element_type=jnp.float32)

def layer_norm(values, gain, bias):
    center = values - lax.optimization_barrier(jnp.mean(values, axis=-1, keepdims=True))
    spread = lax.optimization_barrier(jnp.mean(center * center, axis=-1, keepdims=True))
    return center * lax.rsqrt(spread + EPS) * gain + bias

def features(inner):
    return jnp.concatenate([jax.nn.softmax(inner, axis=-1), jax.nn.softmax(-inner, axis=-1)], axis=-1)

def unpack(vector):
    cuts = [D, D, D, D, D, D, 3 * D, D, FF, D, H * HD * HD, H * HD * HD]
    pieces = []
    offset = 0
    for piece_len in cuts:
        pieces.append(vector[offset:offset + piece_len])
        offset = offset + piece_len
    return pieces

def rate_list():
    return (2.0 * D ** (-0.5), 0.5, D ** (-0.5), (32.0 / D) ** 0.5, D ** (-0.5), FF ** (-0.5), 0.1)

def block_loss(weights, ids_block, target_block, mask_block):
    table, positions, w_qkv, w_out, w_up, w_down, vector = weights
    gain_one, bias_one, gain_two, bias_two, gain_fin, bias_fin, bias_qkv, bias_out, bias_up, bias_down, map_query, map_key = unpack(vector)
    map_query = map_query.reshape(H, HD, HD)
    map_key = map_key.reshape(H, HD, HD)
    seq_count, length = ids_block.shape
    start_sum = low_back(jnp.take(table, ids_block, axis=0) + positions[:length][None])
    normed_one = low(layer_norm(start_sum, gain_one, bias_one)).reshape(-1, D)
    project = low_back(matmul(normed_one, w_qkv)).reshape(seq_count, length, 3 * D) + bias_qkv
    queries = low(project[..., :D]).reshape(seq_count, length, H, HD)
    keys_in = low(project[..., D:2 * D]).reshape(seq_count, length, H, HD)
    values_in = low(project[..., 2 * D:]).reshape(seq_count, length, H, HD)
    inner_q = low_back(jnp.einsum('gshd,hde->gshe', queries, map_query, precision=HIGH))
    inner_k = low_back(jnp.einsum('gshd,hde->gshe', keys_in, map_key, precision=HIGH))
    feat_q = low(features(inner_q))
    feat_k = low(features(inner_k))
    rows_idx = lax.broadcasted_iota(jnp.int32, (length, length), 0)
    cols_idx = lax.broadcasted_iota(jnp.int32, (length, length), 1)
    causal = (rows_idx >= cols_idx).astype(jnp.float32)
    scores = low_back(jnp.einsum('gthf,gshf->ghts', feat_q, feat_k, precision=HIGH) * causal)
    totals = lax.optimization_barrier(jnp.sum(scores, axis=-1))
    numer = low_back(jnp.einsum('ghts,gshd->gthd', low(scores), values_in, precision=HIGH))
    attended = numer / jnp.transpose(totals, (0, 2, 1))[..., None]
    att_low = low(attended).reshape(-1, D)
    resid_one = start_sum + low_back(matmul(att_low, w_out)).reshape(seq_count, length, D) + bias_out
    normed_two = low(layer_norm(resid_one, gain_two, bias_two)).reshape(-1, D)
    pre_act = low_back(matmul(normed_two, w_up)) + bias_up
    act_low = low(jax.nn.gelu(pre_act, approximate=True))
    resid_two = resid_one + (low_back(matmul(act_low, w_down)) + bias_down).reshape(seq_count, length, D)
    final = low(layer_norm(resid_two, gain_fin, bias_fin)).reshape(-1, D)
    logits = low_back(jnp.dot(final, table.T, precision=HIGH, preferred_element_type=jnp.float32))
    log_total = jax.nn.logsumexp(logits, axis=-1)
    picked = jnp.take_along_axis(logits, target_block.reshape(-1, 1), axis=1)[:, 0]
    return jnp.sum((log_total - picked) * mask_block.reshape(-1).astype(jnp.float32))

def total_loss(params, tok_ids, targets, loss_mask, token_total):
    weights = tuple((low(weight) for weight in params))
    per_block = 1
    while per_block * 2 * SEQ <= 4096 and SEQS % (per_block * 2) == 0:
        per_block = per_block * 2
    shaped = (tok_ids.reshape(-1, per_block, SEQ), targets.reshape(-1, per_block, SEQ), loss_mask.reshape(-1, per_block, SEQ))
    checked = jax.checkpoint(block_loss)

    def one_block(block):
        return checked(weights, block[0], block[1], block[2])
    sums = lax.map(one_block, shaped)
    return jnp.sum(sums) / token_total

def reference(tok_ids, targets, loss_mask, embed, embed_m, embed_v, posit, posit_m, posit_v, attn_in, attn_in_m, attn_in_v, attn_out, attn_out_m, attn_out_v, mlp_in, mlp_in_m, mlp_in_v, mlp_out, mlp_out_m, mlp_out_v, small, small_m, small_v):
    params = (embed, posit, attn_in, attn_out, mlp_in, mlp_out, small)
    firsts = (embed_m, posit_m, attn_in_m, attn_out_m, mlp_in_m, mlp_out_m, small_m)
    seconds = (embed_v, posit_v, attn_in_v, attn_out_v, mlp_in_v, mlp_out_v, small_v)
    token_total = jnp.sum(loss_mask.astype(jnp.float32))

    def wrapped(*weights):
        return total_loss(weights, tok_ids, targets, loss_mask, token_total)
    loss, pull = jax.vjp(wrapped, *params)
    grads = pull(jnp.ones_like(loss))
    norm_sq = jnp.float32(0.0)
    for gradient in grads:
        norm_sq = norm_sq + jnp.sum(gradient * gradient)
    grad_norm = jnp.sqrt(norm_sq)
    scale = CLIP_LIMIT / jnp.maximum(grad_norm, CLIP_LIMIT)
    bias_fix = 1.0 - BETA ** STEP
    results = [loss, grad_norm]
    for weight, first_old, second_old, gradient, rate in zip(params, firsts, seconds, grads, rate_list()):
        clipped = gradient * scale
        first_new = BETA * first_old + (1.0 - BETA) * clipped
        second_new = BETA * second_old + (1.0 - BETA) * clipped * clipped
        weight_new = weight - rate * (first_new / bias_fix / (jnp.sqrt(second_new / bias_fix) + ADAM_EPS) + DECAY * weight)
        results.extend([weight_new, first_new, second_new])
    return tuple(results)
```

```python
import functools
from functools import reduce

import jax
import jax.numpy as jnp
from jax import lax
from jax.experimental import pallas as pl
from jax.experimental.pallas import tpu as pltpu
from jax.sharding import PartitionSpec as P

D = 768
H = 12
HD = 64
FF = 3072
STEP = 2


EPS = 1e-05
CLIP_LIMIT = 0.01
BETA = 0.5
DECAY = 0.1
ADAM_EPS = 1e-08


def combined_all(value, axis, join):
    pieces = jax.tree.map(lambda part: lax.all_gather(part, axis), value)
    head = jax.tree.map(lambda part: part[0], pieces)
    tail = jax.tree.map(lambda part: part[1:], pieces)
    subtotal, _ = lax.scan(lambda subtotal, piece: (join(subtotal, piece), None), head, tail)
    return subtotal


def dense(left, right):
    return jnp.dot(left, right, preferred_element_type=jnp.float32)


def dense_tn(left, right):
    return lax.dot_general(
        left, right, (((0,), (0,)), ((), ())), preferred_element_type=jnp.float32
    )


def dense_nt(left, right):
    return lax.dot_general(
        left, right, (((1,), (1,)), ((), ())), preferred_element_type=jnp.float32
    )


def layer_norm(values, gain, bias):
    center = values - jnp.mean(values, axis=-1, keepdims=True)
    spread = jnp.mean(center * center, axis=-1, keepdims=True)
    return center * lax.rsqrt(spread + EPS) * gain + bias


def features(inner):
    return jnp.concatenate(
        [jax.nn.softmax(inner, axis=-1), jax.nn.softmax(-inner, axis=-1)], axis=-1
    )


def gelu_tanh(values):
    return jax.nn.gelu(values, approximate=True)


def unpack(vector):
    cuts = [D, D, D, D, D, D, 3 * D, D, FF, D, H * HD * HD, H * HD * HD]
    pieces = []
    offset = 0
    for piece_len in cuts:
        pieces.append(vector[offset : offset + piece_len])
        offset = offset + piece_len
    return pieces


def rate_list():
    return (2.0 * D ** (-0.5), 0.5, D ** (-0.5), (32.0 / D) ** 0.5, D ** (-0.5), FF ** (-0.5), 0.1)


def norm_pull(values, gain, bias, cotangent):
    unused, pull = jax.vjp(layer_norm, values, gain, bias)
    return pull(cotangent)


def causal_mask(length):
    rows_idx = lax.broadcasted_iota(jnp.int32, (length, length), 0)
    cols_idx = lax.broadcasted_iota(jnp.int32, (length, length), 1)
    return (rows_idx >= cols_idx).astype(jnp.float32)


def layer_forward(inputs, mats, pieces):
    w_qkv, w_out, w_up, w_down = mats
    (
        gain_one,
        bias_one,
        gain_two,
        bias_two,
        gain_fin,
        bias_fin,
        bias_qkv,
        bias_out,
        bias_up,
        bias_down,
        map_query,
        map_key,
    ) = pieces
    length = inputs.shape[0]
    normed_one = layer_norm(inputs, gain_one, bias_one).astype(jnp.bfloat16)
    project = dense(normed_one, w_qkv) + bias_qkv
    queries = project[:, :D].astype(jnp.bfloat16).reshape(length, H, HD)
    keys_in = project[:, D : 2 * D].astype(jnp.bfloat16).reshape(length, H, HD)
    values_in = project[:, 2 * D :].astype(jnp.bfloat16).reshape(length, H, HD)
    maps_q = map_query.reshape(H, HD, HD).astype(jnp.bfloat16)
    maps_k = map_key.reshape(H, HD, HD).astype(jnp.bfloat16)
    inner_q = jnp.einsum("shd,hde->she", queries, maps_q, preferred_element_type=jnp.float32)
    inner_k = jnp.einsum("shd,hde->she", keys_in, maps_k, preferred_element_type=jnp.float32)
    feat_q = features(inner_q).astype(jnp.bfloat16)
    feat_k = features(inner_k).astype(jnp.bfloat16)
    scores = jnp.einsum(
        "thf,shf->hts", feat_q, feat_k, preferred_element_type=jnp.float32
    ) * causal_mask(length)
    totals = jnp.sum(scores, axis=-1)
    scores_low = scores.astype(jnp.bfloat16)
    numer = jnp.einsum("hts,shd->thd", scores_low, values_in, preferred_element_type=jnp.float32)
    attended = numer / jnp.transpose(totals)[:, :, None]
    att_low = attended.reshape(length, D).astype(jnp.bfloat16)
    resid_one = inputs + dense(att_low, w_out) + bias_out
    normed_two = layer_norm(resid_one, gain_two, bias_two).astype(jnp.bfloat16)
    pre_act = dense(normed_two, w_up) + bias_up
    act_low = gelu_tanh(pre_act).astype(jnp.bfloat16)
    resid_two = resid_one + dense(act_low, w_down) + bias_down
    final = layer_norm(resid_two, gain_fin, bias_fin)
    saved = (
        normed_one,
        queries,
        keys_in,
        values_in,
        maps_q,
        maps_k,
        inner_q,
        inner_k,
        feat_q,
        feat_k,
        scores_low,
        totals,
        numer,
        att_low,
        resid_one,
        normed_two,
        pre_act,
        act_low,
        resid_two,
    )
    return (final, saved)


def layer_backward(inputs, mats, pieces, saved, d_final):
    w_qkv, w_out, w_up, w_down = mats
    (
        gain_one,
        bias_one,
        gain_two,
        bias_two,
        gain_fin,
        bias_fin,
        bias_qkv,
        bias_out,
        bias_up,
        bias_down,
        map_query,
        map_key,
    ) = pieces
    (
        normed_one,
        queries,
        keys_in,
        values_in,
        maps_q,
        maps_k,
        inner_q,
        inner_k,
        feat_q,
        feat_k,
        scores_low,
        totals,
        numer,
        att_low,
        resid_one,
        normed_two,
        pre_act,
        act_low,
        resid_two,
    ) = saved
    length = inputs.shape[0]
    d_resid_two, d_gain_fin, d_bias_fin = norm_pull(resid_two, gain_fin, bias_fin, d_final)
    d_bias_down = jnp.sum(d_resid_two, axis=0)
    d_down_low = d_resid_two.astype(jnp.bfloat16)
    g_down = dense_tn(act_low, d_down_low)
    d_act = dense_nt(d_down_low, w_down)
    unused, gelu_back = jax.vjp(gelu_tanh, pre_act)
    d_pre = gelu_back(d_act)[0]
    d_bias_up = jnp.sum(d_pre, axis=0)
    d_pre_low = d_pre.astype(jnp.bfloat16)
    g_up = dense_tn(normed_two, d_pre_low)
    d_normed_two = dense_nt(d_pre_low, w_up)
    d_resid_part, d_gain_two, d_bias_two = norm_pull(resid_one, gain_two, bias_two, d_normed_two)
    d_resid_one = d_resid_two + d_resid_part
    d_bias_out = jnp.sum(d_resid_one, axis=0)
    d_out_low = d_resid_one.astype(jnp.bfloat16)
    g_out = dense_tn(att_low, d_out_low)
    d_attended = dense_nt(d_out_low, w_out).reshape(length, H, HD)
    inverse = 1.0 / jnp.transpose(totals)
    d_numer_low = (d_attended * inverse[:, :, None]).astype(jnp.bfloat16)
    d_totals = jnp.transpose(-jnp.sum(d_attended * numer, axis=-1) * inverse * inverse)
    d_scores = jnp.einsum(
        "thd,shd->hts", d_numer_low, values_in, preferred_element_type=jnp.float32
    )
    d_scores_low = ((d_scores + d_totals[:, :, None]) * causal_mask(length)).astype(jnp.bfloat16)
    d_values = jnp.einsum(
        "hts,thd->shd", scores_low, d_numer_low, preferred_element_type=jnp.float32
    )
    d_feat_q = jnp.einsum("hts,shf->thf", d_scores_low, feat_k, preferred_element_type=jnp.float32)
    d_feat_k = jnp.einsum("hts,thf->shf", d_scores_low, feat_q, preferred_element_type=jnp.float32)
    unused, pull_q = jax.vjp(features, inner_q)
    unused, pull_k = jax.vjp(features, inner_k)
    d_inner_q = pull_q(d_feat_q)[0].astype(jnp.bfloat16)
    d_inner_k = pull_k(d_feat_k)[0].astype(jnp.bfloat16)
    g_map_q = jnp.einsum("shd,she->hde", queries, d_inner_q, preferred_element_type=jnp.float32)
    g_map_k = jnp.einsum("shd,she->hde", keys_in, d_inner_k, preferred_element_type=jnp.float32)
    d_queries = jnp.einsum("she,hde->shd", d_inner_q, maps_q, preferred_element_type=jnp.float32)
    d_keys = jnp.einsum("she,hde->shd", d_inner_k, maps_k, preferred_element_type=jnp.float32)
    d_project = jnp.concatenate(
        [d_queries.reshape(length, D), d_keys.reshape(length, D), d_values.reshape(length, D)],
        axis=1,
    )
    d_bias_qkv = jnp.sum(d_project, axis=0)
    d_project_low = d_project.astype(jnp.bfloat16)
    g_qkv = dense_tn(normed_one, d_project_low)
    d_normed_one = dense_nt(d_project_low, w_qkv)
    d_input_part, d_gain_one, d_bias_one = norm_pull(inputs, gain_one, bias_one, d_normed_one)
    d_inputs = d_resid_one + d_input_part
    g_small = jnp.concatenate(
        [
            d_gain_one,
            d_bias_one,
            d_gain_two,
            d_bias_two,
            d_gain_fin,
            d_bias_fin,
            d_bias_qkv,
            d_bias_out,
            d_bias_up,
            d_bias_down,
            g_map_q.reshape(-1),
            g_map_k.reshape(-1),
        ]
    )
    return (d_inputs, (g_qkv, g_out, g_up, g_down), g_small)


def adam_update(weight, first_old, second_old, gradient, rate):
    first_new = BETA * first_old + (1.0 - BETA) * gradient
    second_new = BETA * second_old + (1.0 - BETA) * gradient * gradient
    bias_fix = 1.0 - BETA**STEP
    weight_new = weight - rate * (
        first_new / bias_fix / (jnp.sqrt(second_new / bias_fix) + ADAM_EPS) + DECAY * weight
    )
    return (weight_new, first_new, second_new)


def combine_lse(first_part, second_part):
    top = jnp.maximum(first_part[0], second_part[0])
    merged = first_part[1] * jnp.exp(first_part[0] - top) + second_part[1] * jnp.exp(
        second_part[0] - top
    )
    return (top, merged, first_part[2] + second_part[2])


def body_general(
    tok_ids,
    targets,
    loss_mask,
    embed,
    embed_m,
    embed_v,
    posit,
    posit_m,
    posit_v,
    attn_in,
    attn_in_m,
    attn_in_v,
    attn_out,
    attn_out_m,
    attn_out_v,
    mlp_in,
    mlp_in_m,
    mlp_in_v,
    mlp_out,
    mlp_out_m,
    mlp_out_v,
    small,
    small_m,
    small_v,
):
    rank = lax.axis_index("fsdp")
    length = tok_ids.shape[1]
    all_ids, all_targets, all_mask = (
        lax.all_gather(tok_ids, "fsdp", axis=0, tiled=True),
        lax.all_gather(targets, "fsdp", axis=0, tiled=True),
        lax.all_gather(loss_mask, "fsdp", axis=0, tiled=True),
    )
    all_ids = all_ids.reshape(-1)
    all_targets = all_targets.reshape(-1)
    mask_all = all_mask.reshape(-1).astype(jnp.float32)
    pos_full, w_qkv, w_out, w_up, w_down, small_full = (
        lax.all_gather(posit.astype(jnp.bfloat16), "fsdp", axis=0, tiled=True),
        lax.all_gather(attn_in.astype(jnp.bfloat16), "fsdp", axis=0, tiled=True),
        lax.all_gather(attn_out.astype(jnp.bfloat16), "fsdp", axis=0, tiled=True),
        lax.all_gather(mlp_in.astype(jnp.bfloat16), "fsdp", axis=0, tiled=True),
        lax.all_gather(mlp_out.astype(jnp.bfloat16), "fsdp", axis=0, tiled=True),
        lax.all_gather(small.astype(jnp.bfloat16), "fsdp", axis=0, tiled=True),
    )
    mats = (w_qkv, w_out, w_up, w_down)
    pieces = unpack(small_full.astype(jnp.float32))
    shard_rows = embed.shape[0]
    first_row = rank * shard_rows
    table = embed.astype(jnp.bfloat16)
    local_ids = all_ids - first_row
    inside = (local_ids >= 0) & (local_ids < shard_rows)
    safe_ids = jnp.clip(local_ids, 0, shard_rows - 1)
    looked = jnp.where(
        inside[:, None], jnp.take(table, safe_ids, axis=0), jnp.zeros((), jnp.bfloat16)
    )
    embedded = lax.psum_scatter(looked, "fsdp", scatter_dimension=0, tiled=True).astype(jnp.float32)
    inputs = embedded + pos_full[:length].astype(jnp.float32)
    final, saved = layer_forward(inputs, mats, pieces)
    final_low = final.astype(jnp.bfloat16)
    target_local = all_targets - first_row
    piece = lax.all_gather(final_low, "fsdp", axis=0, tiled=True)
    logits = dense_nt(piece, table)
    row_max = jnp.max(logits, axis=1)
    row_sum = jnp.sum(jnp.exp(logits - row_max[:, None]), axis=1)
    columns = lax.broadcasted_iota(jnp.int32, logits.shape, 1)
    row_hit = jnp.sum(jnp.where(columns == target_local[:, None], logits, 0.0), axis=1)
    maxes = row_max
    sums = row_sum
    hits = row_hit
    maxes, sums, hits = combined_all((maxes, sums, hits), "fsdp", combine_lse)
    log_total = maxes + jnp.log(sums)
    own_terms = lax.dynamic_slice_in_dim((log_total - hits) * mask_all, rank * length, length)
    loss_sum, token_total = lax.psum(
        (jnp.sum(own_terms), jnp.sum(loss_mask.astype(jnp.float32))), ("dp", "fsdp")
    )
    loss = loss_sum / token_total
    columns = lax.broadcasted_iota(jnp.int32, logits.shape, 1)
    onehot = jnp.where(columns == target_local[:, None], 1.0, 0.0)
    d_logits = (
        (jnp.exp(logits - log_total[:, None]) - onehot) * (mask_all / token_total)[:, None]
    ).astype(jnp.bfloat16)
    g_table = dense_tn(d_logits, piece)
    d_final = lax.psum_scatter(dense(d_logits, table), "fsdp", scatter_dimension=0, tiled=True)
    d_inputs, mat_grads, g_small = layer_backward(inputs, mats, pieces, saved, d_final)
    g_qkv, g_out, g_up, g_down = mat_grads
    d_low = d_inputs.astype(jnp.bfloat16)
    all_back = lax.all_gather(d_low, "fsdp", axis=0, tiled=True)
    g_table = g_table.at[safe_ids].add(
        jnp.where(inside[:, None], all_back.astype(jnp.float32), 0.0)
    )
    g_posit = jnp.concatenate(
        [d_low.astype(jnp.float32), jnp.zeros((pos_full.shape[0] - length, D), jnp.float32)], axis=0
    )
    layer_grads = (g_posit, g_qkv, g_out, g_up, g_down, g_small)
    owned = (
        lax.psum_scatter(
            layer_grads[0].astype(jnp.bfloat16), "fsdp", scatter_dimension=0, tiled=True
        ).astype(jnp.float32),
        lax.psum_scatter(
            layer_grads[1].astype(jnp.bfloat16), "fsdp", scatter_dimension=0, tiled=True
        ).astype(jnp.float32),
        lax.psum_scatter(
            layer_grads[2].astype(jnp.bfloat16), "fsdp", scatter_dimension=0, tiled=True
        ).astype(jnp.float32),
        lax.psum_scatter(
            layer_grads[3].astype(jnp.bfloat16), "fsdp", scatter_dimension=0, tiled=True
        ).astype(jnp.float32),
        lax.psum_scatter(
            layer_grads[4].astype(jnp.bfloat16), "fsdp", scatter_dimension=0, tiled=True
        ).astype(jnp.float32),
        lax.psum_scatter(
            layer_grads[5].astype(jnp.bfloat16), "fsdp", scatter_dimension=0, tiled=True
        ).astype(jnp.float32),
    )
    grads = tuple(
        lax.psum((g_table, owned[0], owned[1], owned[2], owned[3], owned[4], owned[5]), "dp")
    )
    local_sq = reduce(
        lambda acc, gradient: acc + jnp.sum(gradient * gradient), grads, jnp.float32(0.0)
    )
    grad_norm = jnp.sqrt(lax.psum(local_sq, "fsdp"))
    scale = CLIP_LIMIT / jnp.maximum(grad_norm, CLIP_LIMIT)
    params = (embed, posit, attn_in, attn_out, mlp_in, mlp_out, small)
    firsts = (embed_m, posit_m, attn_in_m, attn_out_m, mlp_in_m, mlp_out_m, small_m)
    seconds = (embed_v, posit_v, attn_in_v, attn_out_v, mlp_in_v, mlp_out_v, small_v)
    results = [loss, grad_norm]
    for weight, first_old, second_old, gradient, rate in zip(
        params, firsts, seconds, grads, rate_list()
    ):
        results.extend(adam_update(weight, first_old, second_old, gradient * scale, rate))
    return tuple(results)


BF = jnp.bfloat16
F32 = jnp.float32
MESH = pl.DeviceIdType.MESH
TOK = 128
GROUP = 8 * TOK
VBLK = 1280


def params(cid=None, mib=56):
    if cid is None:
        return pltpu.CompilerParams(vmem_limit_bytes=mib << 20)
    return pltpu.CompilerParams(
        collective_id=cid, has_side_effects=True, vmem_limit_bytes=mib << 20
    )


def vmem(count):
    return [pl.BlockSpec(memory_space=pltpu.VMEM)] * count


def sems(count):
    return [pltpu.SemaphoreType.DMA((count,))] * 2


class Link:
    def __init__(self, send, recv):
        self.send, self.recv, self.used = send, recv, 0

    def copy(self, src, dst, peer, land=None):
        slot = self.used
        self.used += 1
        return pltpu.make_async_remote_copy(
            src_ref=src,
            dst_ref=dst,
            send_sem=self.send.at[slot],
            recv_sem=self.recv.at[slot if land is None else land],
            device_id=peer,
            device_id_type=MESH,
        )


def greet(peers, extra=None):
    barrier = pltpu.get_barrier_semaphore()
    for peer in peers:
        pl.semaphore_signal(barrier, inc=1, device_id=peer, device_id_type=MESH)
    if extra is None:
        pl.semaphore_wait(barrier, len(peers))
    else:
        flag, peer = extra

        @pl.when(flag)
        def _():
            pl.semaphore_signal(barrier, inc=1, device_id=peer, device_id_type=MESH)

        pl.semaphore_wait(barrier, len(peers) + flag.astype(jnp.int32))


def middle_chip(fs):
    chip = fs // 2
    return (chip == 1) | (chip == 2)


def ids_kernel(x_ref, o_ref, send, recv):
    dp, fs = lax.axis_index("dp"), lax.axis_index("fsdp")
    line = [(dp, fs ^ k) for k in range(1, 8)]
    plane = [(dp ^ k, fs) for k in range(1, 4)]
    greet(line + plane)
    link = Link(send, recv)
    o_ref[dp, fs] = x_ref[...]
    first = [link.copy(x_ref, o_ref.at[dp, fs], peer) for peer in line]
    for copy in first:
        copy.start()
    for copy in first:
        copy.wait()
    second = [link.copy(o_ref.at[dp], o_ref.at[dp], peer) for peer in plane]
    for copy in second:
        copy.start()
    for copy in second:
        copy.wait()


def gather_ids(x):
    return pl.pallas_call(
        ids_kernel,
        out_shape=jax.ShapeDtypeStruct((4, 8, 8, TOK), jnp.int32),
        in_specs=vmem(1),
        out_specs=vmem(1)[0],
        scratch_shapes=sems(10),
        compiler_params=params(1, 4),
    )(x)


class Spread:
    slots = 8

    def __init__(self, link, dp, fs, x_ref, o_ref):
        self.fs, self.x, self.o = fs, x_ref, o_ref
        self.mid = middle_chip(fs)
        near, far, across, pair = [(dp, fs ^ k) for k in (2, 4, 6, 1)]
        mine = o_ref.at[fs]
        self.near = link.copy(x_ref, mine, near)
        self.far = link.copy(x_ref, mine, far)
        land = link.used
        self.across = link.copy(x_ref, mine, across, land)
        self.relay = link.copy(o_ref.at[fs ^ 4], o_ref.at[fs ^ 4], near, land)
        self.pair = [
            link.copy(x_ref if k == 0 else o_ref.at[fs ^ k], o_ref.at[fs ^ k], pair)
            for k in (0, 2, 4, 6)
        ]

    def start(self):
        self.far.start()
        self.near.start()

        @pl.when(self.mid)
        def _():
            self.across.start()

        self.pair[0].start()
        self.o[self.fs] = self.x[...]

    def finish(self):
        self.far.wait_recv()

        @pl.when(self.mid)
        def _():
            self.relay.start()

        self.pair[2].start()
        self.near.wait_recv()
        self.pair[1].start()
        self.across.wait_recv()
        self.pair[3].start()
        for copy in self.pair:
            copy.wait()
        self.near.wait_send()
        self.far.wait_send()

        @pl.when(self.mid)
        def _():
            self.across.wait_send()
            self.relay.wait_send()


class Fold:
    slots = 8

    def __init__(self, link, dp, fs, x_ref, part, sums, got):
        self.fs, self.x, self.part, self.sums, self.got = fs, x_ref, part, sums, got
        self.mid = middle_chip(fs)
        near, far, across, pair = [(dp, fs ^ k) for k in (2, 4, 6, 1)]
        self.pair = [link.copy(x_ref.at[fs ^ 1 ^ (2 * k)], part.at[k], pair) for k in range(4)]
        self.near = link.copy(sums.at[1], got.at[0], near)
        self.far = link.copy(sums.at[2], got.at[1], far)
        self.across = link.copy(sums.at[3], got.at[2], across)
        self.relay = link.copy(sums.at[3], got.at[3], near)

    def start(self):
        for k in (3, 2, 1, 0):
            self.pair[k].start()

    def add(self, k):
        self.pair[k].wait_recv()
        return self.x[self.fs ^ (2 * k)].astype(F32) + self.part[k].astype(F32)

    def middle(self):
        self.sums[3] = self.add(3).astype(BF)

        @pl.when(self.mid)
        def _():
            self.across.start()

        @pl.when(jnp.logical_not(self.mid))
        def _():
            self.relay.start()
            self.sums[2] = self.add(2).astype(BF)
            self.far.start()

        self.sums[1] = self.add(1).astype(BF)
        self.near.start()

        @pl.when(self.mid)
        def _():
            both = self.add(2)
            self.relay.wait_recv()
            self.sums[2] = (both + self.got[3].astype(F32)).astype(BF)
            self.far.start()

    def finish(self, o_ref):
        o_ref[...] = self.add(0)
        self.near.wait_recv()
        o_ref[...] += self.got[0].astype(F32)
        self.far.wait_recv()
        o_ref[...] += self.got[1].astype(F32)

        @pl.when(self.mid)
        def _():
            self.across.wait_recv()
            o_ref[...] += self.got[2].astype(F32)
            self.across.wait_send()

        @pl.when(jnp.logical_not(self.mid))
        def _():
            self.relay.wait_send()

        for copy in self.pair:
            copy.wait_send()
        self.near.wait_send()
        self.far.wait_send()


def fold_scratch():
    return [pltpu.VMEM((4, TOK, D), BF)] * 3


def line_peers(dp, fs):
    return [(dp, fs ^ k) for k in (1, 2, 4)], (middle_chip(fs), (dp, fs ^ 6))


def spread_kernel(x_ref, o_ref, send, recv):
    dp, fs = lax.axis_index("dp"), lax.axis_index("fsdp")
    greet(*line_peers(dp, fs))
    spread = Spread(Link(send, recv), dp, fs, x_ref, o_ref)
    spread.start()
    spread.finish()


def gather_tokens(x):
    out = pl.pallas_call(
        spread_kernel,
        out_shape=jax.ShapeDtypeStruct((8, TOK, D), BF),
        in_specs=vmem(1),
        out_specs=vmem(1)[0],
        scratch_shapes=sems(Spread.slots),
        compiler_params=params(2, 16),
    )(x)
    return out.reshape(GROUP, D)


def fold_kernel(x_ref, o_ref, part, sums, got, send, recv):
    dp, fs = lax.axis_index("dp"), lax.axis_index("fsdp")
    greet(*line_peers(dp, fs))
    fold = Fold(Link(send, recv), dp, fs, x_ref, part, sums, got)
    fold.start()
    fold.middle()
    fold.finish(o_ref)


def sum_tokens(x):
    return pl.pallas_call(
        fold_kernel,
        out_shape=jax.ShapeDtypeStruct((TOK, D), F32),
        in_specs=vmem(1),
        out_specs=vmem(1)[0],
        scratch_shapes=fold_scratch() + sems(Fold.slots),
        compiler_params=params(3, 16),
    )(x.reshape(8, TOK, D))


def start_kernel(
    look, wqo, w1, small, pos, e_out, wqo_out, w1_out, small_out, pos_out, part, sums, got, send, recv
):
    dp, fs = lax.axis_index("dp"), lax.axis_index("fsdp")
    core = fs % 2
    line = [(dp, fs ^ k) for k in range(1, 8)]
    plane = [(dp ^ k, fs) for k in range(1, 4)]
    pair = (dp, fs ^ 1)
    greet(line + plane)
    link = Link(send, recv)
    fold = Fold(link, dp, fs, look, part, sums, got)
    fold.start()
    high, wide = wqo.shape[0] // 2, wqo.shape[1] // 2
    rows = pl.ds(pl.multiple_of((dp // 2) * high, 16), high)
    cols = pl.ds(pl.multiple_of((dp % 2) * wide, 128), wide)
    down = [
        link.copy(wqo.at[rows, cols], wqo_out.at[fs, rows, cols], (dp, fs ^ k)) for k in (2, 4, 6)
    ]
    for copy in down:
        copy.start()
    own_pair = link.copy(wqo, wqo_out.at[fs], pair)
    own_pair.start()
    fold.middle()
    tiny = [link.copy(small, small_out.at[fs], peer) for peer in line]
    for copy in tiny:
        copy.start()
    width = w1_out.shape[2]

    def strip(who):
        return w1.at[:, pl.ds(pl.multiple_of(who * width, 128), width)]

    strips = [link.copy(strip(fs ^ k), w1_out.at[fs], (dp, fs ^ k)) for k in range(1, 8)]
    for copy in strips:
        copy.start()
    land = link.used
    pos_line = [link.copy(pos_out, pos_out, (dp, k), land) for k in (2, 4, 6)]
    pos_pair = link.copy(pos_out, pos_out, pair, land)

    @pl.when(fs == 0)
    def _():
        pos_out[...] = pos[...]
        for copy in pos_line:
            copy.start()

    wqo_out[fs] = wqo[...]
    w1_out[fs] = strip(fs)[...]
    small_out[fs] = small[...]
    side = []
    for index, k in enumerate((2, 4, 6)):
        down[index].wait_recv()
        piece = wqo_out.at[fs ^ k, rows, cols]
        copies = [link.copy(piece, piece, peer) for peer in plane]
        for copy in copies:
            copy.start()
        side.append(copies)

    @pl.when(fs != 0)
    def _():
        pos_pair.wait_recv()

    @pl.when(core == 0)
    def _():
        pos_pair.start()

    fold.finish(e_out)
    pairs = [own_pair]
    for index, k in enumerate((2, 4, 6)):
        for copy in side[index]:
            copy.wait_recv()
        copy = link.copy(wqo_out.at[fs ^ k], wqo_out.at[fs ^ k], pair)
        copy.start()
        pairs.append(copy)
    for copy in tiny + strips + pairs:
        copy.wait()
    for copy in down + side[0] + side[1] + side[2]:
        copy.wait_send()

    @pl.when(core == 0)
    def _():
        pos_pair.wait_send()

    @pl.when(fs == 0)
    def _():
        for copy in pos_line:
            copy.wait_send()


def start_exchange(looked, wqo, w1, small, pos):
    n_sems = Fold.slots + 3 + 1 + 7 + 7 + 4 + 9 + 3
    return pl.pallas_call(
        start_kernel,
        out_shape=(
            jax.ShapeDtypeStruct((TOK, D), F32),
            jax.ShapeDtypeStruct((8,) + wqo.shape, BF),
            jax.ShapeDtypeStruct((8, w1.shape[0], w1.shape[1] // 8), BF),
            jax.ShapeDtypeStruct((8,) + small.shape, BF),
            jax.ShapeDtypeStruct(pos.shape, BF),
        ),
        in_specs=vmem(5),
        out_specs=tuple(vmem(5)),
        scratch_shapes=fold_scratch() + sems(n_sems),
        compiler_params=params(4, 40),
    )(looked.reshape(8, TOK, D), wqo, w1, small, pos)


def lse_kernel(st_ref, o_ref, mine, got, send, recv):
    dp, fs = lax.axis_index("dp"), lax.axis_index("fsdp")
    line = [(dp, fs ^ k) for k in range(1, 8)]
    plane = [(dp ^ k, fs) for k in range(1, 4)]
    greet(line + plane)
    link = Link(send, recv)
    blocks = st_ref.shape[0]
    top = st_ref[0, 0:1, :]
    for b in range(1, blocks):
        top = jnp.maximum(top, st_ref[b, 0:1, :])
    total = jnp.zeros_like(top)
    hit = jnp.zeros_like(top)
    for b in range(blocks):
        total = total + st_ref[b, 1:2, :] * jnp.exp(st_ref[b, 0:1, :] - top)
        hit = hit + st_ref[b, 2:3, :]
    for j in range(8):
        lanes = slice(j * TOK, (j + 1) * TOK)
        mine[j : j + 1, :] = top[:, lanes]
        mine[8 + j : 9 + j, :] = total[:, lanes]
        mine[16 + j : 17 + j, :] = hit[:, lanes]
    first = [link.copy(mine, got.at[fs], peer) for peer in line]
    for copy in first:
        copy.start()
    got[fs] = mine[...]
    for copy in first:
        copy.wait()
    top = got[0, 0:8, :]
    for j in range(1, 8):
        top = jnp.maximum(top, got[j, 0:8, :])
    total = jnp.zeros_like(top)
    hit = jnp.zeros_like(top)
    for j in range(8):
        total = total + got[j, 8:16, :] * jnp.exp(got[j, 0:8, :] - top)
        hit = hit + got[j, 16:24, :]
    o_ref[dp, 0:8, :] = top + jnp.log(total)
    o_ref[dp, 8:16, :] = hit
    second = [link.copy(o_ref.at[dp], o_ref.at[dp], peer) for peer in plane]
    for copy in second:
        copy.start()
    for copy in second:
        copy.wait()


def combine_stats(stats):
    return pl.pallas_call(
        lse_kernel,
        out_shape=jax.ShapeDtypeStruct((4, 16, TOK), F32),
        in_specs=vmem(1),
        out_specs=vmem(1)[0],
        scratch_shapes=[pltpu.VMEM((24, TOK), F32), pltpu.VMEM((8, 24, TOK), F32)] + sems(10),
        compiler_params=params(5, 8),
    )(stats)


def total_kernel(x_ref, o_ref, got, send, recv):
    dp, fs = lax.axis_index("dp"), lax.axis_index("fsdp")
    line = [(dp, fs ^ k) for k in range(1, 8)]
    greet(line)
    link = Link(send, recv)
    copies = [link.copy(x_ref, got.at[fs], peer) for peer in line]
    for copy in copies:
        copy.start()
    got[fs] = x_ref[...]
    for copy in copies:
        copy.wait()
    total = got[0]
    for j in range(1, 8):
        total = total + got[j]
    o_ref[...] = total


def line_total(x):
    return pl.pallas_call(
        total_kernel,
        out_shape=jax.ShapeDtypeStruct((8, TOK), F32),
        in_specs=vmem(1),
        out_specs=vmem(1)[0],
        scratch_shapes=[pltpu.VMEM((8, 8, TOK), F32)] + sems(7),
        compiler_params=params(6, 4),
    )(x)


def logits_kernel(rows_here, e_ref, h_ref, t_ref, p_ref, st_ref):
    block = pl.program_id(0)
    logits = dense_nt(e_ref[...], h_ref[...])
    row = lax.broadcasted_iota(jnp.int32, logits.shape, 0) + block * VBLK
    logits = jnp.where(row < rows_here, logits, -jnp.inf)
    top = jnp.max(logits, 0, keepdims=True)
    st_ref[0, 2:3, :] = jnp.sum(jnp.where(row == t_ref[...], logits, 0.0), 0, keepdims=True)
    grown = jnp.exp(logits - top)
    st_ref[0, 0:1, :] = top
    st_ref[0, 1:2, :] = jnp.sum(grown, 0, keepdims=True)
    p_ref[...] = grown.astype(BF)


def own_logits(rows_here, table, hidden, target):
    blocks = table.shape[0] // VBLK
    return pl.pallas_call(
        functools.partial(logits_kernel, rows_here),
        grid=(blocks,),
        in_specs=[
            pl.BlockSpec((VBLK, D), lambda i: (i, 0)),
            pl.BlockSpec((GROUP, D), lambda i: (0, 0)),
            pl.BlockSpec((1, GROUP), lambda i: (0, 0)),
        ],
        out_specs=[
            pl.BlockSpec((VBLK, GROUP), lambda i: (i, 0)),
            pl.BlockSpec((1, 8, GROUP), lambda i: (i, 0, 0)),
        ],
        out_shape=[
            jax.ShapeDtypeStruct((table.shape[0], GROUP), BF),
            jax.ShapeDtypeStruct((blocks, 8, GROUP), F32),
        ],
        compiler_params=params(),
    )(table, hidden, target)


def dhf_kernel(p_ref, st_ref, lse_ref, w_ref, t_ref, e_ref, o_ref, acc):
    block = pl.program_id(0)
    row = lax.broadcasted_iota(jnp.int32, p_ref.shape, 0) + block * VBLK
    factor = w_ref[...] * jnp.exp(st_ref[0, 0:1, :] - lse_ref[...])
    grad = p_ref[...].astype(F32) * factor - jnp.where(row == t_ref[...], w_ref[...], 0.0)
    grad = grad.astype(BF)

    @pl.when(block == 0)
    def _():
        acc[...] = dense_tn(grad, e_ref[...])

    @pl.when(block > 0)
    def _():
        acc[...] += dense_tn(grad, e_ref[...])

    @pl.when(block == pl.num_programs(0) - 1)
    def _():
        o_ref[...] = acc[...].astype(BF)


def final_cotangent(grown, stats, lse, weight, target, table):
    blocks = table.shape[0] // VBLK
    line = pl.BlockSpec((1, GROUP), lambda i: (0, 0))
    return pl.pallas_call(
        dhf_kernel,
        grid=(blocks,),
        in_specs=[
            pl.BlockSpec((VBLK, GROUP), lambda i: (i, 0)),
            pl.BlockSpec((1, 8, GROUP), lambda i: (i, 0, 0)),
            line,
            line,
            line,
            pl.BlockSpec((VBLK, D), lambda i: (i, 0)),
        ],
        out_specs=pl.BlockSpec((GROUP, D), lambda i: (0, 0)),
        out_shape=jax.ShapeDtypeStruct((GROUP, D), BF),
        scratch_shapes=[pltpu.VMEM((GROUP, D), F32)],
        compiler_params=params(),
    )(grown, stats, lse, weight, target, table)


def table_kernel(e_ref, h_ref, lse_ref, w_ref, t_ref, o_ref):
    block = pl.program_id(0)
    table = e_ref[...]
    o_ref[...] = jnp.zeros_like(o_ref)

    def group(d, carry):
        hidden = h_ref[d]
        logits = dense_nt(table, hidden)
        row = lax.broadcasted_iota(jnp.int32, logits.shape, 0) + block * VBLK
        grad = jnp.exp(logits - lse_ref[d]) * w_ref[d]
        grad = grad - jnp.where(row == t_ref[d], w_ref[d], 0.0)
        o_ref[...] += dense(grad.astype(BF), hidden)
        return carry

    lax.fori_loop(0, h_ref.shape[0], group, 0)


def table_gradient(table, hidden, lse, weight, target):
    blocks = table.shape[0] // VBLK
    line = pl.BlockSpec((4, 1, GROUP), lambda i: (0, 0, 0))
    return pl.pallas_call(
        table_kernel,
        grid=(blocks,),
        in_specs=[
            pl.BlockSpec((VBLK, D), lambda i: (i, 0)),
            pl.BlockSpec((4, GROUP, D), lambda i: (0, 0, 0)),
            line,
            line,
            line,
        ],
        out_specs=pl.BlockSpec((VBLK, D), lambda i: (i, 0)),
        out_shape=jax.ShapeDtypeStruct((table.shape[0], D), F32),
        compiler_params=params(),
    )(table, hidden, lse, weight, target)


def scatter_kernel(count_ref, list_ref, row_ref, g_hbm, d_ref, o_hbm, sq_ref, held, sem):
    rows_here = o_hbm.shape[0]
    load = pltpu.make_async_copy(g_hbm.at[pl.ds(0, rows_here)], held, sem.at[0])
    load.start()
    load.wait()

    def one(i, carry):
        token = list_ref[i]
        row = row_ref[token]
        held[pl.ds(row, 1), :] += d_ref[pl.ds(token, 1), :]
        return carry

    lax.fori_loop(0, count_ref[0], one, 0)
    store = pltpu.make_async_copy(held, o_hbm, sem.at[1])
    store.start()
    step = 48

    def square(i, carry):
        part = held[pl.ds(pl.multiple_of(i * step, 8), step), :]
        part = part * part
        for j in range(step // 8):
            carry = carry + part[j * 8 : (j + 1) * 8, :]
        return carry

    sq_ref[...] = lax.fori_loop(0, rows_here // step, square, jnp.zeros((8, D), F32))
    store.wait()


def add_rows(count, order, rows, gradient, d_tokens, rows_here):
    return pl.pallas_call(
        scatter_kernel,
        out_shape=(
            jax.ShapeDtypeStruct((rows_here, D), F32),
            jax.ShapeDtypeStruct((8, D), F32),
        ),
        in_specs=[pl.BlockSpec(memory_space=pltpu.SMEM)] * 3
        + [pl.BlockSpec(memory_space=pl.ANY)]
        + vmem(1),
        out_specs=(pl.BlockSpec(memory_space=pl.ANY), vmem(1)[0]),
        scratch_shapes=[pltpu.VMEM((rows_here, D), F32), pltpu.SemaphoreType.DMA((2,))],
        compiler_params=params(),
    )(count, order, rows, gradient, d_tokens)


def attention_forward(inputs, w_qkv, w_out, pieces):
    gain_one, bias_one = pieces[0], pieces[1]
    bias_qkv, bias_out, map_query, map_key = pieces[6], pieces[7], pieces[10], pieces[11]
    length = inputs.shape[0]
    normed_one = layer_norm(inputs, gain_one, bias_one).astype(BF)
    project = dense(normed_one, w_qkv) + bias_qkv
    queries = project[:, :D].astype(BF).reshape(length, H, HD)
    keys_in = project[:, D : 2 * D].astype(BF).reshape(length, H, HD)
    values_in = project[:, 2 * D :].astype(BF).reshape(length, H, HD)
    maps_q = map_query.reshape(H, HD, HD).astype(BF)
    maps_k = map_key.reshape(H, HD, HD).astype(BF)
    inner_q = jnp.einsum("shd,hde->she", queries, maps_q, preferred_element_type=F32)
    inner_k = jnp.einsum("shd,hde->she", keys_in, maps_k, preferred_element_type=F32)
    feat_q = features(inner_q).astype(BF)
    feat_k = features(inner_k).astype(BF)
    scores = jnp.einsum("thf,shf->hts", feat_q, feat_k, preferred_element_type=F32) * causal_mask(
        length
    )
    totals = jnp.sum(scores, axis=-1)
    scores_low = scores.astype(BF)
    numer = jnp.einsum("hts,shd->thd", scores_low, values_in, preferred_element_type=F32)
    attended = numer / jnp.transpose(totals)[:, :, None]
    att_low = attended.reshape(length, D).astype(BF)
    resid_one = inputs + dense(att_low, w_out) + bias_out
    saved = (
        normed_one,
        queries,
        keys_in,
        values_in,
        maps_q,
        maps_k,
        inner_q,
        inner_k,
        feat_q,
        feat_k,
        scores_low,
        totals,
        numer,
        att_low,
    )
    return resid_one, saved


def attention_backward(inputs, w_qkv, w_out, pieces, saved, d_resid_one):
    gain_one, bias_one = pieces[0], pieces[1]
    (
        normed_one,
        queries,
        keys_in,
        values_in,
        maps_q,
        maps_k,
        inner_q,
        inner_k,
        feat_q,
        feat_k,
        scores_low,
        totals,
        numer,
        att_low,
    ) = saved
    length = inputs.shape[0]
    d_bias_out = jnp.sum(d_resid_one, axis=0)
    d_out_low = d_resid_one.astype(BF)
    g_out = dense_tn(att_low, d_out_low)
    d_attended = dense_nt(d_out_low, w_out).reshape(length, H, HD)
    inverse = 1.0 / jnp.transpose(totals)
    d_numer_low = (d_attended * inverse[:, :, None]).astype(BF)
    d_totals = jnp.transpose(-jnp.sum(d_attended * numer, axis=-1) * inverse * inverse)
    d_scores = jnp.einsum("thd,shd->hts", d_numer_low, values_in, preferred_element_type=F32)
    d_scores_low = ((d_scores + d_totals[:, :, None]) * causal_mask(length)).astype(BF)
    d_values = jnp.einsum("hts,thd->shd", scores_low, d_numer_low, preferred_element_type=F32)
    d_feat_q = jnp.einsum("hts,shf->thf", d_scores_low, feat_k, preferred_element_type=F32)
    d_feat_k = jnp.einsum("hts,thf->shf", d_scores_low, feat_q, preferred_element_type=F32)
    unused, pull_q = jax.vjp(features, inner_q)
    unused, pull_k = jax.vjp(features, inner_k)
    d_inner_q = pull_q(d_feat_q)[0].astype(BF)
    d_inner_k = pull_k(d_feat_k)[0].astype(BF)
    g_map_q = jnp.einsum("shd,she->hde", queries, d_inner_q, preferred_element_type=F32)
    g_map_k = jnp.einsum("shd,she->hde", keys_in, d_inner_k, preferred_element_type=F32)
    d_queries = jnp.einsum("she,hde->shd", d_inner_q, maps_q, preferred_element_type=F32)
    d_keys = jnp.einsum("she,hde->shd", d_inner_k, maps_k, preferred_element_type=F32)
    d_project = jnp.concatenate(
        [d_queries.reshape(length, D), d_keys.reshape(length, D), d_values.reshape(length, D)],
        axis=1,
    )
    d_bias_qkv = jnp.sum(d_project, axis=0)
    d_project_low = d_project.astype(BF)
    g_qkv = dense_tn(normed_one, d_project_low)
    d_normed_one = dense_nt(d_project_low, w_qkv)
    d_input_part, d_gain_one, d_bias_one = norm_pull(inputs, gain_one, bias_one, d_normed_one)
    d_inputs = d_resid_one + d_input_part
    return d_inputs, g_qkv, g_out, (d_gain_one, d_bias_one, d_bias_qkv, d_bias_out, g_map_q, g_map_k)


def body(
    tok_ids,
    targets,
    loss_mask,
    embed,
    embed_m,
    embed_v,
    posit,
    posit_m,
    posit_v,
    attn_in,
    attn_in_m,
    attn_in_v,
    attn_out,
    attn_out_m,
    attn_out_v,
    mlp_in,
    mlp_in_m,
    mlp_in_v,
    mlp_out,
    mlp_out_m,
    mlp_out_v,
    small,
    small_m,
    small_v,
):
    dp, rank = lax.axis_index("dp"), lax.axis_index("fsdp")
    shard_rows = embed.shape[0]
    first_row = rank * shard_rows
    mine = jnp.concatenate([tok_ids, targets, loss_mask, jnp.zeros((5, TOK), jnp.int32)], axis=0)
    shared = gather_ids(mine)
    all_ids = shared[:, :, 0, :].reshape(4, GROUP)
    all_targets = shared[:, :, 1, :].reshape(4, GROUP)
    all_mask = shared[:, :, 2, :].reshape(4, GROUP).astype(F32)
    token_total = jnp.sum(all_mask)
    weight = all_mask / token_total
    local_ids = all_ids - first_row
    inside = (local_ids >= 0) & (local_ids < shard_rows)
    safe_ids = jnp.clip(local_ids, 0, shard_rows - 1)
    target_local = all_targets - first_row
    target_here = (target_local >= 0) & (target_local < shard_rows)
    target_local = jnp.where(target_here, target_local, -1)
    group_ids = lax.dynamic_index_in_dim(safe_ids, dp, 0, False)
    group_in = lax.dynamic_index_in_dim(inside, dp, 0, False)
    own_target = lax.dynamic_slice_in_dim(target_local, dp, 1, 0)
    own_weight = lax.dynamic_slice_in_dim(weight, dp, 1, 0)
    looked = jnp.where(group_in[:, None], jnp.take(embed, group_ids, axis=0), 0.0).astype(BF)
    table = jnp.pad(embed.astype(BF), ((0, -shard_rows % VBLK), (0, 0)))

    small_pad = -small.shape[0] % (16 * TOK)
    w_two = mlp_out.astype(BF)
    embedded, wqo, w_one, small_full, positions = start_exchange(
        looked,
        jnp.concatenate([attn_in, attn_out], axis=1).astype(BF),
        mlp_in.astype(BF),
        jnp.pad(small, (0, small_pad)).astype(BF).reshape(-1, TOK),
        posit.astype(BF),
    )
    wqo = wqo.reshape(D, 4 * D)
    w_qkv, w_out = wqo[:, : 3 * D], wqo[:, 3 * D :]
    w_one = w_one.reshape(D, FF // 8)
    small_full = small_full.reshape(8, -1)[:, : small.shape[0]].reshape(-1)
    pieces = unpack(small_full.astype(F32))
    gain_two, bias_two, gain_fin, bias_fin = pieces[2:6]
    bias_up, bias_down = pieces[8], pieces[9]
    own_up = lax.dynamic_slice_in_dim(bias_up, rank * (FF // 8), FF // 8)

    inputs = embedded + positions.astype(F32)
    resid_one, saved = attention_forward(inputs, w_qkv, w_out, pieces)
    normed_two = gather_tokens(layer_norm(resid_one, gain_two, bias_two).astype(BF))
    pre_act = dense(normed_two, w_one) + own_up
    act_low = gelu_tanh(pre_act).astype(BF)
    resid_two = resid_one + sum_tokens(dense(act_low, w_two).astype(BF)) + bias_down
    final = gather_tokens(layer_norm(resid_two, gain_fin, bias_fin).astype(BF))
    all_final = lax.all_gather(final, "dp")

    grown, stats = own_logits(shard_rows, table, final, own_target)
    shared_stats = combine_stats(stats)
    lse = shared_stats[:, :8, :].reshape(4, GROUP)
    hits = shared_stats[:, 8:, :].reshape(4, GROUP)
    loss = jnp.sum((lse - hits) * all_mask) / token_total
    own_lse = lax.dynamic_slice_in_dim(lse, dp, 1, 0)
    d_final = sum_tokens(
        final_cotangent(grown, stats, own_lse, own_weight, own_target, table)
    )

    d_resid_two, d_gain_fin, d_bias_fin = norm_pull(resid_two, gain_fin, bias_fin, d_final)
    d_bias_down = jnp.sum(d_resid_two, axis=0)
    d_down_low = gather_tokens(d_resid_two.astype(BF))
    g_down = dense_tn(act_low, d_down_low)
    d_act = dense_nt(d_down_low, w_two)
    unused, gelu_back = jax.vjp(gelu_tanh, pre_act)
    d_pre = gelu_back(d_act)[0]
    d_bias_up = lax.dynamic_update_slice_in_dim(
        jnp.zeros((FF,), F32), jnp.sum(d_pre, axis=0), rank * (FF // 8), 0
    )
    d_pre_low = d_pre.astype(BF)
    g_up = dense_tn(normed_two, d_pre_low)
    d_normed_two = sum_tokens(dense_nt(d_pre_low, w_one).astype(BF))
    d_resid_part, d_gain_two, d_bias_two = norm_pull(resid_one, gain_two, bias_two, d_normed_two)
    d_resid_one = d_resid_two + d_resid_part
    d_inputs, g_qkv, g_out, small_parts = attention_backward(
        inputs, w_qkv, w_out, pieces, saved, d_resid_one
    )
    d_gain_one, d_bias_one, d_bias_qkv, d_bias_out, g_map_q, g_map_k = small_parts
    d_low = d_inputs.astype(BF)
    group_back = gather_tokens(d_low)
    all_back = lax.all_gather(group_back, "dp")

    g_small = jnp.concatenate(
        [
            d_gain_one,
            d_bias_one,
            d_gain_two,
            d_bias_two,
            d_gain_fin,
            d_bias_fin,
            d_bias_qkv,
            d_bias_out,
            d_bias_up,
            d_bias_down,
            g_map_q.reshape(-1),
            g_map_k.reshape(-1),
        ]
    )
    g_posit = jnp.concatenate(
        [d_low, jnp.zeros((8 * posit.shape[0] - TOK, D), BF)], axis=0
    )

    def owned(value):
        return lax.psum_scatter(value.astype(BF), "fsdp", scatter_dimension=0, tiled=True)

    g_up_own = lax.all_to_all(
        g_up.astype(BF).reshape(8, D // 8, FF // 8), "fsdp", 0, 0, tiled=False
    )
    g_up_own = jnp.transpose(g_up_own, (1, 0, 2)).reshape(D // 8, FF)
    layer_grads = lax.psum(
        (
            owned(g_posit),
            owned(g_qkv),
            owned(g_out),
            g_up_own,
            g_down.astype(BF),
            lax.psum_scatter(g_small, "fsdp", scatter_dimension=0, tiled=True),
        ),
        "dp",
    )

    g_table = table_gradient(
        table,
        all_final,
        lse.reshape(4, 1, GROUP),
        weight.reshape(4, 1, GROUP),
        target_local.reshape(4, 1, GROUP),
    )
    flat_in = inside.reshape(-1)
    index = lax.iota(jnp.int32, flat_in.shape[0])
    order = lax.sort(jnp.where(flat_in, index, index + flat_in.shape[0]))
    order = jnp.where(order < flat_in.shape[0], order, 0)
    count = jnp.sum(flat_in.astype(jnp.int32)).reshape(1)
    g_table, table_sq = add_rows(
        count,
        order,
        safe_ids.reshape(-1),
        g_table,
        all_back.reshape(-1, D).astype(F32),
        shard_rows,
    )
    grads = (g_table,) + tuple(g.astype(F32) for g in layer_grads)
    local_sq = reduce(
        lambda acc, gradient: acc + jnp.sum(gradient * gradient), grads[1:], jnp.sum(table_sq)
    )
    total_sq = line_total(jnp.broadcast_to(local_sq, (8, TOK)))
    grad_norm = jnp.sqrt(total_sq[0, 0])
    scale = CLIP_LIMIT / jnp.maximum(grad_norm, CLIP_LIMIT)
    params_all = (embed, posit, attn_in, attn_out, mlp_in, mlp_out, small)
    firsts = (embed_m, posit_m, attn_in_m, attn_out_m, mlp_in_m, mlp_out_m, small_m)
    seconds = (embed_v, posit_v, attn_in_v, attn_out_v, mlp_in_v, mlp_out_v, small_v)
    results = [loss, grad_norm]
    for w_old, first_old, second_old, gradient, rate in zip(
        params_all, firsts, seconds, grads, rate_list()
    ):
        results.extend(adam_update(w_old, first_old, second_old, gradient * scale, rate))
    return tuple(results)


def solution(mesh):
    fits = mesh.shape["dp"] == 4 and mesh.shape["fsdp"] == 8
    step = body if fits else body_general
    in_specs = (
        P(("dp", "fsdp"), None),
        P(("dp", "fsdp"), None),
        P(("dp", "fsdp"), None),
        P("fsdp", None),
        P("fsdp", None),
        P("fsdp", None),
        P("fsdp", None),
        P("fsdp", None),
        P("fsdp", None),
        P("fsdp", None),
        P("fsdp", None),
        P("fsdp", None),
        P("fsdp", None),
        P("fsdp", None),
        P("fsdp", None),
        P("fsdp", None),
        P("fsdp", None),
        P("fsdp", None),
        P("fsdp", None),
        P("fsdp", None),
        P("fsdp", None),
        P("fsdp"),
        P("fsdp"),
        P("fsdp"),
    )
    out_specs = (
        P(),
        P(),
        P("fsdp", None),
        P("fsdp", None),
        P("fsdp", None),
        P("fsdp", None),
        P("fsdp", None),
        P("fsdp", None),
        P("fsdp", None),
        P("fsdp", None),
        P("fsdp", None),
        P("fsdp", None),
        P("fsdp", None),
        P("fsdp", None),
        P("fsdp", None),
        P("fsdp", None),
        P("fsdp", None),
        P("fsdp", None),
        P("fsdp", None),
        P("fsdp", None),
        P("fsdp"),
        P("fsdp"),
        P("fsdp"),
    )
    return jax.shard_map(step, mesh=mesh, in_specs=in_specs, out_specs=out_specs, check_vma=False)
```

```python
import functools
from functools import reduce

import jax
import jax.numpy as jnp
from jax import lax
from jax.experimental import pallas as pl
from jax.experimental.pallas import tpu as pltpu
from jax.sharding import PartitionSpec as P

D = 768
H = 12
HD = 64
FF = 3072
STEP = 2


EPS = 1e-05
CLIP_LIMIT = 0.01
BETA = 0.5
DECAY = 0.1
ADAM_EPS = 1e-08


def combined_all(value, axis, join):
    pieces = jax.tree.map(lambda part: lax.all_gather(part, axis), value)
    head = jax.tree.map(lambda part: part[0], pieces)
    tail = jax.tree.map(lambda part: part[1:], pieces)
    subtotal, _ = lax.scan(lambda subtotal, piece: (join(subtotal, piece), None), head, tail)
    return subtotal


def dense(left, right):
    return jnp.dot(left, right, preferred_element_type=jnp.float32)


def dense_tn(left, right):
    return lax.dot_general(
        left, right, (((0,), (0,)), ((), ())), preferred_element_type=jnp.float32
    )


def dense_nt(left, right):
    return lax.dot_general(
        left, right, (((1,), (1,)), ((), ())), preferred_element_type=jnp.float32
    )


def layer_norm(values, gain, bias):
    center = values - jnp.mean(values, axis=-1, keepdims=True)
    spread = jnp.mean(center * center, axis=-1, keepdims=True)
    return center * lax.rsqrt(spread + EPS) * gain + bias


def features(inner):
    return jnp.concatenate(
        [jax.nn.softmax(inner, axis=-1), jax.nn.softmax(-inner, axis=-1)], axis=-1
    )


def gelu_tanh(values):
    return jax.nn.gelu(values, approximate=True)


def unpack(vector):
    cuts = [D, D, D, D, D, D, 3 * D, D, FF, D, H * HD * HD, H * HD * HD]
    pieces = []
    offset = 0
    for piece_len in cuts:
        pieces.append(vector[offset : offset + piece_len])
        offset = offset + piece_len
    return pieces


def rate_list():
    return (2.0 * D ** (-0.5), 0.5, D ** (-0.5), (32.0 / D) ** 0.5, D ** (-0.5), FF ** (-0.5), 0.1)


def norm_pull(values, gain, bias, cotangent):
    unused, pull = jax.vjp(layer_norm, values, gain, bias)
    return pull(cotangent)


def causal_mask(length):
    rows_idx = lax.broadcasted_iota(jnp.int32, (length, length), 0)
    cols_idx = lax.broadcasted_iota(jnp.int32, (length, length), 1)
    return (rows_idx >= cols_idx).astype(jnp.float32)


def layer_forward(inputs, mats, pieces):
    w_qkv, w_out, w_up, w_down = mats
    (
        gain_one,
        bias_one,
        gain_two,
        bias_two,
        gain_fin,
        bias_fin,
        bias_qkv,
        bias_out,
        bias_up,
        bias_down,
        map_query,
        map_key,
    ) = pieces
    length = inputs.shape[0]
    normed_one = layer_norm(inputs, gain_one, bias_one).astype(jnp.bfloat16)
    project = dense(normed_one, w_qkv) + bias_qkv
    queries = project[:, :D].astype(jnp.bfloat16).reshape(length, H, HD)
    keys_in = project[:, D : 2 * D].astype(jnp.bfloat16).reshape(length, H, HD)
    values_in = project[:, 2 * D :].astype(jnp.bfloat16).reshape(length, H, HD)
    maps_q = map_query.reshape(H, HD, HD).astype(jnp.bfloat16)
    maps_k = map_key.reshape(H, HD, HD).astype(jnp.bfloat16)
    inner_q = jnp.einsum("shd,hde->she", queries, maps_q, preferred_element_type=jnp.float32)
    inner_k = jnp.einsum("shd,hde->she", keys_in, maps_k, preferred_element_type=jnp.float32)
    feat_q = features(inner_q).astype(jnp.bfloat16)
    feat_k = features(inner_k).astype(jnp.bfloat16)
    scores = jnp.einsum(
        "thf,shf->hts", feat_q, feat_k, preferred_element_type=jnp.float32
    ) * causal_mask(length)
    totals = jnp.sum(scores, axis=-1)
    scores_low = scores.astype(jnp.bfloat16)
    numer = jnp.einsum("hts,shd->thd", scores_low, values_in, preferred_element_type=jnp.float32)
    attended = numer / jnp.transpose(totals)[:, :, None]
    att_low = attended.reshape(length, D).astype(jnp.bfloat16)
    resid_one = inputs + dense(att_low, w_out) + bias_out
    normed_two = layer_norm(resid_one, gain_two, bias_two).astype(jnp.bfloat16)
    pre_act = dense(normed_two, w_up) + bias_up
    act_low = gelu_tanh(pre_act).astype(jnp.bfloat16)
    resid_two = resid_one + dense(act_low, w_down) + bias_down
    final = layer_norm(resid_two, gain_fin, bias_fin)
    saved = (
        normed_one,
        queries,
        keys_in,
        values_in,
        maps_q,
        maps_k,
        inner_q,
        inner_k,
        feat_q,
        feat_k,
        scores_low,
        totals,
        numer,
        att_low,
        resid_one,
        normed_two,
        pre_act,
        act_low,
        resid_two,
    )
    return (final, saved)


def layer_backward(inputs, mats, pieces, saved, d_final):
    w_qkv, w_out, w_up, w_down = mats
    (
        gain_one,
        bias_one,
        gain_two,
        bias_two,
        gain_fin,
        bias_fin,
        bias_qkv,
        bias_out,
        bias_up,
        bias_down,
        map_query,
        map_key,
    ) = pieces
    (
        normed_one,
        queries,
        keys_in,
        values_in,
        maps_q,
        maps_k,
        inner_q,
        inner_k,
        feat_q,
        feat_k,
        scores_low,
        totals,
        numer,
        att_low,
        resid_one,
        normed_two,
        pre_act,
        act_low,
        resid_two,
    ) = saved
    length = inputs.shape[0]
    d_resid_two, d_gain_fin, d_bias_fin = norm_pull(resid_two, gain_fin, bias_fin, d_final)
    d_bias_down = jnp.sum(d_resid_two, axis=0)
    d_down_low = d_resid_two.astype(jnp.bfloat16)
    g_down = dense_tn(act_low, d_down_low)
    d_act = dense_nt(d_down_low, w_down)
    unused, gelu_back = jax.vjp(gelu_tanh, pre_act)
    d_pre = gelu_back(d_act)[0]
    d_bias_up = jnp.sum(d_pre, axis=0)
    d_pre_low = d_pre.astype(jnp.bfloat16)
    g_up = dense_tn(normed_two, d_pre_low)
    d_normed_two = dense_nt(d_pre_low, w_up)
    d_resid_part, d_gain_two, d_bias_two = norm_pull(resid_one, gain_two, bias_two, d_normed_two)
    d_resid_one = d_resid_two + d_resid_part
    d_bias_out = jnp.sum(d_resid_one, axis=0)
    d_out_low = d_resid_one.astype(jnp.bfloat16)
    g_out = dense_tn(att_low, d_out_low)
    d_attended = dense_nt(d_out_low, w_out).reshape(length, H, HD)
    inverse = 1.0 / jnp.transpose(totals)
    d_numer_low = (d_attended * inverse[:, :, None]).astype(jnp.bfloat16)
    d_totals = jnp.transpose(-jnp.sum(d_attended * numer, axis=-1) * inverse * inverse)
    d_scores = jnp.einsum(
        "thd,shd->hts", d_numer_low, values_in, preferred_element_type=jnp.float32
    )
    d_scores_low = ((d_scores + d_totals[:, :, None]) * causal_mask(length)).astype(jnp.bfloat16)
    d_values = jnp.einsum(
        "hts,thd->shd", scores_low, d_numer_low, preferred_element_type=jnp.float32
    )
    d_feat_q = jnp.einsum("hts,shf->thf", d_scores_low, feat_k, preferred_element_type=jnp.float32)
    d_feat_k = jnp.einsum("hts,thf->shf", d_scores_low, feat_q, preferred_element_type=jnp.float32)
    unused, pull_q = jax.vjp(features, inner_q)
    unused, pull_k = jax.vjp(features, inner_k)
    d_inner_q = pull_q(d_feat_q)[0].astype(jnp.bfloat16)
    d_inner_k = pull_k(d_feat_k)[0].astype(jnp.bfloat16)
    g_map_q = jnp.einsum("shd,she->hde", queries, d_inner_q, preferred_element_type=jnp.float32)
    g_map_k = jnp.einsum("shd,she->hde", keys_in, d_inner_k, preferred_element_type=jnp.float32)
    d_queries = jnp.einsum("she,hde->shd", d_inner_q, maps_q, preferred_element_type=jnp.float32)
    d_keys = jnp.einsum("she,hde->shd", d_inner_k, maps_k, preferred_element_type=jnp.float32)
    d_project = jnp.concatenate(
        [d_queries.reshape(length, D), d_keys.reshape(length, D), d_values.reshape(length, D)],
        axis=1,
    )
    d_bias_qkv = jnp.sum(d_project, axis=0)
    d_project_low = d_project.astype(jnp.bfloat16)
    g_qkv = dense_tn(normed_one, d_project_low)
    d_normed_one = dense_nt(d_project_low, w_qkv)
    d_input_part, d_gain_one, d_bias_one = norm_pull(inputs, gain_one, bias_one, d_normed_one)
    d_inputs = d_resid_one + d_input_part
    g_small = jnp.concatenate(
        [
            d_gain_one,
            d_bias_one,
            d_gain_two,
            d_bias_two,
            d_gain_fin,
            d_bias_fin,
            d_bias_qkv,
            d_bias_out,
            d_bias_up,
            d_bias_down,
            g_map_q.reshape(-1),
            g_map_k.reshape(-1),
        ]
    )
    return (d_inputs, (g_qkv, g_out, g_up, g_down), g_small)


def adam_update(weight, first_old, second_old, gradient, rate):
    first_new = BETA * first_old + (1.0 - BETA) * gradient
    second_new = BETA * second_old + (1.0 - BETA) * gradient * gradient
    bias_fix = 1.0 - BETA**STEP
    weight_new = weight - rate * (
        first_new / bias_fix / (jnp.sqrt(second_new / bias_fix) + ADAM_EPS) + DECAY * weight
    )
    return (weight_new, first_new, second_new)


def combine_lse(first_part, second_part):
    top = jnp.maximum(first_part[0], second_part[0])
    merged = first_part[1] * jnp.exp(first_part[0] - top) + second_part[1] * jnp.exp(
        second_part[0] - top
    )
    return (top, merged, first_part[2] + second_part[2])


def body_general(
    tok_ids,
    targets,
    loss_mask,
    embed,
    embed_m,
    embed_v,
    posit,
    posit_m,
    posit_v,
    attn_in,
    attn_in_m,
    attn_in_v,
    attn_out,
    attn_out_m,
    attn_out_v,
    mlp_in,
    mlp_in_m,
    mlp_in_v,
    mlp_out,
    mlp_out_m,
    mlp_out_v,
    small,
    small_m,
    small_v,
):
    rank = lax.axis_index("fsdp")
    length = tok_ids.shape[1]
    all_ids, all_targets, all_mask = (
        lax.all_gather(tok_ids, "fsdp", axis=0, tiled=True),
        lax.all_gather(targets, "fsdp", axis=0, tiled=True),
        lax.all_gather(loss_mask, "fsdp", axis=0, tiled=True),
    )
    all_ids = all_ids.reshape(-1)
    all_targets = all_targets.reshape(-1)
    mask_all = all_mask.reshape(-1).astype(jnp.float32)
    pos_full, w_qkv, w_out, w_up, w_down, small_full = (
        lax.all_gather(posit.astype(jnp.bfloat16), "fsdp", axis=0, tiled=True),
        lax.all_gather(attn_in.astype(jnp.bfloat16), "fsdp", axis=0, tiled=True),
        lax.all_gather(attn_out.astype(jnp.bfloat16), "fsdp", axis=0, tiled=True),
        lax.all_gather(mlp_in.astype(jnp.bfloat16), "fsdp", axis=0, tiled=True),
        lax.all_gather(mlp_out.astype(jnp.bfloat16), "fsdp", axis=0, tiled=True),
        lax.all_gather(small.astype(jnp.bfloat16), "fsdp", axis=0, tiled=True),
    )
    mats = (w_qkv, w_out, w_up, w_down)
    pieces = unpack(small_full.astype(jnp.float32))
    shard_rows = embed.shape[0]
    first_row = rank * shard_rows
    table = embed.astype(jnp.bfloat16)
    local_ids = all_ids - first_row
    inside = (local_ids >= 0) & (local_ids < shard_rows)
    safe_ids = jnp.clip(local_ids, 0, shard_rows - 1)
    looked = jnp.where(
        inside[:, None], jnp.take(table, safe_ids, axis=0), jnp.zeros((), jnp.bfloat16)
    )
    embedded = lax.psum_scatter(looked, "fsdp", scatter_dimension=0, tiled=True).astype(jnp.float32)
    inputs = embedded + pos_full[:length].astype(jnp.float32)
    final, saved = layer_forward(inputs, mats, pieces)
    final_low = final.astype(jnp.bfloat16)
    target_local = all_targets - first_row
    piece = lax.all_gather(final_low, "fsdp", axis=0, tiled=True)
    logits = dense_nt(piece, table)
    row_max = jnp.max(logits, axis=1)
    row_sum = jnp.sum(jnp.exp(logits - row_max[:, None]), axis=1)
    columns = lax.broadcasted_iota(jnp.int32, logits.shape, 1)
    row_hit = jnp.sum(jnp.where(columns == target_local[:, None], logits, 0.0), axis=1)
    maxes = row_max
    sums = row_sum
    hits = row_hit
    maxes, sums, hits = combined_all((maxes, sums, hits), "fsdp", combine_lse)
    log_total = maxes + jnp.log(sums)
    own_terms = lax.dynamic_slice_in_dim((log_total - hits) * mask_all, rank * length, length)
    loss_sum, token_total = lax.psum(
        (jnp.sum(own_terms), jnp.sum(loss_mask.astype(jnp.float32))), ("dp", "fsdp")
    )
    loss = loss_sum / token_total
    columns = lax.broadcasted_iota(jnp.int32, logits.shape, 1)
    onehot = jnp.where(columns == target_local[:, None], 1.0, 0.0)
    d_logits = (
        (jnp.exp(logits - log_total[:, None]) - onehot) * (mask_all / token_total)[:, None]
    ).astype(jnp.bfloat16)
    g_table = dense_tn(d_logits, piece)
    d_final = lax.psum_scatter(dense(d_logits, table), "fsdp", scatter_dimension=0, tiled=True)
    d_inputs, mat_grads, g_small = layer_backward(inputs, mats, pieces, saved, d_final)
    g_qkv, g_out, g_up, g_down = mat_grads
    d_low = d_inputs.astype(jnp.bfloat16)
    all_back = lax.all_gather(d_low, "fsdp", axis=0, tiled=True)
    g_table = g_table.at[safe_ids].add(
        jnp.where(inside[:, None], all_back.astype(jnp.float32), 0.0)
    )
    g_posit = jnp.concatenate(
        [d_low.astype(jnp.float32), jnp.zeros((pos_full.shape[0] - length, D), jnp.float32)], axis=0
    )
    layer_grads = (g_posit, g_qkv, g_out, g_up, g_down, g_small)
    owned = (
        lax.psum_scatter(
            layer_grads[0].astype(jnp.bfloat16), "fsdp", scatter_dimension=0, tiled=True
        ).astype(jnp.float32),
        lax.psum_scatter(
            layer_grads[1].astype(jnp.bfloat16), "fsdp", scatter_dimension=0, tiled=True
        ).astype(jnp.float32),
        lax.psum_scatter(
            layer_grads[2].astype(jnp.bfloat16), "fsdp", scatter_dimension=0, tiled=True
        ).astype(jnp.float32),
        lax.psum_scatter(
            layer_grads[3].astype(jnp.bfloat16), "fsdp", scatter_dimension=0, tiled=True
        ).astype(jnp.float32),
        lax.psum_scatter(
            layer_grads[4].astype(jnp.bfloat16), "fsdp", scatter_dimension=0, tiled=True
        ).astype(jnp.float32),
        lax.psum_scatter(
            layer_grads[5].astype(jnp.bfloat16), "fsdp", scatter_dimension=0, tiled=True
        ).astype(jnp.float32),
    )
    grads = tuple(
        lax.psum((g_table, owned[0], owned[1], owned[2], owned[3], owned[4], owned[5]), "dp")
    )
    local_sq = reduce(
        lambda acc, gradient: acc + jnp.sum(gradient * gradient), grads, jnp.float32(0.0)
    )
    grad_norm = jnp.sqrt(lax.psum(local_sq, "fsdp"))
    scale = CLIP_LIMIT / jnp.maximum(grad_norm, CLIP_LIMIT)
    params = (embed, posit, attn_in, attn_out, mlp_in, mlp_out, small)
    firsts = (embed_m, posit_m, attn_in_m, attn_out_m, mlp_in_m, mlp_out_m, small_m)
    seconds = (embed_v, posit_v, attn_in_v, attn_out_v, mlp_in_v, mlp_out_v, small_v)
    results = [loss, grad_norm]
    for weight, first_old, second_old, gradient, rate in zip(
        params, firsts, seconds, grads, rate_list()
    ):
        results.extend(adam_update(weight, first_old, second_old, gradient * scale, rate))
    return tuple(results)


BF = jnp.bfloat16
F32 = jnp.float32
MESH = pl.DeviceIdType.MESH
TOK = 128
GROUP = 8 * TOK
VBLK = 1280
FILL = 720
TBLK = 704


def params(cid=None, mib=56):
    if cid is None:
        return pltpu.CompilerParams(vmem_limit_bytes=mib << 20)
    return pltpu.CompilerParams(
        collective_id=cid, has_side_effects=True, vmem_limit_bytes=mib << 20
    )


def vmem(count):
    return [pl.BlockSpec(memory_space=pltpu.VMEM)] * count


def any_specs(count):
    return [pl.BlockSpec(memory_space=pl.ANY)] * count


def hbm_specs(count):
    return [pl.BlockSpec(memory_space=pltpu.HBM)] * count


def sems(count):
    return [pltpu.SemaphoreType.DMA((count,))] * 2


class Link:
    def __init__(self, send, recv):
        self.send, self.recv, self.used = send, recv, 0

    def copy(self, src, dst, peer, land=None):
        slot = self.used
        self.used += 1
        return pltpu.make_async_remote_copy(
            src_ref=src,
            dst_ref=dst,
            send_sem=self.send.at[slot],
            recv_sem=self.recv.at[slot if land is None else land],
            device_id=peer,
            device_id_type=MESH,
        )


def greet(peers, extra=None):
    barrier = pltpu.get_barrier_semaphore()
    for peer in peers:
        pl.semaphore_signal(barrier, inc=1, device_id=peer, device_id_type=MESH)
    if extra is None:
        pl.semaphore_wait(barrier, len(peers))
    else:
        flag, peer = extra

        @pl.when(flag)
        def _():
            pl.semaphore_signal(barrier, inc=1, device_id=peer, device_id_type=MESH)

        pl.semaphore_wait(barrier, len(peers) + flag.astype(jnp.int32))


def middle_chip(fs):
    chip = fs // 2
    return (chip == 1) | (chip == 2)


def quarter_of(who, shape):
    high, wide = shape[-2] // 2, shape[-1] // 2
    return (
        pl.ds(pl.multiple_of((who // 2) * high, 16), high),
        pl.ds(pl.multiple_of((who % 2) * wide, 128), wide),
    )


def first_kernel(
    x_ref, a_in, a_out, m_in, o_ref, zq_ref, wqo, zs_ref, zo_ref, a_wide, o_wide, m_wide, w1, keep, send, recv
):
    dp, fs = lax.axis_index("dp"), lax.axis_index("fsdp")
    chip, core, pair = fs // 2, fs % 2, (dp, fs ^ 1)
    mid = middle_chip(fs)
    line = [(k, (dp, fs ^ k)) for k in range(1, 8)]
    plane = [(k, (dp ^ k, fs)) for k in range(1, 4)]
    fetch = [
        pltpu.make_async_copy(src, dst, keep.at[i])
        for i, (src, dst) in enumerate(((a_in, a_wide), (a_out, o_wide), (m_in, m_wide)))
    ]
    for copy in fetch:
        copy.start()
    greet([peer for k, peer in line + plane])
    link = Link(send, recv)
    o_ref[dp, fs] = x_ref[...]
    ids_line = [link.copy(x_ref, o_ref.at[dp, fs], peer) for k, peer in line]
    ids_plane = [link.copy(o_ref.at[dp], o_ref.at[dp], peer) for k, peer in plane]
    for copy in ids_line:
        copy.start()
    for copy in fetch[:2]:
        copy.wait()
    wqo[:, : 3 * D] = a_wide[...].astype(BF)
    wqo[:, 3 * D :] = o_wide[...].astype(BF)
    near, far, across = [(dp, fs ^ k) for k in (2, 4, 6)]
    piece = wqo.at[quarter_of(dp, wqo.shape)]
    zq_ref[chip] = piece[...]
    to_near = link.copy(piece, zq_ref.at[chip], near)
    to_far = link.copy(piece, zq_ref.at[chip], far)
    land = link.used
    to_across = link.copy(piece, zq_ref.at[chip], across, land)
    relay = link.copy(zq_ref.at[chip ^ 2], zq_ref.at[chip ^ 2], near, land)
    to_far.start()
    to_near.start()

    @pl.when(mid)
    def _():
        to_across.start()

    fetch[2].wait()
    w1[...] = m_wide[...].astype(BF)
    width = zs_ref.shape[2]

    def strip(who):
        return w1.at[:, pl.ds(pl.multiple_of(who * width, 128), width)]

    zo_ref[core] = strip(fs)[...]
    to_pair = link.copy(strip(fs ^ 1), zo_ref.at[core], pair)
    to_pair.start()
    land = link.used
    down = [link.copy(strip(fs ^ k), zs_ref.at[core], peer, land + core) for k, peer in line if k > 1]
    got = [link.copy(zs_ref.at[j], zs_ref.at[j], pair, land + j) for j in range(2)]
    source = chip == dp

    @pl.when(source)
    def _():
        for copy in down:
            copy.start()

    for copy in ids_line:
        copy.wait()
    for copy in ids_plane:
        copy.start()
    to_far.wait_recv()

    @pl.when(mid)
    def _():
        relay.start()

    to_near.wait_recv()
    to_across.wait_recv()
    to_near.wait_send()
    to_far.wait_send()

    @pl.when(mid)
    def _():
        to_across.wait_send()
        relay.wait_send()

    for copy in ids_plane + [to_pair]:
        copy.wait()

    @pl.when(source)
    def _():
        zs_ref[...] = zo_ref[...]
        for copy in down:
            copy.wait_send()

    @pl.when(jnp.logical_not(source))
    def _():
        for copy in got:
            copy.wait_recv()


def first_exchange(x, a_in, a_out, m_in):
    high = a_in.shape[0]
    strips = jax.ShapeDtypeStruct((2, high, FF // 8), BF)
    return pl.pallas_call(
        first_kernel,
        out_shape=(
            jax.ShapeDtypeStruct((4, 8, 8, TOK), jnp.int32),
            jax.ShapeDtypeStruct((4, high // 2, 2 * D), BF),
            jax.ShapeDtypeStruct((high, 4 * D), BF),
            strips,
            strips,
        ),
        in_specs=vmem(1) + any_specs(3),
        out_specs=tuple(vmem(5)),
        scratch_shapes=[
            pltpu.VMEM((high, 3 * D), F32),
            pltpu.VMEM((high, D), F32),
            pltpu.VMEM((high, FF), F32),
            pltpu.VMEM((high, FF), BF),
            pltpu.SemaphoreType.DMA((3,)),
        ]
        + sems(26),
        compiler_params=params(1, 12),
    )(x, a_in, a_out, m_in)


class Spread:
    slots = 8

    def __init__(self, link, dp, fs, x_ref, o_ref):
        self.fs, self.x, self.o = fs, x_ref, o_ref
        self.mid = middle_chip(fs)
        near, far, across, pair = [(dp, fs ^ k) for k in (2, 4, 6, 1)]
        mine = o_ref.at[fs]
        self.near = link.copy(x_ref, mine, near)
        self.far = link.copy(x_ref, mine, far)
        land = link.used
        self.across = link.copy(x_ref, mine, across, land)
        self.relay = link.copy(o_ref.at[fs ^ 4], o_ref.at[fs ^ 4], near, land)
        self.pair = [
            link.copy(x_ref if k == 0 else o_ref.at[fs ^ k], o_ref.at[fs ^ k], pair)
            for k in (0, 2, 4, 6)
        ]

    def start(self):
        self.far.start()
        self.near.start()

        @pl.when(self.mid)
        def _():
            self.across.start()

        self.pair[0].start()
        self.o[self.fs] = self.x[...]

    def forward(self, after=None):
        self.far.wait_recv()

        @pl.when(self.mid)
        def _():
            self.relay.start()

        self.pair[2].start()
        if after:
            after(4)
        self.near.wait_recv()
        self.pair[1].start()
        if after:
            after(2)

    def late(self, after=None):
        self.across.wait_recv()
        self.pair[3].start()
        if after:
            after(6)

    def finish(self):
        for copy in self.pair:
            copy.wait_recv()
        self.sent()

    def sent(self):
        for copy in self.pair:
            copy.wait_send()
        self.near.wait_send()
        self.far.wait_send()

        @pl.when(self.mid)
        def _():
            self.across.wait_send()
            self.relay.wait_send()


class Fold:
    slots = 8

    def __init__(self, link, dp, fs, x_ref, part, sums, got):
        self.fs, self.x, self.part, self.sums, self.got = fs, x_ref, part, sums, got
        self.mid = middle_chip(fs)
        near, far, across, pair = [(dp, fs ^ k) for k in (2, 4, 6, 1)]
        self.pair = [link.copy(x_ref.at[fs ^ 1 ^ (2 * k)], part.at[k], pair) for k in range(4)]
        self.near = link.copy(sums.at[1], got.at[0], near)
        self.far = link.copy(sums.at[2], got.at[1], far)
        self.across = link.copy(sums.at[3], got.at[2], across)
        self.relay = link.copy(sums.at[3], got.at[3], near)

    def start(self):
        for k in (3, 2, 1, 0):
            self.pair[k].start()

    def add(self, k):
        self.pair[k].wait_recv()
        return self.x[self.fs ^ (2 * k)].astype(F32) + self.part[k].astype(F32)

    def first(self):
        self.sums[3] = self.add(3).astype(BF)

        @pl.when(self.mid)
        def _():
            self.across.start()

        @pl.when(jnp.logical_not(self.mid))
        def _():
            self.relay.start()
            self.sums[2] = self.add(2).astype(BF)
            self.far.start()

        self.sums[1] = self.add(1).astype(BF)
        self.near.start()

    def second(self):
        @pl.when(self.mid)
        def _():
            both = self.add(2)
            self.relay.wait_recv()
            self.sums[2] = (both + self.got[3].astype(F32)).astype(BF)
            self.far.start()

    def middle(self):
        self.first()
        self.second()

    def finish(self, o_ref):
        o_ref[...] = self.add(0)
        self.near.wait_recv()
        o_ref[...] += self.got[0].astype(F32)
        self.far.wait_recv()
        o_ref[...] += self.got[1].astype(F32)

        @pl.when(self.mid)
        def _():
            self.across.wait_recv()
            o_ref[...] += self.got[2].astype(F32)
            self.across.wait_send()

        @pl.when(jnp.logical_not(self.mid))
        def _():
            self.relay.wait_send()

        for copy in self.pair:
            copy.wait_send()
        self.near.wait_send()
        self.far.wait_send()


def fold_scratch():
    return [pltpu.VMEM((4, TOK, D), BF)] * 3


def line_peers(dp, fs):
    return [(dp, fs ^ k) for k in (1, 2, 4)], (middle_chip(fs), (dp, fs ^ 6))


def spread_kernel(x_ref, o_ref, send, recv):
    dp, fs = lax.axis_index("dp"), lax.axis_index("fsdp")
    greet(*line_peers(dp, fs))
    spread = Spread(Link(send, recv), dp, fs, x_ref, o_ref)
    spread.start()
    spread.forward()
    spread.late()
    spread.finish()


def gather_tokens(x):
    out = pl.pallas_call(
        spread_kernel,
        out_shape=jax.ShapeDtypeStruct((8, TOK, D), BF),
        in_specs=vmem(1),
        out_specs=vmem(1)[0],
        scratch_shapes=sems(Spread.slots),
        compiler_params=params(2, 16),
    )(x)
    return out.reshape(GROUP, D)


def fold_kernel(x_ref, o_ref, part, sums, got, send, recv):
    dp, fs = lax.axis_index("dp"), lax.axis_index("fsdp")
    greet(*line_peers(dp, fs))
    fold = Fold(Link(send, recv), dp, fs, x_ref, part, sums, got)
    fold.start()
    fold.middle()
    fold.finish(o_ref)


def sum_tokens(x):
    return pl.pallas_call(
        fold_kernel,
        out_shape=jax.ShapeDtypeStruct((TOK, D), F32),
        in_specs=vmem(1),
        out_specs=vmem(1)[0],
        scratch_shapes=fold_scratch() + sems(Fold.slots),
        compiler_params=params(3, 16),
    )(x.reshape(8, TOK, D))


def add_up(first, others):
    total = first.astype(F32)
    for other in others:
        total = total + other.astype(F32)
    return total


def table_terms(table, first_row, low, high, h_ref, lse_ref, w_ref, t_ref, o_ref):
    row = lax.broadcasted_iota(jnp.int32, (table.shape[0], GROUP), 0) + first_row
    logits = dense_nt(table, h_ref[low])
    for d in range(low, high):
        grad = jnp.exp(logits - lse_ref[d]) * w_ref[d]
        grad = (grad - jnp.where(row == t_ref[d], w_ref[d], 0.0)).astype(BF)
        if d + 1 < high:
            logits = dense_nt(table, h_ref[d + 1])
        o_ref[...] += dense(grad, h_ref[d])


class Fill:
    def __init__(self, first_row, refs, o_ref, e_ref, held, acc, sem):
        self.first_row, self.o, self.e, self.held, self.acc, self.sem = first_row, o_ref, e_ref, held, acc, sem
        self.table, self.hidden, *self.lines = refs

    def loads(self, d):
        return pltpu.make_async_copy(self.hidden.at[d], self.held.at[d], self.sem.at[d])

    def start(self, tokens=True):
        rows = pl.ds(self.first_row, self.e.shape[0])
        self.load = pltpu.make_async_copy(self.table.at[rows], self.e, self.sem.at[4])
        self.load.start()
        if tokens:
            for d in range(4):
                self.loads(d).start()
        self.acc[...] = jnp.zeros_like(self.acc)

    def groups(self, low, high, tokens=True):
        if low == 0:
            self.load.wait()
        if tokens:
            for d in range(low, high):
                self.loads(d).wait()
        table_terms(
            self.e[...], self.first_row, low, high, self.held, *self.lines, self.acc
        )
        if high == 4:
            self.store = pltpu.make_async_copy(self.acc, self.o, self.sem.at[5])
            self.store.start()

    def finish(self):
        self.store.wait()


def fill_scratch():
    return [
        pltpu.VMEM((FILL, D), BF),
        pltpu.VMEM((4, GROUP, D), BF),
        pltpu.VMEM((FILL, D), F32),
        pltpu.SemaphoreType.DMA((6,)),
    ]


def fill_call(kernel, ins, in_specs, fill, outs, out_specs, scratch, n_sems, cid):
    return pl.pallas_call(
        kernel,
        out_shape=tuple(outs) + (jax.ShapeDtypeStruct((FILL, D), F32),),
        in_specs=in_specs + any_specs(2) + vmem(3),
        out_specs=tuple(out_specs) + tuple(hbm_specs(1)),
        scratch_shapes=list(scratch) + fill_scratch() + sems(n_sems),
        compiler_params=params(cid, 58),
    )(*ins, *fill)


def fold_fill_kernel(first_row, x_ref, *refs):
    fill_refs, refs = refs[:5], refs[5:]
    o_ref, g_ref, part, sums, got, *fill_held, send, recv = refs
    dp, fs = lax.axis_index("dp"), lax.axis_index("fsdp")
    greet(*line_peers(dp, fs))
    fold = Fold(Link(send, recv), dp, fs, x_ref, part, sums, got)
    fill = Fill(first_row, fill_refs, g_ref, *fill_held)
    fold.start()
    fill.start()
    fold.first()
    fill.groups(0, 1)
    fold.second()
    fill.groups(1, 4)
    fold.finish(o_ref)
    fill.finish()


def sum_tokens_fill(x, fill, first_row, cid):
    return fill_call(
        functools.partial(fold_fill_kernel, first_row),
        (x.reshape(8, TOK, D),),
        vmem(1),
        fill,
        [jax.ShapeDtypeStruct((TOK, D), F32)],
        vmem(1),
        fold_scratch(),
        Fold.slots,
        cid,
    )


GELU_A = (2.0 / jnp.pi) ** 0.5
GELU_B = 0.044715


def gelu_parts(values):
    square = values * values
    bend = jnp.tanh(GELU_A * values * (1.0 + GELU_B * square))
    half = 0.5 * (1.0 + bend)
    slope = half + 0.5 * values * (1.0 - bend * bend) * GELU_A * (1.0 + 3.0 * GELU_B * square)
    return values * half, slope


def two(ref, chip):
    value = ref[pl.ds(2 * chip, 2)]
    return value.reshape(2 * value.shape[1], value.shape[2])


def mlp_kernel(x_ref, w_one, w_two, bias, o_ref, h_ref, u_ref, act_ref, prod, part, sums, got, send, recv):
    dp, fs = lax.axis_index("dp"), lax.axis_index("fsdp")
    chip = fs // 2
    greet(*line_peers(dp, fs))
    link = Link(send, recv)
    spread = Spread(link, dp, fs, x_ref, h_ref)
    fold = Fold(link, dp, fs, prod, part, sums, got)

    def run(k):
        spread.pair[k].wait_recv()
        there = chip ^ k
        pre = dense(two(h_ref, there), w_one[...]) + bias[...]
        act = gelu_parts(pre)[0].astype(BF)
        spot = pl.ds(2 * there, 2)
        u_ref[spot] = pre.reshape(2, TOK, pre.shape[1])
        act_ref[spot] = act.reshape(2, TOK, act.shape[1])
        prod[spot] = dense(act, w_two[...]).astype(BF).reshape(2, TOK, D)

    spread.start()
    run(0)
    spread.forward()
    run(2)
    run(1)
    spread.late()
    run(3)
    fold.start()
    fold.first()
    fold.second()
    fold.finish(o_ref)
    spread.sent()


def mlp_forward(x, w_one, w_two, bias):
    width = w_one.shape[1]
    return pl.pallas_call(
        mlp_kernel,
        out_shape=(
            jax.ShapeDtypeStruct((TOK, D), F32),
            jax.ShapeDtypeStruct((8, TOK, D), BF),
            jax.ShapeDtypeStruct((8, TOK, width), F32),
            jax.ShapeDtypeStruct((8, TOK, width), BF),
        ),
        in_specs=vmem(4),
        out_specs=tuple(vmem(4)),
        scratch_shapes=[pltpu.VMEM((8, TOK, D), BF)]
        + fold_scratch()
        + sems(Fold.slots + Spread.slots),
        compiler_params=params(11, 24),
    )(x, w_one, w_two, bias.reshape(1, width))


def mlp_back_kernel(rows_a, rows_b, x_ref, w_one, w_two, u_ref, act_ref, h_ref, *refs):
    fill_refs, refs = refs[:5], refs[5:]
    o_ref, f_down, g_up, d_bias, g_a, g_b, got_ref, prod, part, sums, got, s_down, r_down, *refs = refs
    e_a, held, acc_a, sem_a, e_b, acc_b, sem_b, send, recv = refs
    dp, fs = lax.axis_index("dp"), lax.axis_index("fsdp")
    plane = [(k, (dp ^ k, fs)) for k in range(1, 4)]
    peers, extra = line_peers(dp, fs)
    greet(peers + [peer for k, peer in plane], extra)
    link = Link(send, recv)
    spread = Spread(link, dp, fs, x_ref, got_ref)
    fold = Fold(link, dp, fs, prod, part, sums, got)
    first = Fill(rows_a, fill_refs, g_a, e_a, held, acc_a, sem_a)
    second = Fill(rows_b, fill_refs, g_b, e_b, held, acc_b, sem_b)
    high = f_down.shape[0]

    def lines(who):
        return pl.ds(pl.multiple_of(who * high, 16), high)

    side = [link.copy(s_down.at[lines(dp ^ k)], r_down.at[k - 1], peer) for k, peer in plane]
    spread.start()
    first.start()
    second.start(False)
    first.groups(0, 1)
    spread.forward()
    first.groups(1, 3)
    spread.late()
    first.groups(3, 4)
    spread.finish()
    width = w_one.shape[1]
    cotangent = got_ref[...].reshape(GROUP, D)
    d_act = dense_nt(cotangent, w_two[...])
    d_pre = d_act * gelu_parts(u_ref[...].reshape(GROUP, width))[1]
    d_low = d_pre.astype(BF)
    prod[...] = dense_nt(d_low, w_one[...]).astype(BF).reshape(8, TOK, D)
    fold.start()
    d_bias[...] = jnp.sum(d_pre, axis=0, keepdims=True)
    s_down[...] = dense_tn(act_ref[...].reshape(GROUP, width), cotangent).astype(BF)
    fold.first()
    for copy in side:
        copy.start()
    g_up[...] = dense_tn(h_ref[...].reshape(GROUP, D), d_low).astype(BF)
    fold.second()
    second.groups(0, 4, False)
    for copy in side:
        copy.wait()
    f_down[...] = add_up(s_down[lines(dp), :], [r_down[j] for j in range(3)]).astype(BF)
    fold.finish(o_ref)
    first.finish()
    second.finish()


def mlp_backward(x, w_one, w_two, pre_act, act_low, normed, fill, rows_a, rows_b, cid):
    width = w_one.shape[1]
    high = w_two.shape[0] // 4
    block = jax.ShapeDtypeStruct((FILL, D), F32)
    extra = fill_scratch()
    return pl.pallas_call(
        functools.partial(mlp_back_kernel, rows_a, rows_b),
        out_shape=(
            jax.ShapeDtypeStruct((TOK, D), F32),
            jax.ShapeDtypeStruct((high, D), BF),
            jax.ShapeDtypeStruct((D, width), BF),
            jax.ShapeDtypeStruct((1, width), F32),
            block,
            block,
        ),
        in_specs=vmem(6) + any_specs(2) + vmem(3),
        out_specs=tuple(vmem(4) + hbm_specs(2)),
        scratch_shapes=[pltpu.VMEM((8, TOK, D), BF)] * 2
        + fold_scratch()
        + [pltpu.VMEM(w_two.shape, BF), pltpu.VMEM((3, high, D), BF)]
        + extra
        + [extra[0], extra[2], extra[3]]
        + sems(Spread.slots + Fold.slots + 3),
        compiler_params=params(cid, 58),
    )(x, w_one, w_two, pre_act, act_low, normed, *fill)


def spread_last_kernel(first_row, x_ref, g_qkv, g_out, g_down, *refs):
    fill_refs, refs = refs[:5], refs[5:]
    o_ref, side_any, q_any, u_any, o_down, g_ref, s_qkv, s_out, p_qkv, p_out, keep, *fill_held, send, recv = refs
    dp, fs = lax.axis_index("dp"), lax.axis_index("fsdp")
    core, chip, pair = fs % 2, fs // 2, (dp, fs ^ 1)
    peers, extra = line_peers(dp, fs)
    greet(peers + [(dp ^ k, fs) for k in (1, 2, 3)], extra)
    link = Link(send, recv)
    spread = Spread(link, dp, fs, x_ref, o_ref)
    fill = Fill(first_row, fill_refs, g_ref, *fill_held)
    both = ((g_qkv, s_qkv, p_qkv), (g_out, s_out, p_out))
    swap = [link.copy(g.at[:, 1 - core], p, pair) for g, s, p in both]
    mine = [pltpu.make_async_copy(g.at[:, core], s, keep.at[i]) for i, (g, s, p) in enumerate(both)]
    sides = {
        k: [
            link.copy(
                x_ref if k == 0 else o_ref.at[fs ^ k],
                side_any.at[j - 1, chip ^ (k // 2)],
                (dp ^ j, fs),
            )
            for j in (1, 2)
        ]
        for k in (0, 2, 4, 6)
    }

    high = g_down.shape[0]
    home = o_down.at[pl.ds(pl.multiple_of(dp * high, 16), high)]
    back = [link.copy(g_down, home, (dp ^ k, fs)) for k in (1, 2, 3)]
    back.append(pltpu.make_async_copy(g_down, home, keep.at[2]))

    def after(k):
        for copy in sides[k]:
            copy.start()

    spread.start()
    after(0)
    for copy in back + swap + mine:
        copy.start()
    fill.start()
    fill.groups(0, 1)
    spread.forward(after)
    fill.groups(1, 3)
    spread.late(after)
    for copy in swap + mine:
        copy.wait()
    for g, s, p in both:
        for j in range(4):
            s[j] = add_up(s[j], [p[j]]).astype(BF)
    out = [
        pltpu.make_async_copy(s_qkv, q_any, keep.at[3]),
        pltpu.make_async_copy(s_out, u_any, keep.at[4]),
    ]
    for copy in out:
        copy.start()
    fill.groups(3, 4)
    for copy in out:
        copy.wait()
    for copy in back:
        copy.wait()
    spread.finish()
    for k in (0, 2, 4, 6):
        for copy in sides[k]:
            copy.wait()
    fill.finish()


def gather_tokens_last(x, g_qkv, g_out, g_down, fill, first_row, cid):
    high = D // 8
    halves = [(4, high, 3 * D), (4, high, D)]
    return fill_call(
        functools.partial(spread_last_kernel, first_row),
        (x, g_qkv.reshape(4, 2, high, 3 * D), g_out.reshape(4, 2, high, D), g_down),
        vmem(1) + any_specs(2) + vmem(1),
        fill,
        [jax.ShapeDtypeStruct((8, TOK, D), BF), jax.ShapeDtypeStruct((2, 4, TOK, D), BF)]
        + [jax.ShapeDtypeStruct(h, BF) for h in halves]
        + [jax.ShapeDtypeStruct((FF // 8, D), BF)],
        vmem(1) + hbm_specs(4),
        [pltpu.VMEM(h, BF) for h in halves] * 2 + [pltpu.SemaphoreType.DMA((5,))],
        Spread.slots + 2 + 8 + 3,
        cid,
    )


def start_kernel(
    look, wqo, zq, zs, zo, small, pos, e_out, wqo_out, w1_out, small_out, pos_out, part, sums, got, send, recv
):
    dp, fs = lax.axis_index("dp"), lax.axis_index("fsdp")
    chip, core, pair = fs // 2, fs % 2, (dp, fs ^ 1)
    line = [(dp, fs ^ k) for k in range(1, 8)]
    plane = [(dp ^ k, fs) for k in range(1, 4)]
    greet(line + plane)
    link = Link(send, recv)
    fold = Fold(link, dp, fs, look, part, sums, got)
    fold.start()
    spot = quarter_of(dp, wqo_out.shape)
    side = {
        k: [
            link.copy(zq.at[chip ^ (k // 2)], wqo_out.at[(fs ^ k,) + spot], peer)
            for peer in plane
        ]
        for k in (2, 4, 6)
    }
    for k in (2, 4, 6):
        for copy in side[k]:
            copy.start()
    wqo_out[fs] = wqo[...]
    pairs = [link.copy(wqo, wqo_out.at[fs], pair)]
    pairs[0].start()
    strips = [
        link.copy(zs, w1_out.at[pl.ds(2 * dp, 2)], (dp ^ k, fs)) for k in range(1, 4)
    ]
    source = chip == dp

    @pl.when(jnp.logical_not(source))
    def _():
        for copy in strips:
            copy.start()

    w1_out[pl.ds(2 * dp, 2)] = zs[...]
    w1_out[pl.ds(2 * chip, 2)] = zo[...]
    fold.first()
    high = pos.shape[0] // 4
    rows = pl.ds(pl.multiple_of(dp * high, 16), high)
    land = link.used
    pos_line = [
        link.copy(pos_out.at[rows], pos_out.at[rows], (dp, k), land) for k in (2, 4, 6)
    ]
    pos_side = [link.copy(pos_out.at[rows], pos_out.at[rows], peer) for peer in plane]
    pos_pair = link.copy(pos_out, pos_out, pair)

    @pl.when(fs == 0)
    def _():
        pos_out[rows] = pos[rows]
        for copy in pos_line:
            copy.start()

    tiny = Spread(link, dp, fs, small, small_out)
    tiny.start()
    for k in (2, 4, 6):
        wqo_out[(fs ^ k,) + spot] = zq[chip ^ (k // 2)]

    fold.second()

    @pl.when(core == 0)
    def _():
        @pl.when(fs != 0)
        def _():
            pos_line[0].wait_recv()

        for copy in pos_side:
            copy.start()

    tiny.forward()
    fold.finish(e_out)

    @pl.when(core == 0)
    def _():
        for copy in pos_side:
            copy.wait()
        pos_pair.start()

    tiny.late()
    tiny.finish()
    for k in (2, 4, 6):
        for copy in side[k]:
            copy.wait_recv()
        copy = link.copy(wqo_out.at[fs ^ k], wqo_out.at[fs ^ k], pair)
        copy.start()
        pairs.append(copy)
    for copy in pairs:
        copy.wait()
    for k in (2, 4, 6):
        for copy in side[k]:
            copy.wait_send()

    @pl.when(jnp.logical_not(source))
    def _():
        for copy in strips:
            copy.wait_send()

    for k, copy in zip(range(1, 4), strips):

        @pl.when(chip != (dp ^ k))
        def _():
            copy.wait_recv()

    @pl.when(core == 0)
    def _():
        pos_pair.wait_send()

    @pl.when(core == 1)
    def _():
        pos_pair.wait_recv()

    @pl.when(fs == 0)
    def _():
        for copy in pos_line:
            copy.wait_send()


def start_exchange(looked, wqo, zq, zs, zo, small, pos):
    n_sems = Fold.slots + 9 + 4 + 3 + 7 + Spread.slots
    return pl.pallas_call(
        start_kernel,
        out_shape=(
            jax.ShapeDtypeStruct((TOK, D), F32),
            jax.ShapeDtypeStruct((8,) + wqo.shape, BF),
            jax.ShapeDtypeStruct((8,) + zs.shape[1:], BF),
            jax.ShapeDtypeStruct((8,) + small.shape, BF),
            jax.ShapeDtypeStruct(pos.shape, BF),
        ),
        in_specs=vmem(7),
        out_specs=tuple(vmem(5)),
        scratch_shapes=fold_scratch() + sems(n_sems),
        compiler_params=params(4, 20),
    )(looked.reshape(8, TOK, D), wqo, zq, zs, zo, small, pos)


def lse_kernel(st_ref, lse_ref, hit_ref, mine, got, both, send, recv):
    dp, fs = lax.axis_index("dp"), lax.axis_index("fsdp")
    line = [(dp, fs ^ k) for k in range(1, 8)]
    plane = [(dp ^ k, fs) for k in range(1, 4)]
    greet(line + plane)
    link = Link(send, recv)
    blocks = st_ref.shape[0]
    top = st_ref[0, 0:1, :]
    for b in range(1, blocks):
        top = jnp.maximum(top, st_ref[b, 0:1, :])
    total = jnp.zeros_like(top)
    hit = jnp.zeros_like(top)
    for b in range(blocks):
        total = total + st_ref[b, 1:2, :] * jnp.exp(st_ref[b, 0:1, :] - top)
        hit = hit + st_ref[b, 2:3, :]
    for j in range(8):
        lanes = slice(j * TOK, (j + 1) * TOK)
        mine[j : j + 1, :] = top[:, lanes]
        mine[8 + j : 9 + j, :] = total[:, lanes]
        mine[16 + j : 17 + j, :] = hit[:, lanes]
    first = [link.copy(mine, got.at[fs], peer) for peer in line]
    for copy in first:
        copy.start()
    got[fs] = mine[...]
    for copy in first:
        copy.wait()
    top = got[0, 0:8, :]
    for j in range(1, 8):
        top = jnp.maximum(top, got[j, 0:8, :])
    total = jnp.zeros_like(top)
    hit = jnp.zeros_like(top)
    for j in range(8):
        total = total + got[j, 8:16, :] * jnp.exp(got[j, 0:8, :] - top)
        hit = hit + got[j, 16:24, :]
    both[dp, 0:8, :] = top + jnp.log(total)
    both[dp, 8:16, :] = hit
    second = [link.copy(both.at[dp], both.at[dp], peer) for peer in plane]
    for copy in second:
        copy.start()
    for copy in second:
        copy.wait()
    for d in range(4):
        for j in range(8):
            lanes = slice(j * TOK, (j + 1) * TOK)
            lse_ref[d, :, lanes] = both[d, j : j + 1, :]
            hit_ref[d, :, lanes] = both[d, 8 + j : 9 + j, :]


def combine_stats(stats):
    return pl.pallas_call(
        lse_kernel,
        out_shape=(jax.ShapeDtypeStruct((4, 1, GROUP), F32),) * 2,
        in_specs=vmem(1),
        out_specs=tuple(vmem(2)),
        scratch_shapes=[
            pltpu.VMEM((24, TOK), F32),
            pltpu.VMEM((8, 24, TOK), F32),
            pltpu.VMEM((4, 16, TOK), F32),
        ]
        + sems(10),
        compiler_params=params(5, 8),
    )(stats)


def logits_kernel(
    rows_here,
    x_ref,
    e_ref,
    t_ref,
    p_ref,
    st_ref,
    table_any,
    h_any,
    o_any,
    held,
    tab,
    keep,
    send,
    recv,
):
    turn, block = pl.program_id(0), pl.program_id(1)
    last = pl.num_programs(1) - 1
    dp, fs = lax.axis_index("dp"), lax.axis_index("fsdp")
    chip, core, pair = fs // 2, fs % 2, (dp, fs ^ 1)
    link = Link(send, recv)
    spread = Spread(link, dp, fs, x_ref, held)
    sides = {
        k: [
            link.copy(
                x_ref if k == 0 else held.at[fs ^ k],
                o_any.at[side - 1, chip ^ (k // 2), core],
                (dp ^ side, fs),
            )
            for side in (1, 2)
        ]
        for k in (0, 2, 4, 6)
    }
    pairs = [link.copy(o_any.at[k, :, core], o_any.at[k, :, core], pair) for k in range(2)]
    keep_table = pltpu.make_async_copy(tab, table_any, keep.at[0])
    keep_held = pltpu.make_async_copy(held, h_any, keep.at[1])

    def after(k):
        for copy in sides[k]:
            copy.start()

    def at(i, b):
        return pl.when((turn == i) & (block == b))

    @at(0, 0)
    def _():
        peers, extra = line_peers(dp, fs)
        greet(peers + [(dp ^ 1, fs), (dp ^ 2, fs)], extra)
        spread.start()
        after(0)
        spread.pair[0].wait_recv()

    @at(0, last)
    def _():
        spread.forward(after)

    @at(1, 0)
    def _():
        spread.pair[1].wait_recv()
        keep_table.start()

    @at(1, last - 1)
    def _():
        spread.late(after)

    @at(2, 0)
    def _():
        spread.pair[2].wait_recv()

    @at(3, 0)
    def _():
        spread.pair[3].wait_recv()
        keep_held.start()

    rows = pl.ds(pl.multiple_of(block * VBLK, 16), VBLK)

    @pl.when(turn == 0)
    def _():
        line = lax.broadcasted_iota(jnp.int32, (VBLK, 1), 0) + block * VBLK
        tab[rows, :] = jnp.where(line < rows_here, e_ref[...], 0.0).astype(BF)

    there = chip ^ turn
    lanes = pl.ds(pl.multiple_of(there * 2 * TOK, 2 * TOK), 2 * TOK)
    tokens = two(held, there)
    wanted = t_ref[dp, :, lanes]
    high = VBLK // 2
    starts = [block * VBLK + half * high for half in range(2)]
    both = [
        dense_nt(tab[pl.ds(pl.multiple_of(start, 16), high), :], tokens) for start in starts
    ]
    for half, (start, logits) in enumerate(zip(starts, both)):
        row = lax.broadcasted_iota(jnp.int32, logits.shape, 0) + start
        logits = jnp.where(row < rows_here, logits, -jnp.inf)
        top = jnp.max(logits, 0, keepdims=True)
        hit = jnp.where(row == wanted, logits, 0.0)
        grown = jnp.exp(logits - top)
        st_ref[2 * block + half, 0:1, lanes] = top
        st_ref[2 * block + half, 1:2, lanes] = jnp.sum(grown, 0, keepdims=True)
        st_ref[2 * block + half, 2:3, lanes] = jnp.sum(hit, 0, keepdims=True)
        p_ref[0, half * high : (half + 1) * high, :] = grown.astype(BF)

    @at(3, last)
    def _():
        for side, copy in enumerate(pairs):
            for k in (0, 2, 4, 6):
                sides[k][side].wait_recv()
            copy.start()
        for copy in pairs + [keep_table, keep_held]:
            copy.wait()
        for k in (0, 2, 4, 6):
            for copy in sides[k]:
                copy.wait_send()
        spread.sent()


def own_logits(embed, hidden, target):
    rows_here = embed.shape[0]
    blocks = pl.cdiv(rows_here, VBLK)
    return pl.pallas_call(
        functools.partial(logits_kernel, rows_here),
        grid=(4, blocks),
        in_specs=[
            pl.BlockSpec((TOK, D), lambda i, j: (0, 0)),
            pl.BlockSpec((VBLK, D), lambda i, j: (jnp.where(i == 0, j, blocks - 1), 0)),
            pl.BlockSpec((4, 1, GROUP), lambda i, j: (0, 0, 0)),
        ],
        out_specs=[
            pl.BlockSpec((1, VBLK, 2 * TOK), lambda i, j: (i, j, 0)),
            pl.BlockSpec((2 * blocks, 8, GROUP), lambda i, j: (0, 0, 0)),
        ]
        + hbm_specs(3),
        out_shape=[
            jax.ShapeDtypeStruct((4, blocks * VBLK, 2 * TOK), BF),
            jax.ShapeDtypeStruct((2 * blocks, 8, GROUP), F32),
            jax.ShapeDtypeStruct((blocks * VBLK, D), BF),
            jax.ShapeDtypeStruct((8, TOK, D), BF),
            jax.ShapeDtypeStruct((2, 4, 2, TOK, D), BF),
        ],
        scratch_shapes=[
            pltpu.VMEM((8, TOK, D), BF),
            pltpu.VMEM((blocks * VBLK, D), BF),
            pltpu.SemaphoreType.DMA((2,)),
        ]
        + sems(Spread.slots + 8 + 2),
        compiler_params=params(7, 58),
    )(hidden, embed, target)


def dhf_kernel(
    p_ref, st_ref, lse_ref, w_ref, t_ref, e_ref, own_any, near_any, o_ref, o_any, acc, held, keep, send, recv
):
    block = pl.program_id(0)
    last = pl.num_programs(0) - 1
    dp, fs = lax.axis_index("dp"), lax.axis_index("fsdp")
    core, pair = fs % 2, (dp, fs ^ 1)
    link = Link(send, recv)
    halves = [
        link.copy(
            near_any.at[2 - k, pl.ds((2 - k) * 2, 2), core],
            held.at[dp ^ (3 - k), pl.ds((2 - k) * 2, 2), core],
            (dp ^ k, fs),
        )
        for k in (1, 2)
    ]
    share = link.copy(held.at[dp ^ 3, :, core], held.at[dp ^ 3, :, core], pair)
    mine = [
        pltpu.make_async_copy(own_any, held.at[dp], keep.at[0]),
        pltpu.make_async_copy(near_any.at[0], held.at[dp ^ 1], keep.at[1]),
        pltpu.make_async_copy(near_any.at[1], held.at[dp ^ 2], keep.at[2]),
    ]
    home = [
        pltpu.make_async_copy(held.at[dp ^ k], o_any.at[dp ^ k], keep.at[3 + k]) for k in range(4)
    ]

    @pl.when(block == 0)
    def _():
        greet([(dp ^ 1, fs), (dp ^ 2, fs), pair])
        for copy in halves + mine:
            copy.start()

    spans = [
        pl.ds(pl.multiple_of((fs // 2 ^ k) * 2 * TOK, 2 * TOK), 2 * TOK) for k in range(4)
    ]

    def lined(pick):
        return jnp.concatenate([pick(span) for span in spans], axis=1)

    weight = lined(lambda span: w_ref[dp, :, span])
    wanted = lined(lambda span: t_ref[dp, :, span])
    lse = lined(lambda span: lse_ref[dp, :, span])
    grown = jnp.concatenate([p_ref[k] for k in range(4)], axis=1).astype(F32)
    row = lax.broadcasted_iota(jnp.int32, grown.shape, 0) + block * VBLK
    high = VBLK // 2
    scaled = []
    for half in range(2):
        factor = weight * jnp.exp(lined(lambda span: st_ref[half, 0:1, span]) - lse)
        scaled.append(grown[half * high : (half + 1) * high, :] * factor)
    grad = jnp.concatenate(scaled, axis=0) - jnp.where(row == wanted, weight, 0.0)
    grad = grad.astype(BF)

    @pl.when(block == 1)
    def _():
        for copy in mine:
            copy.wait()
        for copy in home[:3]:
            copy.start()

    @pl.when(block == 0)
    def _():
        acc[...] = dense_tn(grad, e_ref[...])

    @pl.when(block > 0)
    def _():
        acc[...] += dense_tn(grad, e_ref[...])

    @pl.when(block == last)
    def _():
        for copy in halves:
            copy.wait_recv()
        share.start()
        for k, span in enumerate(spans):
            o_ref[span, :] = acc[k * 2 * TOK : (k + 1) * 2 * TOK, :].astype(BF)
        share.wait()
        home[3].start()
        for copy in halves:
            copy.wait_send()
        for copy in home:
            copy.wait()


def final_cotangent(grown, stats, lse, weight, target, table, own, near):
    blocks = table.shape[0] // VBLK
    line = pl.BlockSpec((4, 1, GROUP), lambda i: (0, 0, 0))
    return pl.pallas_call(
        dhf_kernel,
        grid=(blocks,),
        in_specs=[
            pl.BlockSpec((4, VBLK, 2 * TOK), lambda i: (0, i, 0)),
            pl.BlockSpec((2, 8, GROUP), lambda i: (i, 0, 0)),
            line,
            line,
            line,
            pl.BlockSpec((VBLK, D), lambda i: (i, 0)),
        ]
        + any_specs(2),
        out_specs=[pl.BlockSpec((GROUP, D), lambda i: (0, 0))] + hbm_specs(1),
        out_shape=[
            jax.ShapeDtypeStruct((GROUP, D), BF),
            jax.ShapeDtypeStruct((4, 4, 2, TOK, D), BF),
        ],
        scratch_shapes=[
            pltpu.VMEM((GROUP, D), F32),
            pltpu.VMEM((4, 4, 2, TOK, D), BF),
            pltpu.SemaphoreType.DMA((7,)),
        ]
        + sems(3),
        compiler_params=params(8, 58),
    )(grown, stats, lse, weight, target, table, own.reshape(4, 2, TOK, D), near)


def table_kernel(
    e_ref,
    h_ref,
    lse_ref,
    w_ref,
    t_ref,
    d_own,
    d_near,
    g_qkv,
    g_out,
    g_up,
    g_maps,
    *refs,
):
    vectors, refs = refs[:10], refs[10:]
    (
        o_ref,
        d_all,
        o_qkv,
        o_out,
        o_up,
        o_maps,
        o_vec,
        s_qkv,
        s_out,
        t_qkv,
        t_out,
        r_qkv,
        r_out,
        q_qkv,
        q_out,
        s_up,
        r_up,
        z_qkv,
        z_out,
        f_qkv,
        f_out,
        f_up,
        b_maps,
        r_maps,
        f_maps,
        b_vec,
        r_vec,
        f_vec,
        d_held,
        g_vec,
        local,
        send,
        recv,
    ) = refs
    block, half = pl.program_id(0), pl.program_id(1)
    step = block * 2 + half
    last = pl.num_programs(0) * 2 - 1
    dp, fs = lax.axis_index("dp"), lax.axis_index("fsdp")
    core, chip, pair = fs % 2, fs // 2, (dp, fs ^ 1)
    line = [(k, (dp, fs ^ k)) for k in range(1, 8)]
    plane = [(k, (dp ^ k, fs)) for k in range(1, 4)]
    chips = [(k, (dp, fs ^ (2 * k))) for k in range(1, 4)]
    link = Link(send, recv)
    spots = iter(range(64))

    def here(src, dst):
        return pltpu.make_async_copy(src, dst, local.at[next(spots)])

    def quarter(who, shape):
        high, wide = shape[-2] // 2, shape[-1] // 2
        return (
            pl.ds(pl.multiple_of((who // 2) * high, 16), high),
            pl.ds(pl.multiple_of((who % 2) * wide, 128), wide),
        )

    def strip(who):
        width = g_up.shape[2]
        return pl.ds(pl.multiple_of(who * width, 128), width)

    keep_d = [
        here(d_own, d_held.at[dp]),
        here(d_near.at[0], d_held.at[dp ^ 1, :, core]),
        here(d_near.at[1], d_held.at[dp ^ 2, :, core]),
    ]
    d_home = [here(d_held.at[dp ^ k], d_all.at[dp ^ k]) for k in range(4)]
    d_half = [
        link.copy(
            d_near.at[2 - k, pl.ds((2 - k) * 2, 2)],
            d_held.at[dp ^ (3 - k), pl.ds((2 - k) * 2, 2), core],
            (dp ^ k, fs),
        )
        for k in (1, 2)
    ]
    d_pair = [
        link.copy(d_near.at[0], d_held.at[dp ^ 1, :, core], pair),
        link.copy(d_near.at[1], d_held.at[dp ^ 2, :, core], pair),
    ]
    d_last = link.copy(d_held.at[dp ^ 3, :, core], d_held.at[dp ^ 3, :, core], pair)
    big = (
        (g_qkv, s_qkv, t_qkv, r_qkv, q_qkv, z_qkv, f_qkv, o_qkv),
        (g_out, s_out, t_out, r_out, q_out, z_out, f_out, o_out),
    )

    def slab(g, who, part):
        return g.at[(pl.ds(2 * part, 2),) + quarter(who, g.shape)]

    keep_big = []
    big_first = []
    big_second = []
    for g, s, t, r, q, *_ in big:
        for part in range(2):
            turn, other = (1, 2) if part == 0 else (2, 1)
            keep_big.append(here(slab(g, dp, part), s.at[pl.ds(2 * part, 2)]))
            keep_big.append(here(slab(g, dp ^ other, part), t.at[part]))
            big_first.append(link.copy(slab(g, dp ^ 3, part), r.at[part, 1], (dp ^ turn, fs)))
            big_first.append(link.copy(slab(g, dp ^ turn, part), r.at[part, 0], (dp ^ turn, fs)))
            big_second.append(link.copy(t.at[part], q.at[part], (dp ^ other, fs)))
    big_line = [
        link.copy(s.at[chip ^ k], z.at[k - 1], peer)
        for g, s, t, r, q, z, *_ in big
        for k, peer in chips
    ]
    big_back = [
        link.copy(f, o.at[quarter(dp, o.shape)], peer)
        for g, s, t, r, q, z, f, o in big
        for k, peer in plane
    ]
    big_home = [here(f, o.at[quarter(dp, o.shape)]) for g, s, t, r, q, z, f, o in big]
    keep_up = here(g_up.at[fs], s_up.at[:, strip(fs)])
    up_line = [link.copy(g_up.at[fs ^ k], s_up.at[:, strip(fs)], peer) for k, peer in line]
    up_side = [
        link.copy(s_up.at[quarter(dp ^ k, s_up.shape)], r_up.at[k - 1], peer) for k, peer in plane
    ]
    up_back = [link.copy(f_up, o_up.at[quarter(dp, s_up.shape)], peer) for k, peer in plane]
    up_home = here(f_up, o_up.at[quarter(dp, s_up.shape)])
    keep_maps = here(g_maps.at[fs], b_maps.at[fs])
    maps_line = [link.copy(g_maps.at[fs ^ k], b_maps.at[fs], peer) for k, peer in line]
    maps_side = [link.copy(r_maps.at[dp], r_maps.at[dp], peer) for k, peer in plane]
    maps_back = [link.copy(f_maps, o_maps.at[fs], peer) for k, peer in line]
    maps_home = here(f_maps, o_maps.at[fs])
    keep_vec = here(g_vec, b_vec.at[fs])
    vec_line = [link.copy(g_vec, b_vec.at[fs], peer) for k, peer in line]
    vec_side = [link.copy(r_vec.at[dp], r_vec.at[dp], peer) for k, peer in plane]
    vec_home = here(f_vec, o_vec)

    @pl.when(step == 0)
    def _():
        greet([peer for k, peer in line + plane])
        for copy in big_first + up_line + maps_line + d_pair:
            copy.start()
        g_vec[...] = jnp.zeros_like(g_vec)
        for i in range(6):
            g_vec[i : i + 1, :] = vectors[i][...]
        for i in range(3):
            g_vec[6 + i : 7 + i, :] = vectors[6][:, i * D : (i + 1) * D]
        g_vec[9:10, :] = vectors[7][...]
        width = vectors[8].shape[1]
        for i in range(8):

            @pl.when(fs == i)
            def _():
                first = i * width
                lanes = slice(first % D, first % D + width)
                g_vec[10 + first // D : 11 + first // D, lanes] = vectors[8][...]

        g_vec[14:15, :] = vectors[9][...]
        for copy in vec_line:
            copy.start()
        for copy in keep_d + keep_big + [keep_up, keep_maps, keep_vec]:
            copy.start()

    @pl.when(step == 3)
    def _():
        for copy in keep_big + big_first:
            copy.wait()
        for g, s, t, r, *_ in big:
            for part in range(2):
                t[part] = add_up(t[part], [r[part, 1]]).astype(BF)
        for copy in big_second:
            copy.start()

    @pl.when(step == 4)
    def _():
        for copy in big_second:
            copy.wait()
        for g, s, t, r, q, *_ in big:
            for part in range(2):
                for j in range(2):
                    s[2 * part + j] = add_up(
                        s[2 * part + j], [r[part, 0, j], q[part, j]]
                    ).astype(BF)
        for copy in big_line + d_half:
            copy.start()
        for copy in d_pair + keep_d:
            copy.wait()
        for copy in d_home[:3]:
            copy.start()

    @pl.when(step == 5)
    def _():
        for copy in up_line + [keep_up]:
            copy.wait()
        for copy in up_side:
            copy.start()
        for copy in vec_line + maps_line + [keep_vec, keep_maps]:
            copy.wait()
        r_vec[dp] = add_up(b_vec[0], [b_vec[j] for j in range(1, 8)])
        r_maps[dp] = add_up(b_maps[0], [b_maps[j] for j in range(1, 8)])
        for copy in vec_side + maps_side:
            copy.start()

    @pl.when(step == 6)
    def _():
        for copy in d_half:
            copy.wait()
        d_last.start()

    @pl.when(step == 7)
    def _():
        for copy in up_side:
            copy.wait()
        f_up[...] = add_up(
            s_up[quarter(dp, s_up.shape)], [r_up[j] for j in range(3)]
        ).astype(BF)
        for copy in up_back + [up_home]:
            copy.start()
        for copy in maps_side + vec_side:
            copy.wait()
        f_maps[...] = add_up(r_maps[0], [r_maps[j] for j in range(1, 4)]).astype(BF)
        f_vec[...] = add_up(r_vec[0], [r_vec[j] for j in range(1, 4)])
        for copy in maps_back + [maps_home, vec_home]:
            copy.start()
        d_last.wait()
        d_home[3].start()

    @pl.when(step == 8)
    def _():
        for copy in big_line:
            copy.wait()
        for g, s, t, r, q, z, f, o in big:
            f[...] = add_up(s[chip], [z[i] for i in range(3)]).astype(BF)
        for copy in big_back + big_home:
            copy.start()

    @pl.when(half == 0)
    def _():
        o_ref[...] = jnp.zeros_like(o_ref)

    for part in range(2):

        @pl.when(half == part)
        def _():
            table_terms(
                e_ref[...],
                block * TBLK,
                part * 2,
                part * 2 + 2,
                h_ref,
                lse_ref,
                w_ref,
                t_ref,
                o_ref,
            )

    @pl.when(step == last)
    def _():
        for copy in d_home:
            copy.wait()
        for copy in big_back + big_home + up_back + maps_back:
            copy.wait()
        for copy in [up_home, maps_home, vec_home]:
            copy.wait()


def table_gradient(rows, table, tokens, d_own, d_near, g_qkv, g_out, g_up, g_maps, vectors):
    line = pl.BlockSpec((4, 1, GROUP), lambda i, j: (0, 0, 0))
    high = D // 8

    def like(*shape, dtype=BF):
        return pltpu.VMEM(shape, dtype)

    def quarters(width):
        return (high // 2, width // 2)

    return pl.pallas_call(
        table_kernel,
        grid=(rows // TBLK, 2),
        in_specs=[
            pl.BlockSpec((TBLK, D), lambda i, j: (i, 0)),
            pl.BlockSpec((4, GROUP, D), lambda i, j: (0, 0, 0)),
            line,
            line,
            line,
        ]
        + any_specs(6)
        + [pl.BlockSpec(v.shape, lambda i, j: (0, 0)) for v in vectors],
        out_specs=[pl.BlockSpec((TBLK, D), lambda i, j: (i, 0))] + hbm_specs(6),
        out_shape=[
            jax.ShapeDtypeStruct((rows, D), F32),
            jax.ShapeDtypeStruct((4, 4, 2, TOK, D), BF),
            jax.ShapeDtypeStruct((high, 3 * D), BF),
            jax.ShapeDtypeStruct((high, D), BF),
            jax.ShapeDtypeStruct((high, FF), BF),
            jax.ShapeDtypeStruct((8, 2 * HD // 8, D), BF),
            jax.ShapeDtypeStruct((16, D), F32),
        ],
        scratch_shapes=[
            like(4, *quarters(3 * D)),
            like(4, *quarters(D)),
            like(2, 2, *quarters(3 * D)),
            like(2, 2, *quarters(D)),
            like(2, 2, 2, *quarters(3 * D)),
            like(2, 2, 2, *quarters(D)),
            like(2, 2, *quarters(3 * D)),
            like(2, 2, *quarters(D)),
            like(high, FF),
            like(3, *quarters(FF)),
            like(3, *quarters(3 * D)),
            like(3, *quarters(D)),
            like(*quarters(3 * D)),
            like(*quarters(D)),
            like(*quarters(FF)),
            like(8, 16, D),
            like(4, 16, D, dtype=F32),
            like(16, D),
            like(8, 16, D, dtype=F32),
            like(4, 16, D, dtype=F32),
            like(16, D, dtype=F32),
            like(4, 4, 2, TOK, D),
            like(16, D, dtype=F32),
            pltpu.SemaphoreType.DMA((24,)),
        ]
        + sems(72),
        compiler_params=params(9, 58),
    )(
        table,
        *tokens,
        d_own.reshape(4, 2, TOK, D),
        d_near,
        g_qkv,
        g_out,
        g_up.reshape(8, high, FF // 8),
        g_maps,
        *vectors,
    )


def lane_sum(value):
    rows, lanes = value.shape[0] // 8, value.shape[1] // TOK
    total = None
    for i in range(rows):
        for j in range(lanes):
            tile = value[i * 8 : (i + 1) * 8, j * TOK : (j + 1) * TOK]
            total = tile if total is None else total + tile
    return total


def square_rows(ref, rows, step):
    def one(i, carry):
        part = ref[pl.ds(pl.multiple_of(i * step, step), step), :].astype(F32)
        return carry + lane_sum(part * part)

    return lax.fori_loop(0, rows // step, one, jnp.zeros((8, TOK), F32))


def scatter_kernel(n_pieces, count_ref, list_ref, d_any, *refs):
    pieces, refs = refs[:n_pieces], refs[n_pieces:]
    mats, small, refs = refs[:4], refs[4:6], refs[6:]
    g_any, pos_ref, sq_ref, held, d_low, d_wide, out, sem = refs
    rows_here = g_any.shape[0]
    first_dev = (lax.axis_index("fsdp") == 0).astype(F32)
    fetch = pltpu.make_async_copy(d_any, d_low, sem.at[n_pieces])
    fetch.start()
    loads, first = [], 0
    for i, piece in enumerate(pieces):
        size = min(piece.shape[0], rows_here - first)
        loads.append(
            pltpu.make_async_copy(piece.at[pl.ds(0, size)], held.at[pl.ds(first, size)], sem.at[i])
        )
        first = first + size
    for load in loads:
        load.start()
    total = jnp.zeros((8, TOK), F32)
    for mat in mats:
        total = total + square_rows(mat, mat.shape[0], 16)
    for part in small:
        total = total + square_rows(part, part.shape[0], 16) * first_dev
    fetch.wait()
    pos_ref[...] = jnp.zeros_like(pos_ref)
    chunk = 64

    def widen(i, carry):
        spot = pl.ds(pl.multiple_of(i * chunk, chunk), chunk)
        wide = d_low[spot, :].astype(F32)
        d_wide[spot, :] = wide
        there = pl.ds(pl.multiple_of((i % (TOK // chunk)) * chunk, chunk), chunk)
        pos_ref[there, :] += wide
        return carry

    lax.fori_loop(0, d_low.shape[0] // chunk, widen, 0)
    pos_ref[...] = pos_ref[...] * first_dev
    total = total + square_rows(pos_ref, TOK, 16)
    for load in loads:
        load.wait()

    def several(i, carry):
        for j in range(8):
            entry = list_ref[i * 8 + j]
            row, token = lax.shift_right_logical(entry, 12), entry & 4095
            held[pl.ds(row, 1), :] += d_wide[pl.ds(token, 1), :]
        return carry

    lax.fori_loop(0, (count_ref[0] + 7) // 8, several, 0)
    step = 48
    parts = 3
    part_rows = rows_here // parts

    for k in range(parts):

        def low(i, carry, k=k):
            spot = pl.ds(pl.multiple_of(k * part_rows + i * step, 16), step)
            value = held[spot, :].astype(BF)
            out[spot, :] = value
            value = value.astype(F32)
            return carry + lane_sum(value * value)

        total = lax.fori_loop(0, part_rows // step, low, total)
        if part_rows % step:
            rest = part_rows % step
            spot = pl.ds(k * part_rows + part_rows - rest, rest)
            value = held[spot, :].astype(BF)
            out[spot, :] = value
            value = value.astype(F32)
            total = total + lane_sum(value * value)
        spot = pl.ds(k * part_rows, part_rows)
        pltpu.make_async_copy(out.at[spot], g_any.at[spot], sem.at[n_pieces + 1 + k]).start()
    sq_ref[...] = total
    for k in range(parts):
        spot = pl.ds(k * part_rows, part_rows)
        pltpu.make_async_copy(out.at[spot], g_any.at[spot], sem.at[n_pieces + 1 + k]).wait()


def add_rows(count, order, pieces, d_tokens, mats, small, rows_here):
    return pl.pallas_call(
        functools.partial(scatter_kernel, len(pieces)),
        out_shape=(
            jax.ShapeDtypeStruct((rows_here, D), BF),
            jax.ShapeDtypeStruct((TOK, D), F32),
            jax.ShapeDtypeStruct((8, TOK), F32),
        ),
        in_specs=[pl.BlockSpec(memory_space=pltpu.SMEM)] * 2
        + any_specs(1 + len(pieces))
        + vmem(6),
        out_specs=tuple(hbm_specs(1) + vmem(2)),
        scratch_shapes=[
            pltpu.VMEM((rows_here + 8, D), F32),
            pltpu.VMEM(d_tokens.shape, BF),
            pltpu.VMEM(d_tokens.shape, F32),
            pltpu.VMEM((rows_here, D), BF),
            pltpu.SemaphoreType.DMA((len(pieces) + 4,)),
        ],
        compiler_params=params(mib=60),
    )(count, order, d_tokens, *pieces, *mats, *small)


def total_kernel(x_ref, o_ref, got, send, recv):
    dp, fs = lax.axis_index("dp"), lax.axis_index("fsdp")
    line = [(dp, fs ^ k) for k in range(1, 8)]
    greet(line)
    link = Link(send, recv)
    copies = [link.copy(x_ref, got.at[fs], peer) for peer in line]
    for copy in copies:
        copy.start()
    got[fs] = x_ref[...]
    for copy in copies:
        copy.wait()
    total = got[0]
    for j in range(1, 8):
        total = total + got[j]
    total = jnp.sum(jnp.sum(total, 0, keepdims=True), 1, keepdims=True)
    o_ref[...] = jnp.sqrt(jnp.broadcast_to(total, o_ref.shape))


def line_norm(x):
    return pl.pallas_call(
        total_kernel,
        out_shape=jax.ShapeDtypeStruct((8, TOK), F32),
        in_specs=vmem(1),
        out_specs=vmem(1)[0],
        scratch_shapes=[pltpu.VMEM((8, 8, TOK), F32)] + sems(7),
        compiler_params=params(6, 4),
    )(x)


def adam_kernel(rates, scale_ref, *refs):
    step = pl.program_id(0)
    n = len(rates)
    ins, outs = refs[: 4 * n], refs[4 * n :]
    for i, rate in enumerate(rates):
        w, m, v, g = ins[4 * i : 4 * i + 4]
        spots = outs[3 * i : 3 * i + 3]

        def update(w=w, m=m, v=v, g=g, spots=spots, rate=rate):
            gradient = g[...].astype(F32) * scale_ref[0]
            new = adam_update(w[...], m[...], v[...], gradient, rate)
            for spot, value in zip(spots, new):
                spot[...] = value

        if i == 0:
            update()
        else:
            pl.when(step % 2 == 0)(update)


def adam_all(scale, groups, rates):
    rows = 528
    steps = pl.cdiv(groups[0][0].shape[0], rows)
    specs = [pl.BlockSpec((rows, D), lambda i: (i, 0))]
    for group in groups[1:]:
        pieces = 6 if group[0].shape[0] % 96 == 0 else 2
        high = group[0].shape[0] // pieces
        stride = 2 * (steps // 2 // pieces)
        specs.append(
            pl.BlockSpec((high, group[0].shape[1]), lambda i, stride=stride: (i // stride, 0))
        )
    return pl.pallas_call(
        functools.partial(adam_kernel, rates),
        grid=(steps,),
        in_specs=[pl.BlockSpec(memory_space=pltpu.SMEM)] + [s for s in specs for k in range(4)],
        out_specs=[s for s in specs for k in range(3)],
        out_shape=[jax.ShapeDtypeStruct(g[0].shape, F32) for g in groups for k in range(3)],
        compiler_params=params(mib=56),
    )(scale.reshape(1), *[a for group in groups for a in group])


def norm_back(values, gain, cotangent):
    center = values - jnp.mean(values, axis=-1, keepdims=True)
    rate = lax.rsqrt(jnp.mean(center * center, axis=-1, keepdims=True) + EPS)
    normed = center * rate
    inner = cotangent * gain
    pull = inner - jnp.mean(inner, axis=-1, keepdims=True)
    pull = rate * (pull - normed * jnp.mean(inner * normed, axis=-1, keepdims=True))
    return (
        pull,
        jnp.sum(cotangent * normed, axis=0, keepdims=True),
        jnp.sum(cotangent, axis=0, keepdims=True),
    )


def attention_forward(inputs, w_qkv, w_out, pieces):
    gain_one, bias_one = pieces[0], pieces[1]
    bias_qkv, bias_out, map_query, map_key = pieces[6], pieces[7], pieces[10], pieces[11]
    length = inputs.shape[0]
    normed_one = layer_norm(inputs, gain_one, bias_one).astype(BF)
    project = dense(normed_one, w_qkv) + bias_qkv
    queries = project[:, :D].astype(BF).reshape(length, H, HD)
    keys_in = project[:, D : 2 * D].astype(BF).reshape(length, H, HD)
    values_in = project[:, 2 * D :].astype(BF).reshape(length, H, HD)
    maps_q = map_query.reshape(H, HD, HD).astype(BF)
    maps_k = map_key.reshape(H, HD, HD).astype(BF)
    inner_q = jnp.einsum("shd,hde->she", queries, maps_q, preferred_element_type=F32)
    inner_k = jnp.einsum("shd,hde->she", keys_in, maps_k, preferred_element_type=F32)
    feat_q = features(inner_q).astype(BF)
    feat_k = features(inner_k).astype(BF)
    scores = jnp.einsum("thf,shf->hts", feat_q, feat_k, preferred_element_type=F32) * causal_mask(
        length
    )
    totals = jnp.sum(scores, axis=-1)
    scores_low = scores.astype(BF)
    numer = jnp.einsum("hts,shd->thd", scores_low, values_in, preferred_element_type=F32)
    attended = numer / jnp.transpose(totals)[:, :, None]
    att_low = attended.reshape(length, D).astype(BF)
    resid_one = inputs + dense(att_low, w_out) + bias_out
    saved = (
        normed_one,
        queries,
        keys_in,
        values_in,
        maps_q,
        maps_k,
        inner_q,
        inner_k,
        feat_q,
        feat_k,
        scores_low,
        totals,
        numer,
        att_low,
    )
    return resid_one, saved


def attention_backward(inputs, w_qkv, w_out, pieces, saved, d_resid_one):
    gain_one = pieces[0]
    (
        normed_one,
        queries,
        keys_in,
        values_in,
        maps_q,
        maps_k,
        inner_q,
        inner_k,
        feat_q,
        feat_k,
        scores_low,
        totals,
        numer,
        att_low,
    ) = saved
    length = inputs.shape[0]
    d_bias_out = jnp.sum(d_resid_one, axis=0, keepdims=True)
    d_out_low = d_resid_one.astype(BF)
    g_out = dense_tn(att_low, d_out_low)
    d_attended = dense_nt(d_out_low, w_out).reshape(length, H, HD)
    inverse = 1.0 / jnp.transpose(totals)
    d_numer_low = (d_attended * inverse[:, :, None]).astype(BF)
    d_totals = jnp.transpose(-jnp.sum(d_attended * numer, axis=-1) * inverse * inverse)
    d_scores = jnp.einsum("thd,shd->hts", d_numer_low, values_in, preferred_element_type=F32)
    d_scores_low = ((d_scores + d_totals[:, :, None]) * causal_mask(length)).astype(BF)
    d_values = jnp.einsum("hts,thd->shd", scores_low, d_numer_low, preferred_element_type=F32)
    d_feat_q = jnp.einsum("hts,shf->thf", d_scores_low, feat_k, preferred_element_type=F32)
    d_feat_k = jnp.einsum("hts,thf->shf", d_scores_low, feat_q, preferred_element_type=F32)
    unused, pull_q = jax.vjp(features, inner_q)
    unused, pull_k = jax.vjp(features, inner_k)
    d_inner_q = pull_q(d_feat_q)[0].astype(BF)
    d_inner_k = pull_k(d_feat_k)[0].astype(BF)
    g_map_q = jnp.einsum("shd,she->hde", queries, d_inner_q, preferred_element_type=F32)
    g_map_k = jnp.einsum("shd,she->hde", keys_in, d_inner_k, preferred_element_type=F32)
    d_queries = jnp.einsum("she,hde->shd", d_inner_q, maps_q, preferred_element_type=F32)
    d_keys = jnp.einsum("she,hde->shd", d_inner_k, maps_k, preferred_element_type=F32)
    d_project = jnp.concatenate(
        [d_queries.reshape(length, D), d_keys.reshape(length, D), d_values.reshape(length, D)],
        axis=1,
    )
    d_bias_qkv = jnp.sum(d_project, axis=0, keepdims=True)
    d_project_low = d_project.astype(BF)
    g_qkv = dense_tn(normed_one, d_project_low)
    d_normed_one = dense_nt(d_project_low, w_qkv)
    d_input_part, d_gain_one, d_bias_one = norm_back(inputs, gain_one, d_normed_one)
    d_inputs = d_resid_one + d_input_part
    return d_inputs, g_qkv, g_out, (d_gain_one, d_bias_one, d_bias_qkv, d_bias_out, g_map_q, g_map_k)


def body(
    tok_ids,
    targets,
    loss_mask,
    embed,
    embed_m,
    embed_v,
    posit,
    posit_m,
    posit_v,
    attn_in,
    attn_in_m,
    attn_in_v,
    attn_out,
    attn_out_m,
    attn_out_v,
    mlp_in,
    mlp_in_m,
    mlp_in_v,
    mlp_out,
    mlp_out_m,
    mlp_out_v,
    small,
    small_m,
    small_v,
):
    dp, rank = lax.axis_index("dp"), lax.axis_index("fsdp")
    shard_rows = embed.shape[0]
    first_row = rank * shard_rows
    mine = jnp.concatenate([tok_ids, targets, loss_mask, jnp.zeros((5, TOK), jnp.int32)], axis=0)
    shared, zq, wqo, zs, zo = first_exchange(mine, attn_in, attn_out, mlp_in)
    all_ids = shared[:, :, 0, :].reshape(4, GROUP)
    all_targets = shared[:, :, 1, :].reshape(4, GROUP)
    all_mask = shared[:, :, 2, :].reshape(4, GROUP).astype(F32)
    token_total = jnp.sum(all_mask)
    weight = all_mask / token_total
    local_ids = all_ids - first_row
    inside = (local_ids >= 0) & (local_ids < shard_rows)
    safe_ids = jnp.clip(local_ids, 0, shard_rows - 1)
    target_local = all_targets - first_row
    target_here = (target_local >= 0) & (target_local < shard_rows)
    target_local = jnp.where(target_here, target_local, -1)
    group_ids = lax.dynamic_index_in_dim(safe_ids, dp, 0, False)
    group_in = lax.dynamic_index_in_dim(inside, dp, 0, False)
    target_rows = target_local.reshape(4, 1, GROUP)
    weight_rows = weight.reshape(4, 1, GROUP)
    looked = jnp.where(group_in[:, None], jnp.take(embed, group_ids, axis=0), 0.0).astype(BF)

    small_pad = -small.shape[0] % (16 * TOK)
    w_two = mlp_out.astype(BF)
    embedded, wqo, w_one, small_full, positions = start_exchange(
        looked,
        wqo,
        zq,
        zs,
        zo,
        jnp.pad(small, (0, small_pad)).astype(BF).reshape(-1, TOK),
        posit.astype(BF),
    )
    wqo = wqo.reshape(D, 4 * D)
    w_one = w_one.reshape(D, FF // 8)
    w_qkv, w_out = wqo[:, : 3 * D], wqo[:, 3 * D :]
    small_full = small_full.reshape(8, -1)[:, : small.shape[0]].reshape(-1)
    pieces = unpack(small_full.astype(F32))
    gain_two, bias_two, gain_fin, bias_fin = pieces[2:6]
    bias_up, bias_down = pieces[8], pieces[9]
    own_up = lax.dynamic_slice_in_dim(bias_up, rank * (FF // 8), FF // 8)

    inputs = embedded + positions.astype(F32)
    resid_one, saved = attention_forward(inputs, w_qkv, w_out, pieces)
    mlp_sum, normed_two, pre_act, act_low = mlp_forward(
        layer_norm(resid_one, gain_two, bias_two).astype(BF), w_one, w_two, own_up
    )
    resid_two = resid_one + mlp_sum + bias_down
    final_own = layer_norm(resid_two, gain_fin, bias_fin).astype(BF)
    grown, stats, table, final, near_final = own_logits(embed, final_own, target_rows)
    lse, hits = combine_stats(stats)
    loss = jnp.sum((lse - hits).reshape(4, GROUP) * all_mask) / token_total
    d_final, all_final = final_cotangent(
        grown, stats, lse, weight_rows, target_rows, table, final, near_final
    )
    tokens = (
        all_final.reshape(4, GROUP, D),
        lse,
        weight_rows,
        target_rows,
    )
    fill = (table,) + tokens
    starts = [table.shape[0] - FILL * (4 - i) for i in range(4)]
    d_final, block_a = sum_tokens_fill(d_final, fill, starts[0], 10)

    d_resid_two, d_gain_fin, d_bias_fin = norm_back(resid_two, gain_fin, d_final)
    d_bias_down = jnp.sum(d_resid_two, axis=0, keepdims=True)
    d_normed_two, g_down, g_up, d_bias_own, block_b, block_c = mlp_backward(
        d_resid_two.astype(BF),
        w_one,
        w_two,
        pre_act,
        act_low,
        normed_two,
        fill,
        starts[1],
        starts[2],
        12,
    )
    d_resid_part, d_gain_two, d_bias_two = norm_back(resid_one, gain_two, d_normed_two)
    d_resid_one = d_resid_two + d_resid_part
    d_inputs, g_qkv, g_out, small_parts = attention_backward(
        inputs, w_qkv, w_out, pieces, saved, d_resid_one
    )
    d_gain_one, d_bias_one, d_bias_qkv, d_bias_out, g_map_q, g_map_k = small_parts
    d_low = d_inputs.astype(BF)
    group_back, side_back, s_qkv, s_out, g_down, block_d = gather_tokens_last(
        d_low, g_qkv.astype(BF), g_out.astype(BF), g_down, fill, starts[3], 13
    )

    vectors = (
        (d_gain_one, d_bias_one, d_gain_two, d_bias_two, d_gain_fin, d_bias_fin)
        + (d_bias_qkv, d_bias_out, d_bias_own, d_bias_down)
    )
    g_maps = jnp.concatenate([g_map_q.reshape(HD, D), g_map_k.reshape(HD, D)], axis=0)

    g_table, all_back, g_qkv, g_out, g_up, g_maps, g_vec = table_gradient(
        starts[0],
        table,
        tokens,
        group_back,
        side_back,
        s_qkv,
        s_out,
        g_up,
        g_maps.reshape(8, 2 * HD // 8, D).astype(BF),
        vectors,
    )
    all_back = all_back.reshape(-1, D)
    g_small = jnp.concatenate([g_vec[:15], g_maps.reshape(2 * HD, D).astype(F32)], axis=0)
    g_small = g_small.reshape(-1)
    g_small = lax.dynamic_slice_in_dim(g_small, rank * small.shape[0], small.shape[0])
    flat_in = inside.reshape(-1)
    row_of = jnp.where(flat_in, local_ids.reshape(-1), shard_rows)
    order = lax.sort(row_of * 4096 + lax.iota(jnp.int32, flat_in.shape[0]))
    count = jnp.sum(flat_in.astype(jnp.int32)).reshape(1)
    g_table, g_posit, squares = add_rows(
        count,
        order,
        (g_table, block_a, block_b, block_c, block_d),
        all_back,
        (g_qkv, g_out, g_up, g_down),
        (g_vec, g_maps.reshape(2 * HD, D)),
        shard_rows,
    )
    grad_norm = line_norm(squares)[0, 0]
    scale = CLIP_LIMIT / jnp.maximum(grad_norm, CLIP_LIMIT)
    rates = rate_list()
    groups = (
        (embed, embed_m, embed_v, g_table),
        (posit, posit_m, posit_v, g_posit),
        (attn_in, attn_in_m, attn_in_v, g_qkv),
        (attn_out, attn_out_m, attn_out_v, g_out),
        (mlp_in, mlp_in_m, mlp_in_v, g_up),
        (mlp_out, mlp_out_m, mlp_out_v, g_down),
    )
    new = adam_all(scale, groups, rates[:6])
    new_small = adam_update(small, small_m, small_v, g_small * scale, rates[6])
    return (loss, grad_norm, *new, *new_small)


def solution(mesh):
    fits = mesh.shape["dp"] == 4 and mesh.shape["fsdp"] == 8
    step = body if fits else body_general
    in_specs = (
        P(("dp", "fsdp"), None),
        P(("dp", "fsdp"), None),
        P(("dp", "fsdp"), None),
        P("fsdp", None),
        P("fsdp", None),
        P("fsdp", None),
        P("fsdp", None),
        P("fsdp", None),
        P("fsdp", None),
        P("fsdp", None),
        P("fsdp", None),
        P("fsdp", None),
        P("fsdp", None),
        P("fsdp", None),
        P("fsdp", None),
        P("fsdp", None),
        P("fsdp", None),
        P("fsdp", None),
        P("fsdp", None),
        P("fsdp", None),
        P("fsdp", None),
        P("fsdp"),
        P("fsdp"),
        P("fsdp"),
    )
    out_specs = (
        P(),
        P(),
        P("fsdp", None),
        P("fsdp", None),
        P("fsdp", None),
        P("fsdp", None),
        P("fsdp", None),
        P("fsdp", None),
        P("fsdp", None),
        P("fsdp", None),
        P("fsdp", None),
        P("fsdp", None),
        P("fsdp", None),
        P("fsdp", None),
        P("fsdp", None),
        P("fsdp", None),
        P("fsdp", None),
        P("fsdp", None),
        P("fsdp", None),
        P("fsdp", None),
        P("fsdp"),
        P("fsdp"),
        P("fsdp"),
    )
    return jax.shard_map(step, mesh=mesh, in_specs=in_specs, out_specs=out_specs, check_vma=False)
```

```python
import functools
from functools import reduce

import jax
import jax.numpy as jnp
from jax import lax
from jax.experimental import pallas as pl
from jax.experimental.pallas import tpu as pltpu
from jax.sharding import PartitionSpec as P

D = 768
H = 12
HD = 64
FF = 3072
STEP = 2


EPS = 1e-05
CLIP_LIMIT = 0.01
BETA = 0.5
DECAY = 0.1
ADAM_EPS = 1e-08


def combined_all(value, axis, join):
    pieces = jax.tree.map(lambda part: lax.all_gather(part, axis), value)
    head = jax.tree.map(lambda part: part[0], pieces)
    tail = jax.tree.map(lambda part: part[1:], pieces)
    subtotal, _ = lax.scan(lambda subtotal, piece: (join(subtotal, piece), None), head, tail)
    return subtotal


def dense(left, right):
    return jnp.dot(left, right, preferred_element_type=jnp.float32)


def dense_tn(left, right):
    return lax.dot_general(
        left, right, (((0,), (0,)), ((), ())), preferred_element_type=jnp.float32
    )


def dense_nt(left, right):
    return lax.dot_general(
        left, right, (((1,), (1,)), ((), ())), preferred_element_type=jnp.float32
    )


def layer_norm(values, gain, bias):
    center = values - jnp.mean(values, axis=-1, keepdims=True)
    spread = jnp.mean(center * center, axis=-1, keepdims=True)
    return center * lax.rsqrt(spread + EPS) * gain + bias


def features(inner):
    return jnp.concatenate(
        [jax.nn.softmax(inner, axis=-1), jax.nn.softmax(-inner, axis=-1)], axis=-1
    )


def gelu_tanh(values):
    return jax.nn.gelu(values, approximate=True)


def unpack(vector):
    cuts = [D, D, D, D, D, D, 3 * D, D, FF, D, H * HD * HD, H * HD * HD]
    pieces = []
    offset = 0
    for piece_len in cuts:
        pieces.append(vector[offset : offset + piece_len])
        offset = offset + piece_len
    return pieces


def rate_list():
    return (2.0 * D ** (-0.5), 0.5, D ** (-0.5), (32.0 / D) ** 0.5, D ** (-0.5), FF ** (-0.5), 0.1)


def norm_pull(values, gain, bias, cotangent):
    unused, pull = jax.vjp(layer_norm, values, gain, bias)
    return pull(cotangent)


def causal_mask(length):
    rows_idx = lax.broadcasted_iota(jnp.int32, (length, length), 0)
    cols_idx = lax.broadcasted_iota(jnp.int32, (length, length), 1)
    return (rows_idx >= cols_idx).astype(jnp.float32)


def layer_forward(inputs, mats, pieces):
    w_qkv, w_out, w_up, w_down = mats
    (
        gain_one,
        bias_one,
        gain_two,
        bias_two,
        gain_fin,
        bias_fin,
        bias_qkv,
        bias_out,
        bias_up,
        bias_down,
        map_query,
        map_key,
    ) = pieces
    length = inputs.shape[0]
    normed_one = layer_norm(inputs, gain_one, bias_one).astype(jnp.bfloat16)
    project = dense(normed_one, w_qkv) + bias_qkv
    queries = project[:, :D].astype(jnp.bfloat16).reshape(length, H, HD)
    keys_in = project[:, D : 2 * D].astype(jnp.bfloat16).reshape(length, H, HD)
    values_in = project[:, 2 * D :].astype(jnp.bfloat16).reshape(length, H, HD)
    maps_q = map_query.reshape(H, HD, HD).astype(jnp.bfloat16)
    maps_k = map_key.reshape(H, HD, HD).astype(jnp.bfloat16)
    inner_q = jnp.einsum("shd,hde->she", queries, maps_q, preferred_element_type=jnp.float32)
    inner_k = jnp.einsum("shd,hde->she", keys_in, maps_k, preferred_element_type=jnp.float32)
    feat_q = features(inner_q).astype(jnp.bfloat16)
    feat_k = features(inner_k).astype(jnp.bfloat16)
    scores = jnp.einsum(
        "thf,shf->hts", feat_q, feat_k, preferred_element_type=jnp.float32
    ) * causal_mask(length)
    totals = jnp.sum(scores, axis=-1)
    scores_low = scores.astype(jnp.bfloat16)
    numer = jnp.einsum("hts,shd->thd", scores_low, values_in, preferred_element_type=jnp.float32)
    attended = numer / jnp.transpose(totals)[:, :, None]
    att_low = attended.reshape(length, D).astype(jnp.bfloat16)
    resid_one = inputs + dense(att_low, w_out) + bias_out
    normed_two = layer_norm(resid_one, gain_two, bias_two).astype(jnp.bfloat16)
    pre_act = dense(normed_two, w_up) + bias_up
    act_low = gelu_tanh(pre_act).astype(jnp.bfloat16)
    resid_two = resid_one + dense(act_low, w_down) + bias_down
    final = layer_norm(resid_two, gain_fin, bias_fin)
    saved = (
        normed_one,
        queries,
        keys_in,
        values_in,
        maps_q,
        maps_k,
        inner_q,
        inner_k,
        feat_q,
        feat_k,
        scores_low,
        totals,
        numer,
        att_low,
        resid_one,
        normed_two,
        pre_act,
        act_low,
        resid_two,
    )
    return (final, saved)


def layer_backward(inputs, mats, pieces, saved, d_final):
    w_qkv, w_out, w_up, w_down = mats
    (
        gain_one,
        bias_one,
        gain_two,
        bias_two,
        gain_fin,
        bias_fin,
        bias_qkv,
        bias_out,
        bias_up,
        bias_down,
        map_query,
        map_key,
    ) = pieces
    (
        normed_one,
        queries,
        keys_in,
        values_in,
        maps_q,
        maps_k,
        inner_q,
        inner_k,
        feat_q,
        feat_k,
        scores_low,
        totals,
        numer,
        att_low,
        resid_one,
        normed_two,
        pre_act,
        act_low,
        resid_two,
    ) = saved
    length = inputs.shape[0]
    d_resid_two, d_gain_fin, d_bias_fin = norm_pull(resid_two, gain_fin, bias_fin, d_final)
    d_bias_down = jnp.sum(d_resid_two, axis=0)
    d_down_low = d_resid_two.astype(jnp.bfloat16)
    g_down = dense_tn(act_low, d_down_low)
    d_act = dense_nt(d_down_low, w_down)
    unused, gelu_back = jax.vjp(gelu_tanh, pre_act)
    d_pre = gelu_back(d_act)[0]
    d_bias_up = jnp.sum(d_pre, axis=0)
    d_pre_low = d_pre.astype(jnp.bfloat16)
    g_up = dense_tn(normed_two, d_pre_low)
    d_normed_two = dense_nt(d_pre_low, w_up)
    d_resid_part, d_gain_two, d_bias_two = norm_pull(resid_one, gain_two, bias_two, d_normed_two)
    d_resid_one = d_resid_two + d_resid_part
    d_bias_out = jnp.sum(d_resid_one, axis=0)
    d_out_low = d_resid_one.astype(jnp.bfloat16)
    g_out = dense_tn(att_low, d_out_low)
    d_attended = dense_nt(d_out_low, w_out).reshape(length, H, HD)
    inverse = 1.0 / jnp.transpose(totals)
    d_numer_low = (d_attended * inverse[:, :, None]).astype(jnp.bfloat16)
    d_totals = jnp.transpose(-jnp.sum(d_attended * numer, axis=-1) * inverse * inverse)
    d_scores = jnp.einsum(
        "thd,shd->hts", d_numer_low, values_in, preferred_element_type=jnp.float32
    )
    d_scores_low = ((d_scores + d_totals[:, :, None]) * causal_mask(length)).astype(jnp.bfloat16)
    d_values = jnp.einsum(
        "hts,thd->shd", scores_low, d_numer_low, preferred_element_type=jnp.float32
    )
    d_feat_q = jnp.einsum("hts,shf->thf", d_scores_low, feat_k, preferred_element_type=jnp.float32)
    d_feat_k = jnp.einsum("hts,thf->shf", d_scores_low, feat_q, preferred_element_type=jnp.float32)
    unused, pull_q = jax.vjp(features, inner_q)
    unused, pull_k = jax.vjp(features, inner_k)
    d_inner_q = pull_q(d_feat_q)[0].astype(jnp.bfloat16)
    d_inner_k = pull_k(d_feat_k)[0].astype(jnp.bfloat16)
    g_map_q = jnp.einsum("shd,she->hde", queries, d_inner_q, preferred_element_type=jnp.float32)
    g_map_k = jnp.einsum("shd,she->hde", keys_in, d_inner_k, preferred_element_type=jnp.float32)
    d_queries = jnp.einsum("she,hde->shd", d_inner_q, maps_q, preferred_element_type=jnp.float32)
    d_keys = jnp.einsum("she,hde->shd", d_inner_k, maps_k, preferred_element_type=jnp.float32)
    d_project = jnp.concatenate(
        [d_queries.reshape(length, D), d_keys.reshape(length, D), d_values.reshape(length, D)],
        axis=1,
    )
    d_bias_qkv = jnp.sum(d_project, axis=0)
    d_project_low = d_project.astype(jnp.bfloat16)
    g_qkv = dense_tn(normed_one, d_project_low)
    d_normed_one = dense_nt(d_project_low, w_qkv)
    d_input_part, d_gain_one, d_bias_one = norm_pull(inputs, gain_one, bias_one, d_normed_one)
    d_inputs = d_resid_one + d_input_part
    g_small = jnp.concatenate(
        [
            d_gain_one,
            d_bias_one,
            d_gain_two,
            d_bias_two,
            d_gain_fin,
            d_bias_fin,
            d_bias_qkv,
            d_bias_out,
            d_bias_up,
            d_bias_down,
            g_map_q.reshape(-1),
            g_map_k.reshape(-1),
        ]
    )
    return (d_inputs, (g_qkv, g_out, g_up, g_down), g_small)


def adam_update(weight, first_old, second_old, gradient, rate):
    first_new = BETA * first_old + (1.0 - BETA) * gradient
    second_new = BETA * second_old + (1.0 - BETA) * gradient * gradient
    bias_fix = 1.0 - BETA**STEP
    weight_new = weight - rate * (
        first_new / bias_fix / (jnp.sqrt(second_new / bias_fix) + ADAM_EPS) + DECAY * weight
    )
    return (weight_new, first_new, second_new)


def combine_lse(first_part, second_part):
    top = jnp.maximum(first_part[0], second_part[0])
    merged = first_part[1] * jnp.exp(first_part[0] - top) + second_part[1] * jnp.exp(
        second_part[0] - top
    )
    return (top, merged, first_part[2] + second_part[2])


def body_general(
    tok_ids,
    targets,
    loss_mask,
    embed,
    embed_m,
    embed_v,
    posit,
    posit_m,
    posit_v,
    attn_in,
    attn_in_m,
    attn_in_v,
    attn_out,
    attn_out_m,
    attn_out_v,
    mlp_in,
    mlp_in_m,
    mlp_in_v,
    mlp_out,
    mlp_out_m,
    mlp_out_v,
    small,
    small_m,
    small_v,
):
    rank = lax.axis_index("fsdp")
    length = tok_ids.shape[1]
    all_ids, all_targets, all_mask = (
        lax.all_gather(tok_ids, "fsdp", axis=0, tiled=True),
        lax.all_gather(targets, "fsdp", axis=0, tiled=True),
        lax.all_gather(loss_mask, "fsdp", axis=0, tiled=True),
    )
    all_ids = all_ids.reshape(-1)
    all_targets = all_targets.reshape(-1)
    mask_all = all_mask.reshape(-1).astype(jnp.float32)
    pos_full, w_qkv, w_out, w_up, w_down, small_full = (
        lax.all_gather(posit.astype(jnp.bfloat16), "fsdp", axis=0, tiled=True),
        lax.all_gather(attn_in.astype(jnp.bfloat16), "fsdp", axis=0, tiled=True),
        lax.all_gather(attn_out.astype(jnp.bfloat16), "fsdp", axis=0, tiled=True),
        lax.all_gather(mlp_in.astype(jnp.bfloat16), "fsdp", axis=0, tiled=True),
        lax.all_gather(mlp_out.astype(jnp.bfloat16), "fsdp", axis=0, tiled=True),
        lax.all_gather(small.astype(jnp.bfloat16), "fsdp", axis=0, tiled=True),
    )
    mats = (w_qkv, w_out, w_up, w_down)
    pieces = unpack(small_full.astype(jnp.float32))
    shard_rows = embed.shape[0]
    first_row = rank * shard_rows
    table = embed.astype(jnp.bfloat16)
    local_ids = all_ids - first_row
    inside = (local_ids >= 0) & (local_ids < shard_rows)
    safe_ids = jnp.clip(local_ids, 0, shard_rows - 1)
    looked = jnp.where(
        inside[:, None], jnp.take(table, safe_ids, axis=0), jnp.zeros((), jnp.bfloat16)
    )
    embedded = lax.psum_scatter(looked, "fsdp", scatter_dimension=0, tiled=True).astype(jnp.float32)
    inputs = embedded + pos_full[:length].astype(jnp.float32)
    final, saved = layer_forward(inputs, mats, pieces)
    final_low = final.astype(jnp.bfloat16)
    target_local = all_targets - first_row
    piece = lax.all_gather(final_low, "fsdp", axis=0, tiled=True)
    logits = dense_nt(piece, table)
    row_max = jnp.max(logits, axis=1)
    row_sum = jnp.sum(jnp.exp(logits - row_max[:, None]), axis=1)
    columns = lax.broadcasted_iota(jnp.int32, logits.shape, 1)
    row_hit = jnp.sum(jnp.where(columns == target_local[:, None], logits, 0.0), axis=1)
    maxes = row_max
    sums = row_sum
    hits = row_hit
    maxes, sums, hits = combined_all((maxes, sums, hits), "fsdp", combine_lse)
    log_total = maxes + jnp.log(sums)
    own_terms = lax.dynamic_slice_in_dim((log_total - hits) * mask_all, rank * length, length)
    loss_sum, token_total = lax.psum(
        (jnp.sum(own_terms), jnp.sum(loss_mask.astype(jnp.float32))), ("dp", "fsdp")
    )
    loss = loss_sum / token_total
    columns = lax.broadcasted_iota(jnp.int32, logits.shape, 1)
    onehot = jnp.where(columns == target_local[:, None], 1.0, 0.0)
    d_logits = (
        (jnp.exp(logits - log_total[:, None]) - onehot) * (mask_all / token_total)[:, None]
    ).astype(jnp.bfloat16)
    g_table = dense_tn(d_logits, piece)
    d_final = lax.psum_scatter(dense(d_logits, table), "fsdp", scatter_dimension=0, tiled=True)
    d_inputs, mat_grads, g_small = layer_backward(inputs, mats, pieces, saved, d_final)
    g_qkv, g_out, g_up, g_down = mat_grads
    d_low = d_inputs.astype(jnp.bfloat16)
    all_back = lax.all_gather(d_low, "fsdp", axis=0, tiled=True)
    g_table = g_table.at[safe_ids].add(
        jnp.where(inside[:, None], all_back.astype(jnp.float32), 0.0)
    )
    g_posit = jnp.concatenate(
        [d_low.astype(jnp.float32), jnp.zeros((pos_full.shape[0] - length, D), jnp.float32)], axis=0
    )
    layer_grads = (g_posit, g_qkv, g_out, g_up, g_down, g_small)
    owned = (
        lax.psum_scatter(
            layer_grads[0].astype(jnp.bfloat16), "fsdp", scatter_dimension=0, tiled=True
        ).astype(jnp.float32),
        lax.psum_scatter(
            layer_grads[1].astype(jnp.bfloat16), "fsdp", scatter_dimension=0, tiled=True
        ).astype(jnp.float32),
        lax.psum_scatter(
            layer_grads[2].astype(jnp.bfloat16), "fsdp", scatter_dimension=0, tiled=True
        ).astype(jnp.float32),
        lax.psum_scatter(
            layer_grads[3].astype(jnp.bfloat16), "fsdp", scatter_dimension=0, tiled=True
        ).astype(jnp.float32),
        lax.psum_scatter(
            layer_grads[4].astype(jnp.bfloat16), "fsdp", scatter_dimension=0, tiled=True
        ).astype(jnp.float32),
        lax.psum_scatter(
            layer_grads[5].astype(jnp.bfloat16), "fsdp", scatter_dimension=0, tiled=True
        ).astype(jnp.float32),
    )
    grads = tuple(
        lax.psum((g_table, owned[0], owned[1], owned[2], owned[3], owned[4], owned[5]), "dp")
    )
    local_sq = reduce(
        lambda acc, gradient: acc + jnp.sum(gradient * gradient), grads, jnp.float32(0.0)
    )
    grad_norm = jnp.sqrt(lax.psum(local_sq, "fsdp"))
    scale = CLIP_LIMIT / jnp.maximum(grad_norm, CLIP_LIMIT)
    params = (embed, posit, attn_in, attn_out, mlp_in, mlp_out, small)
    firsts = (embed_m, posit_m, attn_in_m, attn_out_m, mlp_in_m, mlp_out_m, small_m)
    seconds = (embed_v, posit_v, attn_in_v, attn_out_v, mlp_in_v, mlp_out_v, small_v)
    results = [loss, grad_norm]
    for weight, first_old, second_old, gradient, rate in zip(
        params, firsts, seconds, grads, rate_list()
    ):
        results.extend(adam_update(weight, first_old, second_old, gradient * scale, rate))
    return tuple(results)


BF = jnp.bfloat16
F32 = jnp.float32
MESH = pl.DeviceIdType.MESH
TOK = 128
GROUP = 8 * TOK
VBLK = 1280
FILL = 720
TBLK = 704


def params(cid=None, mib=56):
    if cid is None:
        return pltpu.CompilerParams(vmem_limit_bytes=mib << 20)
    return pltpu.CompilerParams(
        collective_id=cid, has_side_effects=True, vmem_limit_bytes=mib << 20
    )


def vmem(count):
    return [pl.BlockSpec(memory_space=pltpu.VMEM)] * count


def any_specs(count):
    return [pl.BlockSpec(memory_space=pl.ANY)] * count


def sems(count):
    return [pltpu.SemaphoreType.DMA((count,))] * 2


class Link:
    def __init__(self, send, recv):
        self.send, self.recv, self.used = send, recv, 0

    def copy(self, src, dst, peer, land=None):
        slot = self.used
        self.used += 1
        return pltpu.make_async_remote_copy(
            src_ref=src,
            dst_ref=dst,
            send_sem=self.send.at[slot],
            recv_sem=self.recv.at[slot if land is None else land],
            device_id=peer,
            device_id_type=MESH,
        )


def greet(peers, extra=None):
    barrier = pltpu.get_barrier_semaphore()
    for peer in peers:
        pl.semaphore_signal(barrier, inc=1, device_id=peer, device_id_type=MESH)
    if extra is None:
        pl.semaphore_wait(barrier, len(peers))
    else:
        flag, peer = extra

        @pl.when(flag)
        def _():
            pl.semaphore_signal(barrier, inc=1, device_id=peer, device_id_type=MESH)

        pl.semaphore_wait(barrier, len(peers) + flag.astype(jnp.int32))


def middle_chip(fs):
    chip = fs // 2
    return (chip == 1) | (chip == 2)


def quarter_of(who, shape):
    high, wide = shape[-2] // 2, shape[-1] // 2
    return (
        pl.ds(pl.multiple_of((who // 2) * high, 16), high),
        pl.ds(pl.multiple_of((who % 2) * wide, 128), wide),
    )


def first_kernel(
    x_ref, a_in, a_out, m_in, o_ref, zq_ref, wqo, zs_ref, zo_ref, a_wide, o_wide, m_wide, w1, keep, send, recv
):
    dp, fs = lax.axis_index("dp"), lax.axis_index("fsdp")
    chip, core, pair = fs // 2, fs % 2, (dp, fs ^ 1)
    mid = middle_chip(fs)
    line = [(k, (dp, fs ^ k)) for k in range(1, 8)]
    plane = [(k, (dp ^ k, fs)) for k in range(1, 4)]
    fetch = [
        pltpu.make_async_copy(src, dst, keep.at[i])
        for i, (src, dst) in enumerate(((a_in, a_wide), (a_out, o_wide), (m_in, m_wide)))
    ]
    for copy in fetch:
        copy.start()
    greet([peer for k, peer in line + plane])
    link = Link(send, recv)
    o_ref[dp, fs] = x_ref[...]
    ids_line = [link.copy(x_ref, o_ref.at[dp, fs], peer) for k, peer in line]
    ids_plane = [link.copy(o_ref.at[dp], o_ref.at[dp], peer) for k, peer in plane]
    for copy in ids_line:
        copy.start()
    for copy in fetch[:2]:
        copy.wait()
    wqo[:, : 3 * D] = a_wide[...].astype(BF)
    wqo[:, 3 * D :] = o_wide[...].astype(BF)
    near, far, across = [(dp, fs ^ k) for k in (2, 4, 6)]
    piece = wqo.at[quarter_of(dp, wqo.shape)]
    zq_ref[chip] = piece[...]
    to_near = link.copy(piece, zq_ref.at[chip], near)
    to_far = link.copy(piece, zq_ref.at[chip], far)
    land = link.used
    to_across = link.copy(piece, zq_ref.at[chip], across, land)
    relay = link.copy(zq_ref.at[chip ^ 2], zq_ref.at[chip ^ 2], near, land)
    to_far.start()
    to_near.start()

    @pl.when(mid)
    def _():
        to_across.start()

    fetch[2].wait()
    w1[...] = m_wide[...].astype(BF)
    width = zs_ref.shape[2]

    def strip(who):
        return w1.at[:, pl.ds(pl.multiple_of(who * width, 128), width)]

    zo_ref[core] = strip(fs)[...]
    to_pair = link.copy(strip(fs ^ 1), zo_ref.at[core], pair)
    to_pair.start()
    land = link.used
    down = [link.copy(strip(fs ^ k), zs_ref.at[core], peer, land + core) for k, peer in line if k > 1]
    got = [link.copy(zs_ref.at[j], zs_ref.at[j], pair, land + j) for j in range(2)]
    source = chip == dp

    @pl.when(source)
    def _():
        for copy in down:
            copy.start()

    for copy in ids_line:
        copy.wait()
    for copy in ids_plane:
        copy.start()
    to_far.wait_recv()

    @pl.when(mid)
    def _():
        relay.start()

    to_near.wait_recv()
    to_across.wait_recv()
    to_near.wait_send()
    to_far.wait_send()

    @pl.when(mid)
    def _():
        to_across.wait_send()
        relay.wait_send()

    for copy in ids_plane + [to_pair]:
        copy.wait()

    @pl.when(source)
    def _():
        zs_ref[...] = zo_ref[...]
        for copy in down:
            copy.wait_send()

    @pl.when(jnp.logical_not(source))
    def _():
        for copy in got:
            copy.wait_recv()


def first_exchange(x, a_in, a_out, m_in):
    high = a_in.shape[0]
    strips = jax.ShapeDtypeStruct((2, high, FF // 8), BF)
    return pl.pallas_call(
        first_kernel,
        out_shape=(
            jax.ShapeDtypeStruct((4, 8, 8, TOK), jnp.int32),
            jax.ShapeDtypeStruct((4, high // 2, 2 * D), BF),
            jax.ShapeDtypeStruct((high, 4 * D), BF),
            strips,
            strips,
        ),
        in_specs=vmem(1) + any_specs(3),
        out_specs=tuple(vmem(5)),
        scratch_shapes=[
            pltpu.VMEM((high, 3 * D), F32),
            pltpu.VMEM((high, D), F32),
            pltpu.VMEM((high, FF), F32),
            pltpu.VMEM((high, FF), BF),
            pltpu.SemaphoreType.DMA((3,)),
        ]
        + sems(26),
        compiler_params=params(1, 12),
    )(x, a_in, a_out, m_in)


class Spread:
    slots = 8

    def __init__(self, link, dp, fs, x_ref, o_ref):
        self.fs, self.x, self.o = fs, x_ref, o_ref
        self.mid = middle_chip(fs)
        near, far, across, pair = [(dp, fs ^ k) for k in (2, 4, 6, 1)]
        mine = o_ref.at[fs]
        self.near = link.copy(x_ref, mine, near)
        self.far = link.copy(x_ref, mine, far)
        land = link.used
        self.across = link.copy(x_ref, mine, across, land)
        self.relay = link.copy(o_ref.at[fs ^ 4], o_ref.at[fs ^ 4], near, land)
        self.pair = [
            link.copy(x_ref if k == 0 else o_ref.at[fs ^ k], o_ref.at[fs ^ k], pair)
            for k in (0, 2, 4, 6)
        ]

    def start(self):
        self.far.start()
        self.near.start()

        @pl.when(self.mid)
        def _():
            self.across.start()

        self.pair[0].start()
        self.o[self.fs] = self.x[...]

    def forward(self, after=None):
        self.far.wait_recv()

        @pl.when(self.mid)
        def _():
            self.relay.start()

        self.pair[2].start()
        if after:
            after(4)
        self.near.wait_recv()
        self.pair[1].start()
        if after:
            after(2)

    def late(self, after=None):
        self.across.wait_recv()
        self.pair[3].start()
        if after:
            after(6)

    def finish(self):
        for copy in self.pair:
            copy.wait_recv()
        self.sent()

    def sent(self):
        for copy in self.pair:
            copy.wait_send()
        self.near.wait_send()
        self.far.wait_send()

        @pl.when(self.mid)
        def _():
            self.across.wait_send()
            self.relay.wait_send()


class Fold:
    slots = 8

    def __init__(self, link, dp, fs, x_ref, part, sums, got):
        self.fs, self.x, self.part, self.sums, self.got = fs, x_ref, part, sums, got
        self.mid = middle_chip(fs)
        near, far, across, pair = [(dp, fs ^ k) for k in (2, 4, 6, 1)]
        self.pair = [link.copy(x_ref.at[fs ^ 1 ^ (2 * k)], part.at[k], pair) for k in range(4)]
        self.near = link.copy(sums.at[1], got.at[0], near)
        self.far = link.copy(sums.at[2], got.at[1], far)
        self.across = link.copy(sums.at[3], got.at[2], across)
        self.relay = link.copy(sums.at[3], got.at[3], near)

    def start(self):
        for k in (3, 2, 1, 0):
            self.pair[k].start()

    def add(self, k):
        self.pair[k].wait_recv()
        return self.x[self.fs ^ (2 * k)].astype(F32) + self.part[k].astype(F32)

    def first(self):
        self.sums[3] = self.add(3).astype(BF)

        @pl.when(self.mid)
        def _():
            self.across.start()

        @pl.when(jnp.logical_not(self.mid))
        def _():
            self.relay.start()
            self.sums[2] = self.add(2).astype(BF)
            self.far.start()

        self.sums[1] = self.add(1).astype(BF)
        self.near.start()

    def second(self):
        @pl.when(self.mid)
        def _():
            both = self.add(2)
            self.relay.wait_recv()
            self.sums[2] = (both + self.got[3].astype(F32)).astype(BF)
            self.far.start()

    def middle(self):
        self.first()
        self.second()

    def finish(self, o_ref):
        o_ref[...] = self.add(0)
        self.near.wait_recv()
        o_ref[...] += self.got[0].astype(F32)
        self.far.wait_recv()
        o_ref[...] += self.got[1].astype(F32)

        @pl.when(self.mid)
        def _():
            self.across.wait_recv()
            o_ref[...] += self.got[2].astype(F32)
            self.across.wait_send()

        @pl.when(jnp.logical_not(self.mid))
        def _():
            self.relay.wait_send()

        for copy in self.pair:
            copy.wait_send()
        self.near.wait_send()
        self.far.wait_send()


def fold_scratch():
    return [pltpu.VMEM((4, TOK, D), BF)] * 3


def line_peers(dp, fs):
    return [(dp, fs ^ k) for k in (1, 2, 4)], (middle_chip(fs), (dp, fs ^ 6))


def spread_kernel(x_ref, o_ref, send, recv):
    dp, fs = lax.axis_index("dp"), lax.axis_index("fsdp")
    greet(*line_peers(dp, fs))
    spread = Spread(Link(send, recv), dp, fs, x_ref, o_ref)
    spread.start()
    spread.forward()
    spread.late()
    spread.finish()


def gather_tokens(x):
    out = pl.pallas_call(
        spread_kernel,
        out_shape=jax.ShapeDtypeStruct((8, TOK, D), BF),
        in_specs=vmem(1),
        out_specs=vmem(1)[0],
        scratch_shapes=sems(Spread.slots),
        compiler_params=params(2, 16),
    )(x)
    return out.reshape(GROUP, D)


def fold_kernel(x_ref, o_ref, part, sums, got, send, recv):
    dp, fs = lax.axis_index("dp"), lax.axis_index("fsdp")
    greet(*line_peers(dp, fs))
    fold = Fold(Link(send, recv), dp, fs, x_ref, part, sums, got)
    fold.start()
    fold.middle()
    fold.finish(o_ref)


def sum_tokens(x):
    return pl.pallas_call(
        fold_kernel,
        out_shape=jax.ShapeDtypeStruct((TOK, D), F32),
        in_specs=vmem(1),
        out_specs=vmem(1)[0],
        scratch_shapes=fold_scratch() + sems(Fold.slots),
        compiler_params=params(3, 16),
    )(x.reshape(8, TOK, D))


def add_up(first, others):
    total = first.astype(F32)
    for other in others:
        total = total + other.astype(F32)
    return total


def table_terms(table, first_row, low, high, h_ref, lse_ref, w_ref, t_ref, o_ref):
    row = lax.broadcasted_iota(jnp.int32, (table.shape[0], GROUP), 0) + first_row
    logits = dense_nt(table, h_ref[low])
    for d in range(low, high):
        grad = jnp.exp(logits - lse_ref[d]) * w_ref[d]
        grad = (grad - jnp.where(row == t_ref[d], w_ref[d], 0.0)).astype(BF)
        if d + 1 < high:
            logits = dense_nt(table, h_ref[d + 1])
        o_ref[...] += dense(grad, h_ref[d])


class Fill:
    def __init__(self, first_row, refs, o_ref, e_ref, held, acc, sem):
        self.first_row, self.o, self.e, self.held, self.acc, self.sem = first_row, o_ref, e_ref, held, acc, sem
        self.table, self.hidden, *self.lines = refs

    def loads(self, d):
        return pltpu.make_async_copy(self.hidden.at[d], self.held.at[d], self.sem.at[d])

    def start(self, tokens=True):
        rows = pl.ds(self.first_row, self.e.shape[0])
        self.load = pltpu.make_async_copy(self.table.at[rows], self.e, self.sem.at[4])
        self.load.start()
        if tokens:
            for d in range(4):
                self.loads(d).start()
        self.acc[...] = jnp.zeros_like(self.acc)

    def groups(self, low, high, tokens=True):
        if low == 0:
            self.load.wait()
        if tokens:
            for d in range(low, high):
                self.loads(d).wait()
        table_terms(
            self.e[...], self.first_row, low, high, self.held, *self.lines, self.acc
        )
        if high == 4:
            self.store = pltpu.make_async_copy(self.acc, self.o, self.sem.at[5])
            self.store.start()

    def finish(self):
        self.store.wait()


def fill_scratch():
    return [
        pltpu.VMEM((FILL, D), BF),
        pltpu.VMEM((4, GROUP, D), BF),
        pltpu.VMEM((FILL, D), F32),
        pltpu.SemaphoreType.DMA((6,)),
    ]


def fill_call(kernel, ins, in_specs, fill, outs, out_specs, scratch, n_sems, cid):
    return pl.pallas_call(
        kernel,
        out_shape=tuple(outs) + (jax.ShapeDtypeStruct((FILL, D), F32),),
        in_specs=in_specs + any_specs(2) + vmem(3),
        out_specs=tuple(out_specs) + tuple(any_specs(1)),
        scratch_shapes=list(scratch) + fill_scratch() + sems(n_sems),
        compiler_params=params(cid, 40),
    )(*ins, *fill)


def fold_fill_kernel(first_row, x_ref, *refs):
    fill_refs, refs = refs[:5], refs[5:]
    o_ref, g_ref, part, sums, got, *fill_held, send, recv = refs
    dp, fs = lax.axis_index("dp"), lax.axis_index("fsdp")
    greet(*line_peers(dp, fs))
    fold = Fold(Link(send, recv), dp, fs, x_ref, part, sums, got)
    fill = Fill(first_row, fill_refs, g_ref, *fill_held)
    fold.start()
    fill.start()
    fold.first()
    fill.groups(0, 1)
    fold.second()
    fill.groups(1, 4)
    fold.finish(o_ref)
    fill.finish()


def sum_tokens_fill(x, fill, first_row, cid):
    return fill_call(
        functools.partial(fold_fill_kernel, first_row),
        (x.reshape(8, TOK, D),),
        vmem(1),
        fill,
        [jax.ShapeDtypeStruct((TOK, D), F32)],
        vmem(1),
        fold_scratch(),
        Fold.slots,
        cid,
    )


GELU_A = (2.0 / jnp.pi) ** 0.5
GELU_B = 0.044715


def gelu_parts(values):
    square = values * values
    bend = jnp.tanh(GELU_A * values * (1.0 + GELU_B * square))
    half = 0.5 * (1.0 + bend)
    slope = half + 0.5 * values * (1.0 - bend * bend) * GELU_A * (1.0 + 3.0 * GELU_B * square)
    return values * half, slope


def two(ref, chip):
    value = ref[pl.ds(2 * chip, 2)]
    return value.reshape(2 * value.shape[1], value.shape[2])


def mlp_kernel(x_ref, w_one, w_two, bias, o_ref, h_ref, u_ref, act_ref, prod, part, sums, got, send, recv):
    dp, fs = lax.axis_index("dp"), lax.axis_index("fsdp")
    chip = fs // 2
    greet(*line_peers(dp, fs))
    link = Link(send, recv)
    spread = Spread(link, dp, fs, x_ref, h_ref)
    fold = Fold(link, dp, fs, prod, part, sums, got)

    def run(k):
        spread.pair[k].wait_recv()
        there = chip ^ k
        pre = dense(two(h_ref, there), w_one[...]) + bias[...]
        act = gelu_parts(pre)[0].astype(BF)
        spot = pl.ds(2 * there, 2)
        u_ref[spot] = pre.reshape(2, TOK, pre.shape[1])
        act_ref[spot] = act.reshape(2, TOK, act.shape[1])
        prod[spot] = dense(act, w_two[...]).astype(BF).reshape(2, TOK, D)

    spread.start()
    run(0)
    spread.forward()
    run(2)
    run(1)
    spread.late()
    run(3)
    fold.start()
    fold.first()
    fold.second()
    fold.finish(o_ref)
    spread.sent()


def mlp_forward(x, w_one, w_two, bias):
    width = w_one.shape[1]
    return pl.pallas_call(
        mlp_kernel,
        out_shape=(
            jax.ShapeDtypeStruct((TOK, D), F32),
            jax.ShapeDtypeStruct((8, TOK, D), BF),
            jax.ShapeDtypeStruct((8, TOK, width), F32),
            jax.ShapeDtypeStruct((8, TOK, width), BF),
        ),
        in_specs=vmem(4),
        out_specs=tuple(vmem(4)),
        scratch_shapes=[pltpu.VMEM((8, TOK, D), BF)]
        + fold_scratch()
        + sems(Fold.slots + Spread.slots),
        compiler_params=params(11, 24),
    )(x, w_one, w_two, bias.reshape(1, width))


def mlp_back_kernel(rows_a, rows_b, x_ref, w_one, w_two, u_ref, act_ref, h_ref, *refs):
    fill_refs, refs = refs[:5], refs[5:]
    o_ref, f_down, g_up, d_bias, g_a, g_b, got_ref, prod, part, sums, got, s_down, r_down, *refs = refs
    e_a, held, acc_a, sem_a, e_b, acc_b, sem_b, send, recv = refs
    dp, fs = lax.axis_index("dp"), lax.axis_index("fsdp")
    plane = [(k, (dp ^ k, fs)) for k in range(1, 4)]
    peers, extra = line_peers(dp, fs)
    greet(peers + [peer for k, peer in plane], extra)
    link = Link(send, recv)
    spread = Spread(link, dp, fs, x_ref, got_ref)
    fold = Fold(link, dp, fs, prod, part, sums, got)
    first = Fill(rows_a, fill_refs, g_a, e_a, held, acc_a, sem_a)
    second = Fill(rows_b, fill_refs, g_b, e_b, held, acc_b, sem_b)
    high = f_down.shape[0]

    def lines(who):
        return pl.ds(pl.multiple_of(who * high, 16), high)

    side = [link.copy(s_down.at[lines(dp ^ k)], r_down.at[k - 1], peer) for k, peer in plane]
    spread.start()
    first.start()
    second.start(False)
    first.groups(0, 1)
    spread.forward()
    first.groups(1, 3)
    spread.late()
    first.groups(3, 4)
    spread.finish()
    width = w_one.shape[1]
    cotangent = got_ref[...].reshape(GROUP, D)
    d_act = dense_nt(cotangent, w_two[...])
    d_pre = d_act * gelu_parts(u_ref[...].reshape(GROUP, width))[1]
    d_low = d_pre.astype(BF)
    prod[...] = dense_nt(d_low, w_one[...]).astype(BF).reshape(8, TOK, D)
    fold.start()
    d_bias[...] = jnp.sum(d_pre, axis=0, keepdims=True)
    s_down[...] = dense_tn(act_ref[...].reshape(GROUP, width), cotangent).astype(BF)
    fold.first()
    for copy in side:
        copy.start()
    g_up[...] = dense_tn(h_ref[...].reshape(GROUP, D), d_low).astype(BF)
    fold.second()
    second.groups(0, 4, False)
    for copy in side:
        copy.wait()
    f_down[...] = add_up(s_down[lines(dp), :], [r_down[j] for j in range(3)]).astype(BF)
    fold.finish(o_ref)
    first.finish()
    second.finish()


def mlp_backward(x, w_one, w_two, pre_act, act_low, normed, fill, rows_a, rows_b, cid):
    width = w_one.shape[1]
    high = w_two.shape[0] // 4
    block = jax.ShapeDtypeStruct((FILL, D), F32)
    extra = fill_scratch()
    return pl.pallas_call(
        functools.partial(mlp_back_kernel, rows_a, rows_b),
        out_shape=(
            jax.ShapeDtypeStruct((TOK, D), F32),
            jax.ShapeDtypeStruct((high, D), BF),
            jax.ShapeDtypeStruct((D, width), BF),
            jax.ShapeDtypeStruct((1, width), F32),
            block,
            block,
        ),
        in_specs=vmem(6) + any_specs(2) + vmem(3),
        out_specs=tuple(vmem(4) + any_specs(2)),
        scratch_shapes=[pltpu.VMEM((8, TOK, D), BF)] * 2
        + fold_scratch()
        + [pltpu.VMEM(w_two.shape, BF), pltpu.VMEM((3, high, D), BF)]
        + extra
        + [extra[0], extra[2], extra[3]]
        + sems(Spread.slots + Fold.slots + 3),
        compiler_params=params(cid, 48),
    )(x, w_one, w_two, pre_act, act_low, normed, *fill)


def spread_last_kernel(first_row, x_ref, g_qkv, g_out, g_down, *refs):
    fill_refs, refs = refs[:5], refs[5:]
    o_ref, side_any, s_qkv, s_out, o_down, g_ref, p_qkv, p_out, keep, *fill_held, send, recv = refs
    dp, fs = lax.axis_index("dp"), lax.axis_index("fsdp")
    core, chip, pair = fs % 2, fs // 2, (dp, fs ^ 1)
    peers, extra = line_peers(dp, fs)
    greet(peers + [(dp ^ k, fs) for k in (1, 2, 3)], extra)
    link = Link(send, recv)
    spread = Spread(link, dp, fs, x_ref, o_ref)
    fill = Fill(first_row, fill_refs, g_ref, *fill_held)
    both = ((g_qkv, s_qkv, p_qkv), (g_out, s_out, p_out))
    swap = [link.copy(g.at[:, 1 - core], p, pair) for g, s, p in both]
    mine = [pltpu.make_async_copy(g.at[:, core], s, keep.at[i]) for i, (g, s, p) in enumerate(both)]
    sides = {
        k: [
            link.copy(
                x_ref if k == 0 else o_ref.at[fs ^ k],
                side_any.at[j - 1, chip ^ (k // 2)],
                (dp ^ j, fs),
            )
            for j in (1, 2)
        ]
        for k in (0, 2, 4, 6)
    }

    high = g_down.shape[0]
    home = o_down.at[pl.ds(pl.multiple_of(dp * high, 16), high)]
    back = [link.copy(g_down, home, (dp ^ k, fs)) for k in (1, 2, 3)]
    back.append(pltpu.make_async_copy(g_down, home, keep.at[2]))

    def after(k):
        for copy in sides[k]:
            copy.start()

    spread.start()
    after(0)
    for copy in back + swap + mine:
        copy.start()
    fill.start()
    fill.groups(0, 1)
    spread.forward(after)
    fill.groups(1, 3)
    spread.late(after)
    for copy in swap + mine:
        copy.wait()
    for g, s, p in both:
        for j in range(4):
            s[j] = add_up(s[j], [p[j]]).astype(BF)
    fill.groups(3, 4)
    for copy in back:
        copy.wait()
    spread.finish()
    for k in (0, 2, 4, 6):
        for copy in sides[k]:
            copy.wait()
    fill.finish()


def gather_tokens_last(x, g_qkv, g_out, g_down, fill, first_row, cid):
    high = D // 8
    halves = [(4, high, 3 * D), (4, high, D)]
    return fill_call(
        functools.partial(spread_last_kernel, first_row),
        (x, g_qkv.reshape(4, 2, high, 3 * D), g_out.reshape(4, 2, high, D), g_down),
        vmem(1) + any_specs(2) + vmem(1),
        fill,
        [jax.ShapeDtypeStruct((8, TOK, D), BF), jax.ShapeDtypeStruct((2, 4, TOK, D), BF)]
        + [jax.ShapeDtypeStruct(h, BF) for h in halves]
        + [jax.ShapeDtypeStruct((FF // 8, D), BF)],
        vmem(1) + any_specs(1) + vmem(2) + any_specs(1),
        [pltpu.VMEM(h, BF) for h in halves] + [pltpu.SemaphoreType.DMA((3,))],
        Spread.slots + 2 + 8 + 3,
        cid,
    )


def start_kernel(
    look, wqo, zq, zs, zo, small, pos, e_out, wqo_out, w1_out, small_out, pos_out, part, sums, got, send, recv
):
    dp, fs = lax.axis_index("dp"), lax.axis_index("fsdp")
    chip, core, pair = fs // 2, fs % 2, (dp, fs ^ 1)
    line = [(dp, fs ^ k) for k in range(1, 8)]
    plane = [(dp ^ k, fs) for k in range(1, 4)]
    greet(line + plane)
    link = Link(send, recv)
    fold = Fold(link, dp, fs, look, part, sums, got)
    fold.start()
    spot = quarter_of(dp, wqo_out.shape)
    side = {
        k: [
            link.copy(zq.at[chip ^ (k // 2)], wqo_out.at[(fs ^ k,) + spot], peer)
            for peer in plane
        ]
        for k in (2, 4, 6)
    }
    for k in (2, 4, 6):
        for copy in side[k]:
            copy.start()
    wqo_out[fs] = wqo[...]
    pairs = [link.copy(wqo, wqo_out.at[fs], pair)]
    pairs[0].start()
    strips = [
        link.copy(zs, w1_out.at[pl.ds(2 * dp, 2)], (dp ^ k, fs)) for k in range(1, 4)
    ]
    source = chip == dp

    @pl.when(jnp.logical_not(source))
    def _():
        for copy in strips:
            copy.start()

    w1_out[pl.ds(2 * dp, 2)] = zs[...]
    w1_out[pl.ds(2 * chip, 2)] = zo[...]
    fold.first()
    high = pos.shape[0] // 4
    rows = pl.ds(pl.multiple_of(dp * high, 16), high)
    land = link.used
    pos_line = [
        link.copy(pos_out.at[rows], pos_out.at[rows], (dp, k), land) for k in (2, 4, 6)
    ]
    pos_side = [link.copy(pos_out.at[rows], pos_out.at[rows], peer) for peer in plane]
    pos_pair = link.copy(pos_out, pos_out, pair)

    @pl.when(fs == 0)
    def _():
        pos_out[rows] = pos[rows]
        for copy in pos_line:
            copy.start()

    tiny = Spread(link, dp, fs, small, small_out)
    tiny.start()
    for k in (2, 4, 6):
        wqo_out[(fs ^ k,) + spot] = zq[chip ^ (k // 2)]

    fold.second()

    @pl.when(core == 0)
    def _():
        @pl.when(fs != 0)
        def _():
            pos_line[0].wait_recv()

        for copy in pos_side:
            copy.start()

    tiny.forward()
    fold.finish(e_out)

    @pl.when(core == 0)
    def _():
        for copy in pos_side:
            copy.wait()
        pos_pair.start()

    tiny.late()
    tiny.finish()
    for k in (2, 4, 6):
        for copy in side[k]:
            copy.wait_recv()
        copy = link.copy(wqo_out.at[fs ^ k], wqo_out.at[fs ^ k], pair)
        copy.start()
        pairs.append(copy)
    for copy in pairs:
        copy.wait()
    for k in (2, 4, 6):
        for copy in side[k]:
            copy.wait_send()

    @pl.when(jnp.logical_not(source))
    def _():
        for copy in strips:
            copy.wait_send()

    for k, copy in zip(range(1, 4), strips):

        @pl.when(chip != (dp ^ k))
        def _():
            copy.wait_recv()

    @pl.when(core == 0)
    def _():
        pos_pair.wait_send()

    @pl.when(core == 1)
    def _():
        pos_pair.wait_recv()

    @pl.when(fs == 0)
    def _():
        for copy in pos_line:
            copy.wait_send()


def start_exchange(looked, wqo, zq, zs, zo, small, pos):
    n_sems = Fold.slots + 9 + 4 + 3 + 7 + Spread.slots
    return pl.pallas_call(
        start_kernel,
        out_shape=(
            jax.ShapeDtypeStruct((TOK, D), F32),
            jax.ShapeDtypeStruct((8,) + wqo.shape, BF),
            jax.ShapeDtypeStruct((8,) + zs.shape[1:], BF),
            jax.ShapeDtypeStruct((8,) + small.shape, BF),
            jax.ShapeDtypeStruct(pos.shape, BF),
        ),
        in_specs=vmem(7),
        out_specs=tuple(vmem(5)),
        scratch_shapes=fold_scratch() + sems(n_sems),
        compiler_params=params(4, 20),
    )(looked.reshape(8, TOK, D), wqo, zq, zs, zo, small, pos)


def lse_kernel(st_ref, lse_ref, hit_ref, mine, got, both, send, recv):
    dp, fs = lax.axis_index("dp"), lax.axis_index("fsdp")
    line = [(dp, fs ^ k) for k in range(1, 8)]
    plane = [(dp ^ k, fs) for k in range(1, 4)]
    greet(line + plane)
    link = Link(send, recv)
    blocks = st_ref.shape[0]
    top = st_ref[0, 0:1, :]
    for b in range(1, blocks):
        top = jnp.maximum(top, st_ref[b, 0:1, :])
    total = jnp.zeros_like(top)
    hit = jnp.zeros_like(top)
    for b in range(blocks):
        total = total + st_ref[b, 1:2, :] * jnp.exp(st_ref[b, 0:1, :] - top)
        hit = hit + st_ref[b, 2:3, :]
    for j in range(8):
        lanes = slice(j * TOK, (j + 1) * TOK)
        mine[j : j + 1, :] = top[:, lanes]
        mine[8 + j : 9 + j, :] = total[:, lanes]
        mine[16 + j : 17 + j, :] = hit[:, lanes]
    first = [link.copy(mine, got.at[fs], peer) for peer in line]
    for copy in first:
        copy.start()
    got[fs] = mine[...]
    for copy in first:
        copy.wait()
    top = got[0, 0:8, :]
    for j in range(1, 8):
        top = jnp.maximum(top, got[j, 0:8, :])
    total = jnp.zeros_like(top)
    hit = jnp.zeros_like(top)
    for j in range(8):
        total = total + got[j, 8:16, :] * jnp.exp(got[j, 0:8, :] - top)
        hit = hit + got[j, 16:24, :]
    both[dp, 0:8, :] = top + jnp.log(total)
    both[dp, 8:16, :] = hit
    second = [link.copy(both.at[dp], both.at[dp], peer) for peer in plane]
    for copy in second:
        copy.start()
    for copy in second:
        copy.wait()
    for d in range(4):
        for j in range(8):
            lanes = slice(j * TOK, (j + 1) * TOK)
            lse_ref[d, :, lanes] = both[d, j : j + 1, :]
            hit_ref[d, :, lanes] = both[d, 8 + j : 9 + j, :]


def combine_stats(stats):
    return pl.pallas_call(
        lse_kernel,
        out_shape=(jax.ShapeDtypeStruct((4, 1, GROUP), F32),) * 2,
        in_specs=vmem(1),
        out_specs=tuple(vmem(2)),
        scratch_shapes=[
            pltpu.VMEM((24, TOK), F32),
            pltpu.VMEM((8, 24, TOK), F32),
            pltpu.VMEM((4, 16, TOK), F32),
        ]
        + sems(10),
        compiler_params=params(5, 8),
    )(stats)


def logits_kernel(
    rows_here,
    x_ref,
    e_ref,
    t_ref,
    p_ref,
    st_ref,
    table_any,
    h_any,
    o_any,
    held,
    tab,
    keep,
    send,
    recv,
):
    turn, block = pl.program_id(0), pl.program_id(1)
    last = pl.num_programs(1) - 1
    dp, fs = lax.axis_index("dp"), lax.axis_index("fsdp")
    chip, core, pair = fs // 2, fs % 2, (dp, fs ^ 1)
    link = Link(send, recv)
    spread = Spread(link, dp, fs, x_ref, held)
    sides = {
        k: [
            link.copy(
                x_ref if k == 0 else held.at[fs ^ k],
                o_any.at[side - 1, chip ^ (k // 2), core],
                (dp ^ side, fs),
            )
            for side in (1, 2)
        ]
        for k in (0, 2, 4, 6)
    }
    pairs = [link.copy(o_any.at[k, :, core], o_any.at[k, :, core], pair) for k in range(2)]
    keep_table = pltpu.make_async_copy(tab, table_any, keep.at[0])
    keep_held = pltpu.make_async_copy(held, h_any, keep.at[1])

    def after(k):
        for copy in sides[k]:
            copy.start()

    def at(i, b):
        return pl.when((turn == i) & (block == b))

    @at(0, 0)
    def _():
        peers, extra = line_peers(dp, fs)
        greet(peers + [(dp ^ 1, fs), (dp ^ 2, fs)], extra)
        spread.start()
        after(0)
        spread.pair[0].wait_recv()

    @at(0, last)
    def _():
        spread.forward(after)

    @at(1, 0)
    def _():
        spread.pair[1].wait_recv()
        keep_table.start()

    @at(1, last - 1)
    def _():
        spread.late(after)

    @at(2, 0)
    def _():
        spread.pair[2].wait_recv()

    @at(3, 0)
    def _():
        spread.pair[3].wait_recv()
        keep_held.start()

    rows = pl.ds(pl.multiple_of(block * VBLK, 16), VBLK)

    @pl.when(turn == 0)
    def _():
        line = lax.broadcasted_iota(jnp.int32, (VBLK, 1), 0) + block * VBLK
        tab[rows, :] = jnp.where(line < rows_here, e_ref[...], 0.0).astype(BF)

    there = chip ^ turn
    lanes = pl.ds(pl.multiple_of(there * 2 * TOK, 2 * TOK), 2 * TOK)
    tokens = two(held, there)
    wanted = t_ref[dp, :, lanes]
    high = VBLK // 2
    starts = [block * VBLK + half * high for half in range(2)]
    both = [
        dense_nt(tab[pl.ds(pl.multiple_of(start, 16), high), :], tokens) for start in starts
    ]
    for half, (start, logits) in enumerate(zip(starts, both)):
        row = lax.broadcasted_iota(jnp.int32, logits.shape, 0) + start
        logits = jnp.where(row < rows_here, logits, -jnp.inf)
        top = jnp.max(logits, 0, keepdims=True)
        hit = jnp.where(row == wanted, logits, 0.0)
        grown = jnp.exp(logits - top)
        st_ref[2 * block + half, 0:1, lanes] = top
        st_ref[2 * block + half, 1:2, lanes] = jnp.sum(grown, 0, keepdims=True)
        st_ref[2 * block + half, 2:3, lanes] = jnp.sum(hit, 0, keepdims=True)
        p_ref[0, half * high : (half + 1) * high, :] = grown.astype(BF)

    @at(3, last)
    def _():
        for side, copy in enumerate(pairs):
            for k in (0, 2, 4, 6):
                sides[k][side].wait_recv()
            copy.start()
        for copy in pairs + [keep_table, keep_held]:
            copy.wait()
        for k in (0, 2, 4, 6):
            for copy in sides[k]:
                copy.wait_send()
        spread.sent()


def own_logits(embed, hidden, target):
    rows_here = embed.shape[0]
    blocks = pl.cdiv(rows_here, VBLK)
    return pl.pallas_call(
        functools.partial(logits_kernel, rows_here),
        grid=(4, blocks),
        in_specs=[
            pl.BlockSpec((TOK, D), lambda i, j: (0, 0)),
            pl.BlockSpec((VBLK, D), lambda i, j: (jnp.where(i == 0, j, blocks - 1), 0)),
            pl.BlockSpec((4, 1, GROUP), lambda i, j: (0, 0, 0)),
        ],
        out_specs=[
            pl.BlockSpec((1, VBLK, 2 * TOK), lambda i, j: (i, j, 0)),
            pl.BlockSpec((2 * blocks, 8, GROUP), lambda i, j: (0, 0, 0)),
        ]
        + any_specs(3),
        out_shape=[
            jax.ShapeDtypeStruct((4, blocks * VBLK, 2 * TOK), BF),
            jax.ShapeDtypeStruct((2 * blocks, 8, GROUP), F32),
            jax.ShapeDtypeStruct((blocks * VBLK, D), BF),
            jax.ShapeDtypeStruct((8, TOK, D), BF),
            jax.ShapeDtypeStruct((2, 4, 2, TOK, D), BF),
        ],
        scratch_shapes=[
            pltpu.VMEM((8, TOK, D), BF),
            pltpu.VMEM((blocks * VBLK, D), BF),
            pltpu.SemaphoreType.DMA((2,)),
        ]
        + sems(Spread.slots + 8 + 2),
        compiler_params=params(7, 40),
    )(hidden, embed, target)


def dhf_kernel(
    p_ref, st_ref, lse_ref, w_ref, t_ref, e_ref, own_any, near_any, o_ref, o_any, acc, held, keep, send, recv
):
    block = pl.program_id(0)
    last = pl.num_programs(0) - 1
    dp, fs = lax.axis_index("dp"), lax.axis_index("fsdp")
    core, pair = fs % 2, (dp, fs ^ 1)
    link = Link(send, recv)
    halves = [
        link.copy(
            near_any.at[2 - k, pl.ds((2 - k) * 2, 2), core],
            held.at[dp ^ (3 - k), pl.ds((2 - k) * 2, 2), core],
            (dp ^ k, fs),
        )
        for k in (1, 2)
    ]
    share = link.copy(held.at[dp ^ 3, :, core], held.at[dp ^ 3, :, core], pair)
    mine = [
        pltpu.make_async_copy(own_any, held.at[dp], keep.at[0]),
        pltpu.make_async_copy(near_any.at[0], held.at[dp ^ 1], keep.at[1]),
        pltpu.make_async_copy(near_any.at[1], held.at[dp ^ 2], keep.at[2]),
    ]
    home = [
        pltpu.make_async_copy(held.at[dp ^ k], o_any.at[dp ^ k], keep.at[3 + k]) for k in range(4)
    ]

    @pl.when(block == 0)
    def _():
        greet([(dp ^ 1, fs), (dp ^ 2, fs), pair])
        for copy in halves + mine:
            copy.start()

    spans = [
        pl.ds(pl.multiple_of((fs // 2 ^ k) * 2 * TOK, 2 * TOK), 2 * TOK) for k in range(4)
    ]

    def lined(pick):
        return jnp.concatenate([pick(span) for span in spans], axis=1)

    weight = lined(lambda span: w_ref[dp, :, span])
    wanted = lined(lambda span: t_ref[dp, :, span])
    lse = lined(lambda span: lse_ref[dp, :, span])
    grown = jnp.concatenate([p_ref[k] for k in range(4)], axis=1).astype(F32)
    row = lax.broadcasted_iota(jnp.int32, grown.shape, 0) + block * VBLK
    high = VBLK // 2
    scaled = []
    for half in range(2):
        factor = weight * jnp.exp(lined(lambda span: st_ref[half, 0:1, span]) - lse)
        scaled.append(grown[half * high : (half + 1) * high, :] * factor)
    grad = jnp.concatenate(scaled, axis=0) - jnp.where(row == wanted, weight, 0.0)
    grad = grad.astype(BF)

    @pl.when(block == 1)
    def _():
        for copy in mine:
            copy.wait()
        for copy in home[:3]:
            copy.start()

    @pl.when(block == 0)
    def _():
        acc[...] = dense_tn(grad, e_ref[...])

    @pl.when(block > 0)
    def _():
        acc[...] += dense_tn(grad, e_ref[...])

    @pl.when(block == last)
    def _():
        for copy in halves:
            copy.wait_recv()
        share.start()
        for k, span in enumerate(spans):
            o_ref[span, :] = acc[k * 2 * TOK : (k + 1) * 2 * TOK, :].astype(BF)
        share.wait()
        home[3].start()
        for copy in halves:
            copy.wait_send()
        for copy in home:
            copy.wait()


def final_cotangent(grown, stats, lse, weight, target, table, own, near):
    blocks = table.shape[0] // VBLK
    line = pl.BlockSpec((4, 1, GROUP), lambda i: (0, 0, 0))
    return pl.pallas_call(
        dhf_kernel,
        grid=(blocks,),
        in_specs=[
            pl.BlockSpec((4, VBLK, 2 * TOK), lambda i: (0, i, 0)),
            pl.BlockSpec((2, 8, GROUP), lambda i: (i, 0, 0)),
            line,
            line,
            line,
            pl.BlockSpec((VBLK, D), lambda i: (i, 0)),
        ]
        + any_specs(2),
        out_specs=[pl.BlockSpec((GROUP, D), lambda i: (0, 0))] + any_specs(1),
        out_shape=[
            jax.ShapeDtypeStruct((GROUP, D), BF),
            jax.ShapeDtypeStruct((4, 4, 2, TOK, D), BF),
        ],
        scratch_shapes=[
            pltpu.VMEM((GROUP, D), F32),
            pltpu.VMEM((4, 4, 2, TOK, D), BF),
            pltpu.SemaphoreType.DMA((7,)),
        ]
        + sems(3),
        compiler_params=params(8, 48),
    )(grown, stats, lse, weight, target, table, own.reshape(4, 2, TOK, D), near)


def table_kernel(
    e_ref,
    h_ref,
    lse_ref,
    w_ref,
    t_ref,
    d_own,
    d_near,
    g_qkv,
    g_out,
    g_up,
    g_maps,
    *refs,
):
    vectors, refs = refs[:10], refs[10:]
    (
        o_ref,
        d_all,
        o_qkv,
        o_out,
        o_up,
        o_maps,
        o_vec,
        s_qkv,
        s_out,
        t_qkv,
        t_out,
        r_qkv,
        r_out,
        q_qkv,
        q_out,
        s_up,
        r_up,
        z_qkv,
        z_out,
        f_qkv,
        f_out,
        f_up,
        b_maps,
        r_maps,
        f_maps,
        b_vec,
        r_vec,
        f_vec,
        d_held,
        g_vec,
        local,
        send,
        recv,
    ) = refs
    block, half = pl.program_id(0), pl.program_id(1)
    step = block * 2 + half
    last = pl.num_programs(0) * 2 - 1
    dp, fs = lax.axis_index("dp"), lax.axis_index("fsdp")
    core, chip, pair = fs % 2, fs // 2, (dp, fs ^ 1)
    line = [(k, (dp, fs ^ k)) for k in range(1, 8)]
    plane = [(k, (dp ^ k, fs)) for k in range(1, 4)]
    chips = [(k, (dp, fs ^ (2 * k))) for k in range(1, 4)]
    link = Link(send, recv)
    spots = iter(range(64))

    def here(src, dst):
        return pltpu.make_async_copy(src, dst, local.at[next(spots)])

    def quarter(who, shape):
        high, wide = shape[-2] // 2, shape[-1] // 2
        return (
            pl.ds(pl.multiple_of((who // 2) * high, 16), high),
            pl.ds(pl.multiple_of((who % 2) * wide, 128), wide),
        )

    def strip(who):
        width = g_up.shape[2]
        return pl.ds(pl.multiple_of(who * width, 128), width)

    keep_d = [
        here(d_own, d_held.at[dp]),
        here(d_near.at[0], d_held.at[dp ^ 1, :, core]),
        here(d_near.at[1], d_held.at[dp ^ 2, :, core]),
    ]
    d_home = [here(d_held.at[dp ^ k], d_all.at[dp ^ k]) for k in range(4)]
    d_half = [
        link.copy(
            d_near.at[2 - k, pl.ds((2 - k) * 2, 2)],
            d_held.at[dp ^ (3 - k), pl.ds((2 - k) * 2, 2), core],
            (dp ^ k, fs),
        )
        for k in (1, 2)
    ]
    d_pair = [
        link.copy(d_near.at[0], d_held.at[dp ^ 1, :, core], pair),
        link.copy(d_near.at[1], d_held.at[dp ^ 2, :, core], pair),
    ]
    d_last = link.copy(d_held.at[dp ^ 3, :, core], d_held.at[dp ^ 3, :, core], pair)
    big = (
        (g_qkv, s_qkv, t_qkv, r_qkv, q_qkv, z_qkv, f_qkv, o_qkv),
        (g_out, s_out, t_out, r_out, q_out, z_out, f_out, o_out),
    )

    def slab(g, who, part):
        return g.at[(pl.ds(2 * part, 2),) + quarter(who, g.shape)]

    keep_big = []
    big_first = []
    big_second = []
    for g, s, t, r, q, *_ in big:
        for part in range(2):
            turn, other = (1, 2) if part == 0 else (2, 1)
            keep_big.append(here(slab(g, dp, part), s.at[pl.ds(2 * part, 2)]))
            keep_big.append(here(slab(g, dp ^ other, part), t.at[part]))
            big_first.append(link.copy(slab(g, dp ^ 3, part), r.at[part, 1], (dp ^ turn, fs)))
            big_first.append(link.copy(slab(g, dp ^ turn, part), r.at[part, 0], (dp ^ turn, fs)))
            big_second.append(link.copy(t.at[part], q.at[part], (dp ^ other, fs)))
    big_line = [
        link.copy(s.at[chip ^ k], z.at[k - 1], peer)
        for g, s, t, r, q, z, *_ in big
        for k, peer in chips
    ]
    big_back = [
        link.copy(f, o.at[quarter(dp, o.shape)], peer)
        for g, s, t, r, q, z, f, o in big
        for k, peer in plane
    ]
    big_home = [here(f, o.at[quarter(dp, o.shape)]) for g, s, t, r, q, z, f, o in big]
    keep_up = here(g_up.at[fs], s_up.at[:, strip(fs)])
    up_line = [link.copy(g_up.at[fs ^ k], s_up.at[:, strip(fs)], peer) for k, peer in line]
    up_side = [
        link.copy(s_up.at[quarter(dp ^ k, s_up.shape)], r_up.at[k - 1], peer) for k, peer in plane
    ]
    up_back = [link.copy(f_up, o_up.at[quarter(dp, s_up.shape)], peer) for k, peer in plane]
    up_home = here(f_up, o_up.at[quarter(dp, s_up.shape)])
    keep_maps = here(g_maps.at[fs], b_maps.at[fs])
    maps_line = [link.copy(g_maps.at[fs ^ k], b_maps.at[fs], peer) for k, peer in line]
    maps_side = [link.copy(r_maps.at[dp], r_maps.at[dp], peer) for k, peer in plane]
    maps_back = [link.copy(f_maps, o_maps.at[fs], peer) for k, peer in line]
    maps_home = here(f_maps, o_maps.at[fs])
    keep_vec = here(g_vec, b_vec.at[fs])
    vec_line = [link.copy(g_vec, b_vec.at[fs], peer) for k, peer in line]
    vec_side = [link.copy(r_vec.at[dp], r_vec.at[dp], peer) for k, peer in plane]
    vec_home = here(f_vec, o_vec)

    @pl.when(step == 0)
    def _():
        greet([peer for k, peer in line + plane])
        for copy in big_first + up_line + maps_line + d_pair:
            copy.start()
        g_vec[...] = jnp.zeros_like(g_vec)
        for i in range(6):
            g_vec[i : i + 1, :] = vectors[i][...]
        for i in range(3):
            g_vec[6 + i : 7 + i, :] = vectors[6][:, i * D : (i + 1) * D]
        g_vec[9:10, :] = vectors[7][...]
        width = vectors[8].shape[1]
        for i in range(8):

            @pl.when(fs == i)
            def _():
                first = i * width
                lanes = slice(first % D, first % D + width)
                g_vec[10 + first // D : 11 + first // D, lanes] = vectors[8][...]

        g_vec[14:15, :] = vectors[9][...]
        for copy in vec_line:
            copy.start()
        for copy in keep_d + keep_big + [keep_up, keep_maps, keep_vec]:
            copy.start()

    @pl.when(step == 3)
    def _():
        for copy in keep_big + big_first:
            copy.wait()
        for g, s, t, r, *_ in big:
            for part in range(2):
                t[part] = add_up(t[part], [r[part, 1]]).astype(BF)
        for copy in big_second:
            copy.start()

    @pl.when(step == 4)
    def _():
        for copy in big_second:
            copy.wait()
        for g, s, t, r, q, *_ in big:
            for part in range(2):
                for j in range(2):
                    s[2 * part + j] = add_up(
                        s[2 * part + j], [r[part, 0, j], q[part, j]]
                    ).astype(BF)
        for copy in big_line + d_half:
            copy.start()
        for copy in d_pair + keep_d:
            copy.wait()
        for copy in d_home[:3]:
            copy.start()

    @pl.when(step == 5)
    def _():
        for copy in up_line + [keep_up]:
            copy.wait()
        for copy in up_side:
            copy.start()
        for copy in vec_line + maps_line + [keep_vec, keep_maps]:
            copy.wait()
        r_vec[dp] = add_up(b_vec[0], [b_vec[j] for j in range(1, 8)])
        r_maps[dp] = add_up(b_maps[0], [b_maps[j] for j in range(1, 8)])
        for copy in vec_side + maps_side:
            copy.start()

    @pl.when(step == 6)
    def _():
        for copy in d_half:
            copy.wait()
        d_last.start()

    @pl.when(step == 7)
    def _():
        for copy in up_side:
            copy.wait()
        f_up[...] = add_up(
            s_up[quarter(dp, s_up.shape)], [r_up[j] for j in range(3)]
        ).astype(BF)
        for copy in up_back + [up_home]:
            copy.start()
        for copy in maps_side + vec_side:
            copy.wait()
        f_maps[...] = add_up(r_maps[0], [r_maps[j] for j in range(1, 4)]).astype(BF)
        f_vec[...] = add_up(r_vec[0], [r_vec[j] for j in range(1, 4)])
        for copy in maps_back + [maps_home, vec_home]:
            copy.start()
        d_last.wait()
        d_home[3].start()

    @pl.when(step == 8)
    def _():
        for copy in big_line:
            copy.wait()
        for g, s, t, r, q, z, f, o in big:
            f[...] = add_up(s[chip], [z[i] for i in range(3)]).astype(BF)
        for copy in big_back + big_home:
            copy.start()

    @pl.when(half == 0)
    def _():
        o_ref[...] = jnp.zeros_like(o_ref)

    for part in range(2):

        @pl.when(half == part)
        def _():
            table_terms(
                e_ref[...],
                block * TBLK,
                part * 2,
                part * 2 + 2,
                h_ref,
                lse_ref,
                w_ref,
                t_ref,
                o_ref,
            )

    @pl.when(step == last)
    def _():
        for copy in d_home:
            copy.wait()
        for copy in big_back + big_home + up_back + maps_back:
            copy.wait()
        for copy in [up_home, maps_home, vec_home]:
            copy.wait()


def table_gradient(rows, table, tokens, d_own, d_near, g_qkv, g_out, g_up, g_maps, vectors):
    line = pl.BlockSpec((4, 1, GROUP), lambda i, j: (0, 0, 0))
    high = D // 8

    def like(*shape, dtype=BF):
        return pltpu.VMEM(shape, dtype)

    def quarters(width):
        return (high // 2, width // 2)

    return pl.pallas_call(
        table_kernel,
        grid=(rows // TBLK, 2),
        in_specs=[
            pl.BlockSpec((TBLK, D), lambda i, j: (i, 0)),
            pl.BlockSpec((4, GROUP, D), lambda i, j: (0, 0, 0)),
            line,
            line,
            line,
        ]
        + any_specs(6)
        + [pl.BlockSpec(v.shape, lambda i, j: (0, 0)) for v in vectors],
        out_specs=[pl.BlockSpec((TBLK, D), lambda i, j: (i, 0))] + any_specs(6),
        out_shape=[
            jax.ShapeDtypeStruct((rows, D), F32),
            jax.ShapeDtypeStruct((4, 4, 2, TOK, D), BF),
            jax.ShapeDtypeStruct((high, 3 * D), BF),
            jax.ShapeDtypeStruct((high, D), BF),
            jax.ShapeDtypeStruct((high, FF), BF),
            jax.ShapeDtypeStruct((8, 2 * HD // 8, D), BF),
            jax.ShapeDtypeStruct((16, D), F32),
        ],
        scratch_shapes=[
            like(4, *quarters(3 * D)),
            like(4, *quarters(D)),
            like(2, 2, *quarters(3 * D)),
            like(2, 2, *quarters(D)),
            like(2, 2, 2, *quarters(3 * D)),
            like(2, 2, 2, *quarters(D)),
            like(2, 2, *quarters(3 * D)),
            like(2, 2, *quarters(D)),
            like(high, FF),
            like(3, *quarters(FF)),
            like(3, *quarters(3 * D)),
            like(3, *quarters(D)),
            like(*quarters(3 * D)),
            like(*quarters(D)),
            like(*quarters(FF)),
            like(8, 16, D),
            like(4, 16, D, dtype=F32),
            like(16, D),
            like(8, 16, D, dtype=F32),
            like(4, 16, D, dtype=F32),
            like(16, D, dtype=F32),
            like(4, 4, 2, TOK, D),
            like(16, D, dtype=F32),
            pltpu.SemaphoreType.DMA((24,)),
        ]
        + sems(72),
        compiler_params=params(9, 58),
    )(
        table,
        *tokens,
        d_own.reshape(4, 2, TOK, D),
        d_near,
        g_qkv,
        g_out,
        g_up.reshape(8, high, FF // 8),
        g_maps,
        *vectors,
    )


def lane_sum(value):
    rows, lanes = value.shape[0] // 8, value.shape[1] // TOK
    total = None
    for i in range(rows):
        for j in range(lanes):
            tile = value[i * 8 : (i + 1) * 8, j * TOK : (j + 1) * TOK]
            total = tile if total is None else total + tile
    return total


def square_rows(ref, rows, step):
    def one(i, carry):
        part = ref[pl.ds(pl.multiple_of(i * step, step), step), :].astype(F32)
        return carry + lane_sum(part * part)

    return lax.fori_loop(0, rows // step, one, jnp.zeros((8, TOK), F32))


def scatter_kernel(n_pieces, count_ref, list_ref, d_any, *refs):
    pieces, refs = refs[:n_pieces], refs[n_pieces:]
    mats, small, refs = refs[:4], refs[4:6], refs[6:]
    g_any, pos_ref, sq_ref, held, d_low, d_wide, out, sem = refs
    rows_here = g_any.shape[0]
    first_dev = (lax.axis_index("fsdp") == 0).astype(F32)
    fetch = pltpu.make_async_copy(d_any, d_low, sem.at[n_pieces])
    fetch.start()
    loads, first = [], 0
    for i, piece in enumerate(pieces):
        size = min(piece.shape[0], rows_here - first)
        loads.append(
            pltpu.make_async_copy(piece.at[pl.ds(0, size)], held.at[pl.ds(first, size)], sem.at[i])
        )
        first = first + size
    for load in loads:
        load.start()
    total = jnp.zeros((8, TOK), F32)
    for mat in mats:
        total = total + square_rows(mat, mat.shape[0], 16)
    for part in small:
        total = total + square_rows(part, part.shape[0], 16) * first_dev
    fetch.wait()
    pos_ref[...] = jnp.zeros_like(pos_ref)
    chunk = 64

    def widen(i, carry):
        spot = pl.ds(pl.multiple_of(i * chunk, chunk), chunk)
        wide = d_low[spot, :].astype(F32)
        d_wide[spot, :] = wide
        there = pl.ds(pl.multiple_of((i % (TOK // chunk)) * chunk, chunk), chunk)
        pos_ref[there, :] += wide
        return carry

    lax.fori_loop(0, d_low.shape[0] // chunk, widen, 0)
    pos_ref[...] = pos_ref[...] * first_dev
    total = total + square_rows(pos_ref, TOK, 16)
    for load in loads:
        load.wait()

    def several(i, carry):
        for j in range(8):
            entry = list_ref[i * 8 + j]
            row, token = lax.shift_right_logical(entry, 12), entry & 4095
            held[pl.ds(row, 1), :] += d_wide[pl.ds(token, 1), :]
        return carry

    lax.fori_loop(0, (count_ref[0] + 7) // 8, several, 0)
    step = 48
    parts = 3
    part_rows = rows_here // parts

    for k in range(parts):

        def low(i, carry, k=k):
            spot = pl.ds(pl.multiple_of(k * part_rows + i * step, 16), step)
            value = held[spot, :].astype(BF)
            out[spot, :] = value
            value = value.astype(F32)
            return carry + lane_sum(value * value)

        total = lax.fori_loop(0, part_rows // step, low, total)
        if part_rows % step:
            rest = part_rows % step
            spot = pl.ds(k * part_rows + part_rows - rest, rest)
            value = held[spot, :].astype(BF)
            out[spot, :] = value
            value = value.astype(F32)
            total = total + lane_sum(value * value)
        spot = pl.ds(k * part_rows, part_rows)
        pltpu.make_async_copy(out.at[spot], g_any.at[spot], sem.at[n_pieces + 1 + k]).start()
    sq_ref[...] = total
    for k in range(parts):
        spot = pl.ds(k * part_rows, part_rows)
        pltpu.make_async_copy(out.at[spot], g_any.at[spot], sem.at[n_pieces + 1 + k]).wait()


def add_rows(count, order, pieces, d_tokens, mats, small, rows_here):
    return pl.pallas_call(
        functools.partial(scatter_kernel, len(pieces)),
        out_shape=(
            jax.ShapeDtypeStruct((rows_here, D), BF),
            jax.ShapeDtypeStruct((TOK, D), F32),
            jax.ShapeDtypeStruct((8, TOK), F32),
        ),
        in_specs=[pl.BlockSpec(memory_space=pltpu.SMEM)] * 2
        + any_specs(1 + len(pieces))
        + vmem(6),
        out_specs=tuple(any_specs(1) + vmem(2)),
        scratch_shapes=[
            pltpu.VMEM((rows_here + 8, D), F32),
            pltpu.VMEM(d_tokens.shape, BF),
            pltpu.VMEM(d_tokens.shape, F32),
            pltpu.VMEM((rows_here, D), BF),
            pltpu.SemaphoreType.DMA((len(pieces) + 4,)),
        ],
        compiler_params=params(mib=60),
    )(count, order, d_tokens, *pieces, *mats, *small)


def total_kernel(x_ref, o_ref, got, send, recv):
    dp, fs = lax.axis_index("dp"), lax.axis_index("fsdp")
    line = [(dp, fs ^ k) for k in range(1, 8)]
    greet(line)
    link = Link(send, recv)
    copies = [link.copy(x_ref, got.at[fs], peer) for peer in line]
    for copy in copies:
        copy.start()
    got[fs] = x_ref[...]
    for copy in copies:
        copy.wait()
    total = got[0]
    for j in range(1, 8):
        total = total + got[j]
    total = jnp.sum(jnp.sum(total, 0, keepdims=True), 1, keepdims=True)
    o_ref[...] = jnp.sqrt(jnp.broadcast_to(total, o_ref.shape))


def line_norm(x):
    return pl.pallas_call(
        total_kernel,
        out_shape=jax.ShapeDtypeStruct((8, TOK), F32),
        in_specs=vmem(1),
        out_specs=vmem(1)[0],
        scratch_shapes=[pltpu.VMEM((8, 8, TOK), F32)] + sems(7),
        compiler_params=params(6, 4),
    )(x)


def adam_kernel(rates, scale_ref, *refs):
    step = pl.program_id(0)
    n = len(rates)
    ins, outs = refs[: 4 * n], refs[4 * n :]
    for i, rate in enumerate(rates):
        w, m, v, g = ins[4 * i : 4 * i + 4]
        spots = outs[3 * i : 3 * i + 3]

        def update(w=w, m=m, v=v, g=g, spots=spots, rate=rate):
            gradient = g[...].astype(F32) * scale_ref[0]
            new = adam_update(w[...], m[...], v[...], gradient, rate)
            for spot, value in zip(spots, new):
                spot[...] = value

        if i == 0:
            update()
        else:
            pl.when(step % 2 == 0)(update)


def adam_all(scale, groups, rates):
    rows = 528
    steps = pl.cdiv(groups[0][0].shape[0], rows)
    specs = [pl.BlockSpec((rows, D), lambda i: (i, 0))]
    for group in groups[1:]:
        pieces = 6 if group[0].shape[0] % 96 == 0 else 2
        high = group[0].shape[0] // pieces
        stride = 2 * (steps // 2 // pieces)
        specs.append(
            pl.BlockSpec((high, group[0].shape[1]), lambda i, stride=stride: (i // stride, 0))
        )
    return pl.pallas_call(
        functools.partial(adam_kernel, rates),
        grid=(steps,),
        in_specs=[pl.BlockSpec(memory_space=pltpu.SMEM)] + [s for s in specs for k in range(4)],
        out_specs=[s for s in specs for k in range(3)],
        out_shape=[jax.ShapeDtypeStruct(g[0].shape, F32) for g in groups for k in range(3)],
        compiler_params=params(mib=56),
    )(scale.reshape(1), *[a for group in groups for a in group])


def norm_back(values, gain, cotangent):
    center = values - jnp.mean(values, axis=-1, keepdims=True)
    rate = lax.rsqrt(jnp.mean(center * center, axis=-1, keepdims=True) + EPS)
    normed = center * rate
    inner = cotangent * gain
    pull = inner - jnp.mean(inner, axis=-1, keepdims=True)
    pull = rate * (pull - normed * jnp.mean(inner * normed, axis=-1, keepdims=True))
    return (
        pull,
        jnp.sum(cotangent * normed, axis=0, keepdims=True),
        jnp.sum(cotangent, axis=0, keepdims=True),
    )


def attention_forward(inputs, w_qkv, w_out, pieces):
    gain_one, bias_one = pieces[0], pieces[1]
    bias_qkv, bias_out, map_query, map_key = pieces[6], pieces[7], pieces[10], pieces[11]
    length = inputs.shape[0]
    normed_one = layer_norm(inputs, gain_one, bias_one).astype(BF)
    project = dense(normed_one, w_qkv) + bias_qkv
    queries = project[:, :D].astype(BF).reshape(length, H, HD)
    keys_in = project[:, D : 2 * D].astype(BF).reshape(length, H, HD)
    values_in = project[:, 2 * D :].astype(BF).reshape(length, H, HD)
    maps_q = map_query.reshape(H, HD, HD).astype(BF)
    maps_k = map_key.reshape(H, HD, HD).astype(BF)
    inner_q = jnp.einsum("shd,hde->she", queries, maps_q, preferred_element_type=F32)
    inner_k = jnp.einsum("shd,hde->she", keys_in, maps_k, preferred_element_type=F32)
    feat_q = features(inner_q).astype(BF)
    feat_k = features(inner_k).astype(BF)
    scores = jnp.einsum("thf,shf->hts", feat_q, feat_k, preferred_element_type=F32) * causal_mask(
        length
    )
    totals = jnp.sum(scores, axis=-1)
    scores_low = scores.astype(BF)
    numer = jnp.einsum("hts,shd->thd", scores_low, values_in, preferred_element_type=F32)
    attended = numer / jnp.transpose(totals)[:, :, None]
    att_low = attended.reshape(length, D).astype(BF)
    resid_one = inputs + dense(att_low, w_out) + bias_out
    saved = (
        normed_one,
        queries,
        keys_in,
        values_in,
        maps_q,
        maps_k,
        inner_q,
        inner_k,
        feat_q,
        feat_k,
        scores_low,
        totals,
        numer,
        att_low,
    )
    return resid_one, saved


def attention_backward(inputs, w_qkv, w_out, pieces, saved, d_resid_one):
    gain_one = pieces[0]
    (
        normed_one,
        queries,
        keys_in,
        values_in,
        maps_q,
        maps_k,
        inner_q,
        inner_k,
        feat_q,
        feat_k,
        scores_low,
        totals,
        numer,
        att_low,
    ) = saved
    length = inputs.shape[0]
    d_bias_out = jnp.sum(d_resid_one, axis=0, keepdims=True)
    d_out_low = d_resid_one.astype(BF)
    g_out = dense_tn(att_low, d_out_low)
    d_attended = dense_nt(d_out_low, w_out).reshape(length, H, HD)
    inverse = 1.0 / jnp.transpose(totals)
    d_numer_low = (d_attended * inverse[:, :, None]).astype(BF)
    d_totals = jnp.transpose(-jnp.sum(d_attended * numer, axis=-1) * inverse * inverse)
    d_scores = jnp.einsum("thd,shd->hts", d_numer_low, values_in, preferred_element_type=F32)
    d_scores_low = ((d_scores + d_totals[:, :, None]) * causal_mask(length)).astype(BF)
    d_values = jnp.einsum("hts,thd->shd", scores_low, d_numer_low, preferred_element_type=F32)
    d_feat_q = jnp.einsum("hts,shf->thf", d_scores_low, feat_k, preferred_element_type=F32)
    d_feat_k = jnp.einsum("hts,thf->shf", d_scores_low, feat_q, preferred_element_type=F32)
    unused, pull_q = jax.vjp(features, inner_q)
    unused, pull_k = jax.vjp(features, inner_k)
    d_inner_q = pull_q(d_feat_q)[0].astype(BF)
    d_inner_k = pull_k(d_feat_k)[0].astype(BF)
    g_map_q = jnp.einsum("shd,she->hde", queries, d_inner_q, preferred_element_type=F32)
    g_map_k = jnp.einsum("shd,she->hde", keys_in, d_inner_k, preferred_element_type=F32)
    d_queries = jnp.einsum("she,hde->shd", d_inner_q, maps_q, preferred_element_type=F32)
    d_keys = jnp.einsum("she,hde->shd", d_inner_k, maps_k, preferred_element_type=F32)
    d_project = jnp.concatenate(
        [d_queries.reshape(length, D), d_keys.reshape(length, D), d_values.reshape(length, D)],
        axis=1,
    )
    d_bias_qkv = jnp.sum(d_project, axis=0, keepdims=True)
    d_project_low = d_project.astype(BF)
    g_qkv = dense_tn(normed_one, d_project_low)
    d_normed_one = dense_nt(d_project_low, w_qkv)
    d_input_part, d_gain_one, d_bias_one = norm_back(inputs, gain_one, d_normed_one)
    d_inputs = d_resid_one + d_input_part
    return d_inputs, g_qkv, g_out, (d_gain_one, d_bias_one, d_bias_qkv, d_bias_out, g_map_q, g_map_k)


def body(
    tok_ids,
    targets,
    loss_mask,
    embed,
    embed_m,
    embed_v,
    posit,
    posit_m,
    posit_v,
    attn_in,
    attn_in_m,
    attn_in_v,
    attn_out,
    attn_out_m,
    attn_out_v,
    mlp_in,
    mlp_in_m,
    mlp_in_v,
    mlp_out,
    mlp_out_m,
    mlp_out_v,
    small,
    small_m,
    small_v,
):
    dp, rank = lax.axis_index("dp"), lax.axis_index("fsdp")
    shard_rows = embed.shape[0]
    first_row = rank * shard_rows
    mine = jnp.concatenate([tok_ids, targets, loss_mask, jnp.zeros((5, TOK), jnp.int32)], axis=0)
    shared, zq, wqo, zs, zo = first_exchange(mine, attn_in, attn_out, mlp_in)
    all_ids = shared[:, :, 0, :].reshape(4, GROUP)
    all_targets = shared[:, :, 1, :].reshape(4, GROUP)
    all_mask = shared[:, :, 2, :].reshape(4, GROUP).astype(F32)
    token_total = jnp.sum(all_mask)
    weight = all_mask / token_total
    local_ids = all_ids - first_row
    inside = (local_ids >= 0) & (local_ids < shard_rows)
    safe_ids = jnp.clip(local_ids, 0, shard_rows - 1)
    target_local = all_targets - first_row
    target_here = (target_local >= 0) & (target_local < shard_rows)
    target_local = jnp.where(target_here, target_local, -1)
    group_ids = lax.dynamic_index_in_dim(safe_ids, dp, 0, False)
    group_in = lax.dynamic_index_in_dim(inside, dp, 0, False)
    target_rows = target_local.reshape(4, 1, GROUP)
    weight_rows = weight.reshape(4, 1, GROUP)
    looked = jnp.where(group_in[:, None], jnp.take(embed, group_ids, axis=0), 0.0).astype(BF)

    small_pad = -small.shape[0] % (16 * TOK)
    w_two = mlp_out.astype(BF)
    embedded, wqo, w_one, small_full, positions = start_exchange(
        looked,
        wqo,
        zq,
        zs,
        zo,
        jnp.pad(small, (0, small_pad)).astype(BF).reshape(-1, TOK),
        posit.astype(BF),
    )
    wqo = wqo.reshape(D, 4 * D)
    w_one = w_one.reshape(D, FF // 8)
    w_qkv, w_out = wqo[:, : 3 * D], wqo[:, 3 * D :]
    small_full = small_full.reshape(8, -1)[:, : small.shape[0]].reshape(-1)
    pieces = unpack(small_full.astype(F32))
    gain_two, bias_two, gain_fin, bias_fin = pieces[2:6]
    bias_up, bias_down = pieces[8], pieces[9]
    own_up = lax.dynamic_slice_in_dim(bias_up, rank * (FF // 8), FF // 8)

    inputs = embedded + positions.astype(F32)
    resid_one, saved = attention_forward(inputs, w_qkv, w_out, pieces)
    mlp_sum, normed_two, pre_act, act_low = mlp_forward(
        layer_norm(resid_one, gain_two, bias_two).astype(BF), w_one, w_two, own_up
    )
    resid_two = resid_one + mlp_sum + bias_down
    final_own = layer_norm(resid_two, gain_fin, bias_fin).astype(BF)
    grown, stats, table, final, near_final = own_logits(embed, final_own, target_rows)
    lse, hits = combine_stats(stats)
    loss = jnp.sum((lse - hits).reshape(4, GROUP) * all_mask) / token_total
    d_final, all_final = final_cotangent(
        grown, stats, lse, weight_rows, target_rows, table, final, near_final
    )
    tokens = (
        all_final.reshape(4, GROUP, D),
        lse,
        weight_rows,
        target_rows,
    )
    fill = (table,) + tokens
    starts = [table.shape[0] - FILL * (4 - i) for i in range(4)]
    d_final, block_a = sum_tokens_fill(d_final, fill, starts[0], 10)

    d_resid_two, d_gain_fin, d_bias_fin = norm_back(resid_two, gain_fin, d_final)
    d_bias_down = jnp.sum(d_resid_two, axis=0, keepdims=True)
    d_normed_two, g_down, g_up, d_bias_own, block_b, block_c = mlp_backward(
        d_resid_two.astype(BF),
        w_one,
        w_two,
        pre_act,
        act_low,
        normed_two,
        fill,
        starts[1],
        starts[2],
        12,
    )
    d_resid_part, d_gain_two, d_bias_two = norm_back(resid_one, gain_two, d_normed_two)
    d_resid_one = d_resid_two + d_resid_part
    d_inputs, g_qkv, g_out, small_parts = attention_backward(
        inputs, w_qkv, w_out, pieces, saved, d_resid_one
    )
    d_gain_one, d_bias_one, d_bias_qkv, d_bias_out, g_map_q, g_map_k = small_parts
    d_low = d_inputs.astype(BF)
    group_back, side_back, s_qkv, s_out, g_down, block_d = gather_tokens_last(
        d_low, g_qkv.astype(BF), g_out.astype(BF), g_down, fill, starts[3], 13
    )

    vectors = (
        (d_gain_one, d_bias_one, d_gain_two, d_bias_two, d_gain_fin, d_bias_fin)
        + (d_bias_qkv, d_bias_out, d_bias_own, d_bias_down)
    )
    g_maps = jnp.concatenate([g_map_q.reshape(HD, D), g_map_k.reshape(HD, D)], axis=0)

    g_table, all_back, g_qkv, g_out, g_up, g_maps, g_vec = table_gradient(
        starts[0],
        table,
        tokens,
        group_back,
        side_back,
        s_qkv,
        s_out,
        g_up,
        g_maps.reshape(8, 2 * HD // 8, D).astype(BF),
        vectors,
    )
    all_back = all_back.reshape(-1, D)
    g_small = jnp.concatenate([g_vec[:15], g_maps.reshape(2 * HD, D).astype(F32)], axis=0)
    g_small = g_small.reshape(-1)
    g_small = lax.dynamic_slice_in_dim(g_small, rank * small.shape[0], small.shape[0])
    flat_in = inside.reshape(-1)
    row_of = jnp.where(flat_in, local_ids.reshape(-1), shard_rows)
    order = lax.sort(row_of * 4096 + lax.iota(jnp.int32, flat_in.shape[0]))
    count = jnp.sum(flat_in.astype(jnp.int32)).reshape(1)
    g_table, g_posit, squares = add_rows(
        count,
        order,
        (g_table, block_a, block_b, block_c, block_d),
        all_back,
        (g_qkv, g_out, g_up, g_down),
        (g_vec, g_maps.reshape(2 * HD, D)),
        shard_rows,
    )
    grad_norm = line_norm(squares)[0, 0]
    scale = CLIP_LIMIT / jnp.maximum(grad_norm, CLIP_LIMIT)
    rates = rate_list()
    groups = (
        (embed, embed_m, embed_v, g_table),
        (posit, posit_m, posit_v, g_posit),
        (attn_in, attn_in_m, attn_in_v, g_qkv),
        (attn_out, attn_out_m, attn_out_v, g_out),
        (mlp_in, mlp_in_m, mlp_in_v, g_up),
        (mlp_out, mlp_out_m, mlp_out_v, g_down),
    )
    new = adam_all(scale, groups, rates[:6])
    new_small = adam_update(small, small_m, small_v, g_small * scale, rates[6])
    return (loss, grad_norm, *new, *new_small)


def solution(mesh):
    fits = mesh.shape["dp"] == 4 and mesh.shape["fsdp"] == 8
    step = body if fits else body_general
    in_specs = (
        P(("dp", "fsdp"), None),
        P(("dp", "fsdp"), None),
        P(("dp", "fsdp"), None),
        P("fsdp", None),
        P("fsdp", None),
        P("fsdp", None),
        P("fsdp", None),
        P("fsdp", None),
        P("fsdp", None),
        P("fsdp", None),
        P("fsdp", None),
        P("fsdp", None),
        P("fsdp", None),
        P("fsdp", None),
        P("fsdp", None),
        P("fsdp", None),
        P("fsdp", None),
        P("fsdp", None),
        P("fsdp", None),
        P("fsdp", None),
        P("fsdp", None),
        P("fsdp"),
        P("fsdp"),
        P("fsdp"),
    )
    out_specs = (
        P(),
        P(),
        P("fsdp", None),
        P("fsdp", None),
        P("fsdp", None),
        P("fsdp", None),
        P("fsdp", None),
        P("fsdp", None),
        P("fsdp", None),
        P("fsdp", None),
        P("fsdp", None),
        P("fsdp", None),
        P("fsdp", None),
        P("fsdp", None),
        P("fsdp", None),
        P("fsdp", None),
        P("fsdp", None),
        P("fsdp", None),
        P("fsdp", None),
        P("fsdp", None),
        P("fsdp"),
        P("fsdp"),
        P("fsdp"),
    )
    return jax.shard_map(step, mesh=mesh, in_specs=in_specs, out_specs=out_specs, check_vma=False)
```
